32 devices in a mesh: grp: 16 (over z, x, core), tp: 2 (over y).
Axes of the slice: x: 2, y: 2, z: 4, core: 2. Of those that a mesh axis runs over, the one named last changes fastest.
Arguments:
- tokens: bfloat16 [16, 1024, 2048], P(None, 'grp'), may hold values from -6 to 6
- w_query: bfloat16 [2048, 2048], P(None, 'tp'), may hold values from -0.375 to 0.375
- w_key: bfloat16 [2048, 2048], P(None, 'tp'), may hold values from -0.125 to 0.125
- w_value: bfloat16 [2048, 2048], P(None, 'tp'), may hold values from -0.125 to 0.125
- w_out: bfloat16 [2048, 2048], P('tp'), may hold values from -0.125 to 0.125
- own_cache: bfloat16 [16, 2, 2048, 2048], P('grp', None, None, 'tp'), may hold values from -330 to 330
- guest_cache: bfloat16 [16, 2, 2048, 2048], P('grp', None, None, 'tp'), may hold values from -6 to 6
- rec_hidden: bfloat16 [16, 256, 2048], P('grp'), may hold values from -6 to 6
- deal_order: int32 [16], replicated, may hold values from 0 to 15, each once
- own_len: int32 [16], replicated, may hold values from 256 to 2048, as said below
- guest_len: int32 [16], replicated, may hold values from 0 to 2048, as said below
- rec_index: int32 [16, 256], P('grp'), may hold values from 0 to 2047, as said below
Outputs:
- attn_out: bfloat16 [16, 1024, 2048], P(None, 'grp', 'tp')
The draws below stay inside these ranges and needn't reach their ends.
Inputs may be any that keep to these rules, and one draw needn't show every extreme that they name: Rows 0 to own_len[g] - 1 of group g's own slot hold cached positions 0 to own_len[g] - 1 of the request served at group g; a request whose cache continues in a guest region fills its own slot. The guest_len[g] used rows of group g's guest region continue the cache of the request served at group (g + 8) mod 16. rec_index[g] holds 256 distinct rows of group g's own slot, each below own_len[g].
All inputs are finite; a program needn't handle non-finite values.
Results may differ from the reference program's by a relative error of at most 0.02.
The reference program's roundings to bfloat16 on the way count: a program that leaves them out, or rounds other values in their place, can miss the bound.
Values may be sent and summed in bfloat16 or wider, within the bound.
No kernel may reach another device: no remote copies, remote signals or barrier semaphores. Data moves between devices by JAX's collectives and lax.ppermute only.
A program may use at most 192 MiB of HBM per device.

```python
import jax
import jax.numpy as jnp
from jax import lax

D = 2048
HEADS = 16
HEAD_DIM = 128
SPAN = 1024
CAP = 2048
GCAP = 2048
RECOMP = 256
N_GRP = 16
N_TP = 2


def cache_layout(key):
    base_key = jax.random.fold_in(key, 7)
    key_short, key_flag, key_pair, key_side, key_extra, key_other = jax.random.split(base_key, 6)
    half_count = N_GRP // 2
    pair_ids = jnp.arange(half_count, dtype=jnp.int32)
    short_rows = jax.random.randint(key_short, (N_GRP,), CAP // 8, CAP + 1)
    forced_pair = jax.random.randint(key_pair, (), 0, half_count)
    long_flag = jnp.where(pair_ids == forced_pair, 1, jax.random.randint(key_flag, (half_count,), 0, 2))
    side_flag = jax.random.randint(key_side, (half_count,), 0, 2)
    both_long = jnp.where(pair_ids == 0, 1, 0)
    extra_rows = jnp.where((pair_ids == forced_pair) | (pair_ids == 0), GCAP, jax.random.randint(key_extra, (half_count,), 1, GCAP + 1))
    other_rows = jnp.where(pair_ids == 0, GCAP, jax.random.randint(key_other, (half_count,), 1, GCAP + 1))
    lower_long = jnp.maximum(long_flag * (1 - side_flag), both_long)
    upper_long = jnp.maximum(long_flag * side_flag, both_long)
    is_long = jnp.concatenate([lower_long, upper_long])
    own_rows = jnp.where(is_long == 1, CAP, short_rows).astype(jnp.int32)
    guest_rows = jnp.concatenate([upper_long * extra_rows, lower_long * other_rows]).astype(jnp.int32)
    return (own_rows, guest_rows)


def draw_own_len(key, part):
    return cache_layout(key)[0]


def draw_guest_len(key, part):
    return cache_layout(key)[1]


def draw_rec_index(key, part):
    own_rows = cache_layout(key)[0]
    ranking = jax.random.randint(jax.random.fold_in(key, 11), (N_GRP, CAP), 0, 4096)
    position = jnp.arange(CAP, dtype=jnp.int32)[None, :]
    keyed = jnp.where(position < own_rows[:, None], ranking * CAP + position, 4096 * CAP + position)
    ordering = jnp.argsort(keyed, axis=1)
    return ordering[:, :CAP // 8].astype(jnp.int32)


def draw_own_cache(key, part):
    key_base = jax.random.fold_in(jax.random.fold_in(key, 3), 0)
    full_width = HEADS * HEAD_DIM
    shape = (N_GRP, 2, CAP, full_width)
    drawn = jnp.clip(jax.random.normal(key_base, shape, jnp.float32), -6.0, 6.0)
    return drawn.astype(jnp.bfloat16)


def shard_levels(key, dims, shards, low, high):
    loudness = 1.0
    for axis_at, parts in shards:
        heights = jax.random.uniform(jax.random.fold_in(jax.random.fold_in(key, 6), axis_at), (parts,), jnp.float32, low / len(shards), high / len(shards))
        loudness = loudness * jnp.repeat(jnp.exp(heights), dims[axis_at] // parts).reshape((-1,) + (1,) * (len(dims) - 1 - axis_at))
    return loudness


def noise(stream_key, extent, spread, bound, cuts=(), kind=jnp.bfloat16):
    result = spread * jax.random.normal(stream_key, extent, jnp.float32)
    if cuts:
        result = result * shard_levels(stream_key, extent, cuts, -0.22, 0.18)
    return jnp.clip(result, -bound, bound).astype(kind)


def setup_inputs(seed: int = 0) -> dict:
    keys = jax.random.split(jax.random.key(seed), 13)
    return {
        "tokens": noise(keys[0], (N_GRP, SPAN, D), 1.0, 6.0, ((1, 16),)),
        "w_query": noise(keys[1], (D, HEADS * HEAD_DIM), (D // 9) ** -0.5, 0.375, ((1, 2),)),
        "w_key": noise(keys[2], (D, HEADS * HEAD_DIM), D ** -0.5, 0.125, ((1, 2),)),
        "w_value": noise(keys[3], (D, HEADS * HEAD_DIM), D ** -0.5, 0.125, ((1, 2),)),
        "w_out": noise(keys[4], (HEADS * HEAD_DIM, D), (HEADS * HEAD_DIM) ** -0.5, 0.125, ((0, 2),)),
        "own_cache": draw_own_cache(jax.random.fold_in(keys[12], 71), 0),
        "guest_cache": noise(keys[6], (N_GRP, 2, GCAP, HEADS * HEAD_DIM), 1.0, 6.0, ((0, 16), (3, 2))),
        "rec_hidden": noise(keys[7], (N_GRP, RECOMP, D), 1.0, 6.0, ((0, 16),)),
        "deal_order": jax.random.permutation(keys[8], N_GRP).astype(jnp.int32),
        "own_len": draw_own_len(jax.random.fold_in(keys[12], 71), 0),
        "guest_len": draw_guest_len(jax.random.fold_in(keys[12], 71), 0),
        "rec_index": draw_rec_index(jax.random.fold_in(keys[12], 71), 0),
    }


rope_base = 10000.0
norm_eps = 1e-05

def layer_norm(token_rows):
    widened = token_rows.astype(jnp.float32)
    centred = widened - lax.optimization_barrier(jnp.mean(widened, axis=-1, keepdims=True))
    variance = lax.optimization_barrier(jnp.mean(centred * centred, axis=-1, keepdims=True))
    return centred * lax.rsqrt(variance + norm_eps)

def rotate(projected, positions, head_dim):
    half_dim = head_dim // 2
    frequency = jnp.exp(-jnp.log(rope_base) * jnp.arange(half_dim, dtype=jnp.float32) / half_dim)
    angles = positions.astype(jnp.float32)[:, None] * frequency[None, :]
    cosine = jnp.cos(angles)[:, None, :]
    sine_part = jnp.sin(angles)[:, None, :]
    shaped = projected.reshape(projected.shape[0], -1, head_dim)
    first_half = shaped[..., :half_dim]
    second = shaped[..., half_dim:]
    turned = jnp.concatenate([first_half * cosine - second * sine_part, second * cosine + first_half * sine_part], axis=-1)
    return turned.reshape(projected.shape)

def reference(tokens, w_query, w_key, w_value, w_out, own_cache, guest_cache, rec_hidden, deal_order, own_len, guest_len, rec_index):
    full_width = HEADS * HEAD_DIM
    block_width = full_width // N_TP
    score_scale = HEAD_DIM ** (-0.5)

    def one_group(group_id):
        partner_id = (group_id + N_GRP // 2) % N_GRP
        own_count = own_len[group_id]
        guest_count = guest_len[partner_id]
        token_rows = tokens[deal_order[group_id]]
        positions = own_count + guest_count + jnp.arange(SPAN, dtype=jnp.int32)
        normed = layer_norm(token_rows).astype(jnp.bfloat16)
        queries = rotate(jnp.dot(normed, w_query, preferred_element_type=jnp.float32), positions, HEAD_DIM).astype(jnp.bfloat16)
        new_keys = rotate(jnp.dot(normed, w_key, preferred_element_type=jnp.float32), positions, HEAD_DIM).astype(jnp.bfloat16)
        new_values = jnp.dot(normed, w_value, preferred_element_type=jnp.float32).astype(jnp.bfloat16)
        rec_rows = layer_norm(rec_hidden[group_id]).astype(jnp.bfloat16)
        rec_positions = rec_index[group_id].astype(jnp.int32)
        rec_keys = rotate(jnp.dot(rec_rows, w_key, preferred_element_type=jnp.float32), rec_positions, HEAD_DIM).astype(jnp.bfloat16)
        rec_values = jnp.dot(rec_rows, w_value, preferred_element_type=jnp.float32).astype(jnp.bfloat16)
        cached_keys = own_cache[group_id, 0].at[rec_positions].set(rec_keys)
        cached_values = own_cache[group_id, 1].at[rec_positions].set(rec_values)
        all_keys = jnp.concatenate([cached_keys, guest_cache[partner_id, 0], new_keys], axis=0)
        all_values = jnp.concatenate([cached_values, guest_cache[partner_id, 1], new_values], axis=0)
        query_place = jnp.arange(SPAN, dtype=jnp.int32)[:, None]
        is_valid = jnp.concatenate([jnp.broadcast_to(jnp.arange(CAP, dtype=jnp.int32)[None, :] < own_count, (SPAN, CAP)), jnp.broadcast_to(jnp.arange(GCAP, dtype=jnp.int32)[None, :] < guest_count, (SPAN, GCAP)), jnp.arange(SPAN, dtype=jnp.int32)[None, :] <= query_place], axis=1)
        query_heads = queries.astype(jnp.float32).reshape(SPAN, HEADS, HEAD_DIM)
        key_heads = all_keys.astype(jnp.float32).reshape(-1, HEADS, HEAD_DIM)
        value_heads = all_values.astype(jnp.float32).reshape(-1, HEADS, HEAD_DIM)
        scores = jnp.einsum('qhd,khd->hqk', query_heads, key_heads) * score_scale
        scores = jnp.where(is_valid[None], scores, -jnp.inf)
        top_score = lax.optimization_barrier(jnp.max(scores, axis=-1, keepdims=True))
        expanded = jnp.exp(scores - top_score)
        weight_sum = lax.optimization_barrier(jnp.sum(expanded, axis=-1))
        weights = lax.optimization_barrier(expanded.astype(jnp.bfloat16))
        numerator = jnp.einsum('hqk,khd->qhd', weights.astype(jnp.float32), value_heads)
        attended = (numerator / jnp.transpose(weight_sum)[:, :, None]).astype(jnp.bfloat16).reshape(SPAN, full_width)
        mixed_sum = jnp.zeros((SPAN, D), jnp.float32)
        for tp_block in range(N_TP):
            lower_edge = tp_block * block_width
            term_part = jnp.dot(attended[:, lower_edge:lower_edge + block_width], w_out[lower_edge:lower_edge + block_width], preferred_element_type=jnp.float32)
            rounded = lax.optimization_barrier(term_part.astype(jnp.bfloat16))
            mixed_sum = mixed_sum + rounded.astype(jnp.float32)
        return mixed_sum.astype(jnp.bfloat16)
    outputs = lax.map(one_group, jnp.arange(N_GRP, dtype=jnp.int32))
    return jnp.zeros_like(outputs).at[deal_order].set(outputs)
```

```python
import functools
import math

import jax
import jax.numpy as jnp
from jax import lax
from jax.experimental import pallas as pl
from jax.experimental.pallas import tpu as pltpu
from jax.sharding import PartitionSpec as P

HEAD_DIM = 128
KEY_BLOCK = 512
ROW_BLOCK = 256
VMEM_LIMIT = 50 * 1024 * 1024

rope_base = 10000.0
norm_eps = 1e-05
LOG2E = math.log2(math.e)
LOWEST = -1e30


def params():
    return pltpu.CompilerParams(vmem_limit_bytes=VMEM_LIMIT)


def layer_norm(token_rows):
    widened = token_rows.astype(jnp.float32)
    centred = widened - jnp.mean(widened, axis=-1, keepdims=True)
    variance = jnp.mean(centred * centred, axis=-1, keepdims=True)
    return centred * lax.rsqrt(variance + norm_eps)


def rope_tables(positions):
    half_dim = HEAD_DIM // 2
    frequency = jnp.exp(-jnp.log(rope_base) * jnp.arange(half_dim, dtype=jnp.float32) / half_dim)
    angles = positions.astype(jnp.float32)[:, None] * frequency[None, :]
    cosine = jnp.cos(angles)
    sine = jnp.sin(angles)
    return (
        jnp.concatenate([cosine, cosine], axis=-1),
        jnp.concatenate([-sine, sine], axis=-1),
    )


def deal_kernel(deal_ref, tp_ref, x_ref, own_ref, guest_ref):
    normed = layer_norm(x_ref[0]).astype(jnp.bfloat16)
    own_ref[0] = normed
    guest_ref[0] = normed


def deal(tokens, deal_order, tp_index, piece):
    groups, _, width = tokens.shape
    half = groups // 2
    out = jax.ShapeDtypeStruct((groups, piece, width), jnp.bfloat16)
    return pl.pallas_call(
        deal_kernel,
        grid_spec=pltpu.PrefetchScalarGridSpec(
            num_scalar_prefetch=2,
            grid=(groups,),
            in_specs=[pl.BlockSpec((1, piece, width), lambda d, order, t: (order[d], t[0], 0))],
            out_specs=[
                pl.BlockSpec((1, piece, width), lambda d, order, t: (d, 0, 0)),
                pl.BlockSpec((1, piece, width), lambda d, order, t: ((d + half) % groups, 0, 0)),
            ],
        ),
        out_shape=[out, out],
        compiler_params=params(),
        name="deal",
    )(deal_order, tp_index, tokens)


def project_kernel(turned, heads, x_ref, cos_ref, sin_ref, *refs):
    count = len(turned)
    x = x_ref[...]
    for w_ref, out_ref, turn in zip(refs[:count], refs[count:], turned):
        product = jnp.dot(x, w_ref[...], preferred_element_type=jnp.float32)
        if not turn:
            out_ref[...] = product.astype(jnp.bfloat16)
            continue
        for head in range(heads):
            cut = slice(head * HEAD_DIM, (head + 1) * HEAD_DIM)
            part = product[:, cut]
            swapped = pltpu.roll(part, HEAD_DIM // 2, 1)
            out_ref[:, cut] = (part * cos_ref[...] + swapped * sin_ref[...]).astype(jnp.bfloat16)


def project(x, tables, weights, turned):
    rows, depth = x.shape
    width = weights[0].shape[1]
    block = min(256, width)
    whole = pl.BlockSpec((rows, depth), lambda n: (0, 0))
    table = pl.BlockSpec((rows, HEAD_DIM), lambda n: (0, 0))
    count = len(weights)
    return pl.pallas_call(
        functools.partial(project_kernel, turned, block // HEAD_DIM),
        grid=(width // block,),
        in_specs=[whole, table, table] + [pl.BlockSpec((depth, block), lambda n: (0, n))] * count,
        out_specs=[pl.BlockSpec((rows, block), lambda n: (0, n))] * count,
        out_shape=[jax.ShapeDtypeStruct((rows, width), jnp.bfloat16)] * count,
        compiler_params=params(),
        cost_estimate=pl.CostEstimate(
            flops=2 * rows * depth * width * count,
            bytes_accessed=2 * (rows * depth + count * width * (rows + depth)),
            transcendentals=0,
        ),
        name="project",
    )(x, *tables, *weights)


def replace_kernel(block, index_ref, cache_ref, fresh_ref, out_ref):
    first = pl.program_id(1) * block
    count = index_ref.shape[1]
    row = first + lax.broadcasted_iota(jnp.int32, (block, count), 0)
    hits = jnp.where(row == index_ref[...], 1.0, 0.0)
    picked = jnp.dot(
        hits.astype(jnp.bfloat16), fresh_ref[0], preferred_element_type=jnp.float32
    )
    is_hit = jnp.sum(hits, axis=1, keepdims=True) > 0.5
    out_ref[0] = jnp.where(is_hit, picked, cache_ref[0, 0].astype(jnp.float32)).astype(jnp.bfloat16)


def replace_rows(cache, fresh, rec_index):
    _, _, rows, width = cache.shape
    count = rec_index.shape[1]
    block = 512
    return pl.pallas_call(
        functools.partial(replace_kernel, block),
        grid=(2, rows // block),
        in_specs=[
            pl.BlockSpec((1, count), lambda c, r: (0, 0)),
            pl.BlockSpec((1, 1, block, width), lambda c, r: (0, c, r, 0)),
            pl.BlockSpec((1, count, width), lambda c, r: (c, 0, 0)),
        ],
        out_specs=pl.BlockSpec((1, block, width), lambda c, r: (c, r, 0)),
        out_shape=jax.ShapeDtypeStruct((2, rows, width), jnp.bfloat16),
        compiler_params=params(),
        name="replace_rows",
    )(rec_index, cache, fresh)


def fold_block(rows, scale, q_ref, m_ref, acc_ref, keys, values, mask):
    ones = jnp.ones(values.shape, jnp.bfloat16)
    widened = jnp.concatenate([values, ones], axis=1)
    q = q_ref[rows, :]
    scores = lax.dot_general(
        q, keys, (((1,), (1,)), ((), ())), preferred_element_type=jnp.float32
    )
    if mask is not None:
        scores = jnp.where(mask, scores, LOWEST)
    old_max = m_ref[rows, :]
    new_max = jnp.maximum(old_max, jnp.max(scores, axis=1, keepdims=True))
    factor = jnp.exp2((old_max - new_max) * scale)
    shift = new_max[:, :1] * scale
    weights = jnp.exp2(scores * scale - shift).astype(jnp.bfloat16)
    product = jnp.dot(weights, widened, preferred_element_type=jnp.float32)
    acc_ref[rows, :] = acc_ref[rows, :] * jnp.concatenate([factor, factor], axis=1) + product
    m_ref[rows, :] = new_max


def attend_kernel(causal, count_ref, q_ref, k_ref, v_ref, *refs):
    if causal:
        nk_ref, nv_ref, o_ref, lse_ref, m_ref, acc_ref = refs
    else:
        o_ref, lse_ref, m_ref, acc_ref = refs
    head = pl.program_id(0)
    scale = HEAD_DIM**-0.5 * LOG2E
    span = q_ref.shape[0]
    used = count_ref[0]
    parts = [pl.ds(i * ROW_BLOCK, ROW_BLOCK) for i in range(span // ROW_BLOCK)]
    m_ref[...] = jnp.full(m_ref.shape, LOWEST, jnp.float32)
    acc_ref[...] = jnp.zeros(acc_ref.shape, jnp.float32)
    cache = k_ref.at[(0,) * (len(k_ref.shape) - 2)], v_ref.at[(0,) * (len(v_ref.shape) - 2)]

    def visit(block, masked):
        start = pl.multiple_of(block * KEY_BLOCK, KEY_BLOCK)
        keys = cache[0][pl.ds(start, KEY_BLOCK), :]
        values = cache[1][pl.ds(start, KEY_BLOCK), :]
        mask = None
        if masked:
            place = lax.broadcasted_iota(jnp.int32, (1, KEY_BLOCK), 1)
            mask = place < used - start
        for rows in parts:
            fold_block(rows, scale, q_ref, m_ref, acc_ref, keys, values, mask)

    full = used // KEY_BLOCK
    pl.loop(0, full)(lambda block: visit(block, False))

    @pl.when(used % KEY_BLOCK > 0)
    def _():
        visit(full, True)

    if causal:
        for i, rows in enumerate(parts):
            width = (i + 1) * ROW_BLOCK
            key_at = lax.broadcasted_iota(jnp.int32, (ROW_BLOCK, width), 1)
            row_at = lax.broadcasted_iota(jnp.int32, (ROW_BLOCK, width), 0) + i * ROW_BLOCK
            fold_block(
                rows, scale, q_ref, m_ref, acc_ref, nk_ref[:width, :], nv_ref[:width, :], key_at <= row_at
            )

    for rows in parts:
        total = acc_ref[rows, HEAD_DIM:]
        seen = total > 0.0
        safe = jnp.where(seen, total, 1.0)
        o_ref[rows, :] = (acc_ref[rows, :HEAD_DIM] / safe).astype(jnp.bfloat16)
        lse = jnp.where(seen, m_ref[rows, :] * scale + jnp.log2(safe), LOWEST)
        lane = lax.broadcasted_iota(jnp.int32, (ROW_BLOCK, HEAD_DIM), 1)
        before = jnp.where(head == 0, 0.0, lse_ref[rows, :])
        lse_ref[rows, :] = jnp.where(lane == head, lse, before)


def attend(count, queries, cache, new_keys=None, new_values=None):
    span, width = queries.shape
    heads = width // HEAD_DIM
    rows = cache.shape[-2]
    causal = new_keys is not None
    by_head = pl.BlockSpec((span, HEAD_DIM), lambda h, n: (0, h))
    lead = cache.ndim - 3
    shape = (1,) * (lead + 1) + (rows, HEAD_DIM)

    def half(which):
        return pl.BlockSpec(shape, lambda h, n: (0,) * lead + (which, 0, h))

    keys_seen = rows + (span // 2 if causal else 0)
    return pl.pallas_call(
        functools.partial(attend_kernel, causal),
        grid_spec=pltpu.PrefetchScalarGridSpec(
            num_scalar_prefetch=1,
            grid=(heads,),
            in_specs=[by_head, half(0), half(1)] + [by_head] * (2 if causal else 0),
            out_specs=[by_head, pl.BlockSpec((span, HEAD_DIM), lambda h, n: (0, 0))],
            scratch_shapes=[
                pltpu.VMEM((span, HEAD_DIM), jnp.float32),
                pltpu.VMEM((span, 2 * HEAD_DIM), jnp.float32),
            ],
        ),
        out_shape=[
            jax.ShapeDtypeStruct((span, width), jnp.bfloat16),
            jax.ShapeDtypeStruct((span, HEAD_DIM), jnp.float32),
        ],
        compiler_params=params(),
        cost_estimate=pl.CostEstimate(
            flops=8 * span * keys_seen * width,
            bytes_accessed=4 * rows * width + 4 * span * width,
            transcendentals=span * keys_seen * heads,
        ),
        name="attend_own" if causal else "attend_guest",
    )(count, queries, cache, cache, *((new_keys, new_values) if causal else ()))


def merge_kernel(groups, heads, inverse_ref, own_ref, guest_ref, own_lse_ref, guest_lse_ref, w_ref, out_ref, att_ref):
    piece = own_ref.shape[1]

    @pl.when(pl.program_id(0) == 0)
    def _():
        def one_request(request, carry):
            source = inverse_ref[request]
            helper = lax.rem(source + groups // 2, groups)
            own_lse = own_lse_ref[source]
            guest_lse = guest_lse_ref[helper]
            top = jnp.maximum(own_lse, guest_lse)
            own_share = jnp.exp2(own_lse - top)
            guest_share = jnp.exp2(guest_lse - top)
            total = own_share + guest_share
            own_share = own_share / total
            guest_share = guest_share / total
            rows = pl.ds(pl.multiple_of(request * piece, piece), piece)
            for head in range(heads):
                cut = slice(head * HEAD_DIM, (head + 1) * HEAD_DIM)
                merged = own_ref[source, :, cut].astype(jnp.float32) * own_share[
                    :, head : head + 1
                ] + guest_ref[helper, :, cut].astype(jnp.float32) * guest_share[:, head : head + 1]
                att_ref[rows, cut] = merged.astype(jnp.bfloat16)
            return carry

        lax.fori_loop(0, groups, one_request, 0)

    out_ref[...] = jnp.dot(
        att_ref[...], w_ref[...], preferred_element_type=jnp.float32
    ).astype(jnp.bfloat16)


def merge(inverse, own, guest, own_lse, guest_lse, w_out):
    groups, piece, width = own.shape
    heads = width // HEAD_DIM
    columns = w_out.shape[1]
    block = 256
    parts = pl.BlockSpec(own.shape, lambda n, i: (0, 0, 0))
    lse = pl.BlockSpec(own_lse.shape, lambda n, i: (0, 0, 0))
    rows = groups * piece
    return pl.pallas_call(
        functools.partial(merge_kernel, groups, heads),
        grid_spec=pltpu.PrefetchScalarGridSpec(
            num_scalar_prefetch=1,
            grid=(columns // block,),
            in_specs=[parts, parts, lse, lse, pl.BlockSpec((width, block), lambda n, i: (0, n))],
            out_specs=pl.BlockSpec((rows, block), lambda n, i: (0, n)),
            scratch_shapes=[pltpu.VMEM((rows, width), jnp.bfloat16)],
        ),
        out_shape=jax.ShapeDtypeStruct((rows, columns), jnp.bfloat16),
        compiler_params=params(),
        cost_estimate=pl.CostEstimate(
            flops=2 * rows * width * columns,
            bytes_accessed=2 * (2 * rows * width + width * columns + rows * columns),
            transcendentals=0,
        ),
        name="merge",
    )(inverse, own, guest, own_lse, guest_lse, w_out)


def exchange(value):
    return lax.all_to_all(value, "grp", split_axis=0, concat_axis=0, tiled=True)


def shards(
    tokens,
    w_query,
    w_key,
    w_value,
    w_out,
    own_cache,
    guest_cache,
    rec_hidden,
    deal_order,
    own_len,
    guest_len,
    rec_index,
):
    groups = lax.axis_size("grp")
    tp_size = lax.axis_size("tp")
    group_id = lax.axis_index("grp")
    tp_id = lax.axis_index("tp")
    partner_id = (group_id + groups // 2) % groups
    width = w_query.shape[1]
    heads = width // HEAD_DIM
    shard_rows = tokens.shape[1]
    span = shard_rows * groups
    piece = shard_rows // tp_size

    if piece % 16 == 0:
        own_rows, guest_rows = deal(tokens, deal_order, tp_id.astype(jnp.int32)[None], piece)
    else:
        mine = lax.dynamic_slice_in_dim(tokens, tp_id * piece, piece, 1)
        normed = layer_norm(mine).astype(jnp.bfloat16)
        own_rows = jnp.take(normed, deal_order, axis=0)
        guest_rows = jnp.roll(own_rows, groups // 2, axis=0)

    def gathered(rows):
        arrived = lax.all_gather(exchange(rows), "tp", axis=0)
        return jnp.transpose(arrived, (1, 0, 2, 3)).reshape(span, -1)

    own_x = gathered(own_rows)
    guest_x = gathered(guest_rows)

    def place(owner, helper):
        return own_len[owner] + guest_len[helper] + jnp.arange(span, dtype=jnp.int32)

    own_tables = rope_tables(place(group_id, partner_id))
    guest_tables = rope_tables(place(partner_id, group_id))
    rec_tables = rope_tables(rec_index[0])

    rec_rows = layer_norm(rec_hidden[0]).astype(jnp.bfloat16)
    rec_keys, rec_values = project(rec_rows, rec_tables, (w_key, w_value), (True, False))
    cache = replace_rows(own_cache, jnp.stack([rec_keys, rec_values]), rec_index)

    queries, new_keys, new_values = project(
        own_x, own_tables, (w_query, w_key, w_value), (True, True, False)
    )
    (guest_queries,) = project(guest_x, guest_tables, (w_query,), (True,))

    own_out, own_lse = attend(own_len[group_id][None], queries, cache, new_keys, new_values)
    guest_out, guest_lse = attend(guest_len[group_id][None], guest_queries, guest_cache)

    def by_row_owner(value):
        return exchange(value.reshape(groups, shard_rows, -1))

    def stats(lse):
        turned = jnp.transpose(lse[:, :heads].reshape(groups, shard_rows, heads), (0, 2, 1))
        return jnp.transpose(exchange(turned), (0, 2, 1))

    inverse = jnp.zeros_like(deal_order).at[deal_order].set(
        jnp.arange(groups, dtype=deal_order.dtype)
    )
    partial = merge(
        inverse, by_row_owner(own_out), by_row_owner(guest_out), stats(own_lse), stats(guest_lse), w_out
    )
    mixed = lax.psum_scatter(partial, "tp", scatter_dimension=1, tiled=True)
    return mixed.reshape(groups, shard_rows, -1)


def solution(mesh):
    return jax.shard_map(
        shards,
        mesh=mesh,
        in_specs=(
            P(None, "grp", None),
            P(None, "tp"),
            P(None, "tp"),
            P(None, "tp"),
            P("tp", None),
            P("grp", None, None, "tp"),
            P("grp", None, None, "tp"),
            P("grp", None, None),
            P(),
            P(),
            P(),
            P("grp", None),
        ),
        out_specs=P(None, "grp", "tp"),
        check_vma=False,
    )
```

```python
import functools
import math

import jax
import jax.numpy as jnp
from jax import lax
from jax.experimental import pallas as pl
from jax.experimental.pallas import tpu as pltpu
from jax.sharding import PartitionSpec as P

HEAD_DIM = 128
KEY_BLOCK = 1024
ROW_BLOCK = 256
VMEM_LIMIT = 50 * 1024 * 1024

rope_base = 10000.0
norm_eps = 1e-05
LOG2E = math.log2(math.e)
LOWEST = -1e30


def params():
    return pltpu.CompilerParams(vmem_limit_bytes=VMEM_LIMIT)


def layer_norm(token_rows):
    widened = token_rows.astype(jnp.float32)
    centred = widened - jnp.mean(widened, axis=-1, keepdims=True)
    variance = jnp.mean(centred * centred, axis=-1, keepdims=True)
    return centred * lax.rsqrt(variance + norm_eps)


def rope_tables(positions):
    half_dim = HEAD_DIM // 2
    frequency = jnp.exp(-jnp.log(rope_base) * jnp.arange(half_dim, dtype=jnp.float32) / half_dim)
    angles = positions.astype(jnp.float32)[:, None] * frequency[None, :]
    cosine = jnp.cos(angles)
    sine = jnp.sin(angles)
    return (
        jnp.concatenate([cosine, cosine], axis=-1),
        jnp.concatenate([-sine, sine], axis=-1),
    )


def deal_kernel(order_ref, tp_ref, x_ref, own_ref, guest_ref):
    first = pl.program_id(0) * own_ref.shape[0]
    for at in range(own_ref.shape[0]):
        normed = layer_norm(x_ref[order_ref[first + at]]).astype(jnp.bfloat16)
        own_ref[at] = normed
        guest_ref[at] = normed


def deal(tokens, deal_order, tp_index, piece):
    groups, _, width = tokens.shape
    each = 4
    steps = groups // each
    out = jax.ShapeDtypeStruct((groups, piece, width), jnp.bfloat16)
    return pl.pallas_call(
        deal_kernel,
        grid_spec=pltpu.PrefetchScalarGridSpec(
            num_scalar_prefetch=2,
            grid=(steps,),
            in_specs=[pl.BlockSpec((groups, piece, width), lambda d, order, t: (0, t[0], 0))],
            out_specs=[
                pl.BlockSpec((each, piece, width), lambda d, order, t: (d, 0, 0)),
                pl.BlockSpec(
                    (each, piece, width), lambda d, order, t: ((d + steps // 2) % steps, 0, 0)
                ),
            ],
        ),
        out_shape=[out, out],
        compiler_params=params(),
        name="deal",
    )(deal_order, tp_index, tokens)


def project_kernel(turned, heads, halves, tp_ref, *refs):
    if halves:
        mine_ref, other_ref, cos_ref, sin_ref, *refs, x_ref = refs
        shards_in, piece, _ = mine_ref.shape

        @pl.when(pl.program_id(0) == 0)
        def _():
            t = tp_ref[0]
            for shard in range(shards_in):
                for half_ref, at in ((mine_ref, t), (other_ref, 1 - t)):
                    start = pl.multiple_of((2 * shard + at) * piece, piece)
                    x_ref[pl.ds(start, piece), :] = half_ref[shard]
    else:
        x_ref, cos_ref, sin_ref, *refs = refs
    count = len(turned)
    x = x_ref[...]
    for w_ref, out_ref, turn in zip(refs[:count], refs[count:], turned):
        product = jnp.dot(x, w_ref[...], preferred_element_type=jnp.float32)
        if not turn:
            out_ref[...] = product.astype(jnp.bfloat16)
            continue
        for head in range(heads):
            cut = slice(head * HEAD_DIM, (head + 1) * HEAD_DIM)
            part = product[:, cut]
            swapped = pltpu.roll(part, HEAD_DIM // 2, 1)
            out_ref[:, cut] = (part * cos_ref[...] + swapped * sin_ref[...]).astype(jnp.bfloat16)


def project(x, tp_index, tables, weights, turned):
    depth = x[0].shape[-1]
    rows = math.prod(x[0].shape[:-1]) * len(x)
    width = weights[0].shape[1]
    block = min(256, width)
    halves = len(x) == 2
    table = pl.BlockSpec((rows, HEAD_DIM), lambda n, t: (0, 0))
    count = len(weights)
    return pl.pallas_call(
        functools.partial(project_kernel, turned, block // HEAD_DIM, halves),
        grid_spec=pltpu.PrefetchScalarGridSpec(
            num_scalar_prefetch=1,
            grid=(width // block,),
            in_specs=[pl.BlockSpec(part.shape, lambda n, t, r=part.ndim: (0,) * r) for part in x]
            + [table, table]
            + [pl.BlockSpec((depth, block), lambda n, t: (0, n))] * count,
            out_specs=[pl.BlockSpec((rows, block), lambda n, t: (0, n))] * count,
            scratch_shapes=[pltpu.VMEM((rows, depth), jnp.bfloat16)] if halves else [],
        ),
        out_shape=[jax.ShapeDtypeStruct((rows, width), jnp.bfloat16)] * count,
        compiler_params=params(),
        cost_estimate=pl.CostEstimate(
            flops=2 * rows * depth * width * count,
            bytes_accessed=2 * (rows * depth + count * width * (rows + depth)),
            transcendentals=0,
        ),
        name="project",
    )(tp_index, *x, *tables, *weights)


def replace_kernel(block, index_ref, cache_ref, fresh_ref, out_ref):
    first = pl.program_id(1) * block
    count = index_ref.shape[1]
    row = first + lax.broadcasted_iota(jnp.int32, (block, count), 0)
    hits = jnp.where(row == index_ref[...], 1.0, 0.0)
    picked = jnp.dot(
        hits.astype(jnp.bfloat16), fresh_ref[0], preferred_element_type=jnp.float32
    )
    is_hit = jnp.sum(hits, axis=1, keepdims=True) > 0.5
    out_ref[0] = jnp.where(is_hit, picked, cache_ref[0, 0].astype(jnp.float32)).astype(jnp.bfloat16)


def replace_rows(cache, fresh, rec_index):
    _, _, rows, width = cache.shape
    count = rec_index.shape[1]
    block = 512
    return pl.pallas_call(
        functools.partial(replace_kernel, block),
        grid=(2, rows // block),
        in_specs=[
            pl.BlockSpec((1, count), lambda c, r: (0, 0)),
            pl.BlockSpec((1, 1, block, width), lambda c, r: (0, c, r, 0)),
            pl.BlockSpec((1, count, width), lambda c, r: (c, 0, 0)),
        ],
        out_specs=pl.BlockSpec((1, block, width), lambda c, r: (c, r, 0)),
        out_shape=jax.ShapeDtypeStruct((2, rows, width), jnp.bfloat16),
        compiler_params=params(),
        cost_estimate=pl.CostEstimate(
            flops=4 * rows * count * width, bytes_accessed=10 * rows * width, transcendentals=0
        ),
        name="replace_rows",
    )(rec_index, cache, fresh)


def fold_keys(jobs, q_ref, m_ref, acc_ref):
    scale = HEAD_DIM**-0.5 * LOG2E

    def scores_of(job):
        rows, keys, _, mask = job
        scores = lax.dot_general(
            q_ref[rows, :], keys(), (((1,), (1,)), ((), ())), preferred_element_type=jnp.float32
        )
        return scores if mask is None else jnp.where(mask, scores, LOWEST)

    upcoming = scores_of(jobs[0])
    for at, (rows, _, values, _) in enumerate(jobs):
        scores = upcoming
        if at + 1 < len(jobs):
            upcoming = scores_of(jobs[at + 1])
        old_max = m_ref[rows, :]
        new_max = jnp.maximum(old_max, jnp.max(scores, axis=1, keepdims=True))
        factor = jnp.exp2((old_max - new_max) * scale)
        shift = new_max * scale
        tiles = scores.shape[1] // HEAD_DIM
        weights = jnp.exp2(scores * scale - jnp.concatenate([shift] * tiles, axis=1))
        seen = values()
        widened = jnp.concatenate([seen, jnp.ones(seen.shape, jnp.bfloat16)], axis=1)
        product = jnp.dot(
            weights.astype(jnp.bfloat16), widened, preferred_element_type=jnp.float32
        )
        acc_ref[rows, :] = acc_ref[rows, :] * jnp.concatenate([factor, factor], axis=1) + product
        m_ref[rows, :] = new_max


def attend_kernel(causal, chunks, count_ref, q_ref, k_ref, v_ref, *refs):
    if causal:
        nk_ref, nv_ref, *refs = refs
    *o_refs, lse_ref, m_ref, acc_ref = refs
    scale = HEAD_DIM**-0.5 * LOG2E
    span = q_ref.shape[0]
    used = count_ref[0]
    parts = [pl.ds(i * ROW_BLOCK, ROW_BLOCK) for i in range(span // ROW_BLOCK)]
    m_ref[...] = jnp.full(m_ref.shape, LOWEST, jnp.float32)
    acc_ref[...] = jnp.zeros(acc_ref.shape, jnp.float32)
    k_all = k_ref.at[(0,) * (len(k_ref.shape) - 2)]
    v_all = v_ref.at[(0,) * (len(v_ref.shape) - 2)]

    def visit(block, masked):
        start = pl.multiple_of(block * KEY_BLOCK, KEY_BLOCK)
        mask = None
        if masked:
            place = lax.broadcasted_iota(jnp.int32, (1, KEY_BLOCK), 1)
            mask = place < used - start
        picked = pl.ds(start, KEY_BLOCK)
        jobs = [(rows, lambda: k_all[picked, :], lambda: v_all[picked, :], mask) for rows in parts]
        fold_keys(jobs, q_ref, m_ref, acc_ref)

    full = used // KEY_BLOCK
    pl.loop(0, full)(lambda block: visit(block, False))

    @pl.when(used % KEY_BLOCK > 0)
    def _():
        visit(full, True)

    if causal:
        jobs = []
        for i, rows in enumerate(parts):
            width = (i + 1) * ROW_BLOCK
            key_at = lax.broadcasted_iota(jnp.int32, (ROW_BLOCK, width), 1)
            row_at = lax.broadcasted_iota(jnp.int32, (ROW_BLOCK, width), 0) + i * ROW_BLOCK
            jobs.append(
                (
                    rows,
                    lambda width=width: nk_ref[:width, :],
                    lambda width=width: nv_ref[:width, :],
                    key_at <= row_at,
                )
            )
        fold_keys(jobs, q_ref, m_ref, acc_ref)

    shard_rows = o_refs[0].shape[1] * chunks
    piece = shard_rows // chunks
    for i, rows in enumerate(parts):
        total = acc_ref[rows, HEAD_DIM:]
        seen = total > 0.0
        safe = jnp.where(seen, total, 1.0)
        out = (acc_ref[rows, :HEAD_DIM] / safe).astype(jnp.bfloat16)
        for at in range(0, ROW_BLOCK, piece):
            shard, chunk = divmod(i * ROW_BLOCK + at, shard_rows)
            o_refs[chunk // piece][shard] = out[at : at + piece, :]
        lse = jnp.where(seen, m_ref[rows, :] * scale + jnp.log2(safe), LOWEST)
        lse_ref[0, :, rows] = jnp.transpose(lse)[:1, :]


def attend(count, groups, chunks, queries, cache, new_keys=None, new_values=None):
    span, width = queries.shape
    heads = width // HEAD_DIM
    rows = cache.shape[-2]
    causal = new_keys is not None
    by_head = pl.BlockSpec((span, HEAD_DIM), lambda h, n: (0, h))
    lead = cache.ndim - 3
    shape = (1,) * (lead + 1) + (rows, HEAD_DIM)
    piece = span // groups // chunks

    def half(which):
        return pl.BlockSpec(shape, lambda h, n: (0,) * lead + (which, 0, h))

    keys_seen = rows + (span // 2 if causal else 0)
    return pl.pallas_call(
        functools.partial(attend_kernel, causal, chunks),
        grid_spec=pltpu.PrefetchScalarGridSpec(
            num_scalar_prefetch=1,
            grid=(heads,),
            in_specs=[by_head, half(0), half(1)] + [by_head] * (2 if causal else 0),
            out_specs=[pl.BlockSpec((groups, piece, HEAD_DIM), lambda h, n: (0, 0, h))] * chunks
            + [pl.BlockSpec((1, 1, span), lambda h, n: (h, 0, 0))],
            scratch_shapes=[
                pltpu.VMEM((span, HEAD_DIM), jnp.float32),
                pltpu.VMEM((span, 2 * HEAD_DIM), jnp.float32),
            ],
        ),
        out_shape=[jax.ShapeDtypeStruct((groups, piece, width), jnp.bfloat16)] * chunks
        + [jax.ShapeDtypeStruct((heads, 1, span), jnp.float32)],
        compiler_params=params(),
        cost_estimate=pl.CostEstimate(
            flops=16 * span * keys_seen * width,
            bytes_accessed=4 * rows * width + 4 * span * width,
            transcendentals=span * keys_seen * heads,
        ),
        name="attend_own" if causal else "attend_guest",
    )(count, queries, cache, cache, *((new_keys, new_values) if causal else ()))


def merge_kernel(groups, heads, inverse_ref, own_ref, guest_ref, own_lse_ref, guest_lse_ref, w_ref, out_ref, att_ref):
    piece = own_ref.shape[1]

    @pl.when(pl.program_id(0) == 0)
    def _():
        def one_request(request, carry):
            source = inverse_ref[request]
            helper = lax.rem(source + groups // 2, groups)
            own_lse = own_lse_ref[source]
            guest_lse = guest_lse_ref[helper]
            top = jnp.maximum(own_lse, guest_lse)
            own_share = jnp.exp2(own_lse - top)
            guest_share = jnp.exp2(guest_lse - top)
            total = own_share + guest_share
            own_share = own_share / total
            guest_share = guest_share / total
            rows = pl.ds(pl.multiple_of(request * piece, piece), piece)
            for head in range(heads):
                cut = slice(head * HEAD_DIM, (head + 1) * HEAD_DIM)
                merged = own_ref[source, :, cut].astype(jnp.float32) * own_share[
                    :, head : head + 1
                ] + guest_ref[helper, :, cut].astype(jnp.float32) * guest_share[:, head : head + 1]
                att_ref[rows, cut] = merged.astype(jnp.bfloat16)
            return carry

        lax.fori_loop(0, groups, one_request, 0)

    out_ref[...] = jnp.dot(
        att_ref[...], w_ref[...], preferred_element_type=jnp.float32
    ).astype(jnp.bfloat16)


def merge(inverse, chunk, own, guest, own_lse, guest_lse, w_out):
    groups, piece, width = guest.shape
    heads = width // HEAD_DIM
    columns = w_out.shape[1]
    block = 512
    rows = groups * piece

    def part(last):
        return pl.BlockSpec((groups, piece, last), lambda n, i: (0, chunk, 0))

    return pl.pallas_call(
        functools.partial(merge_kernel, groups, heads),
        grid_spec=pltpu.PrefetchScalarGridSpec(
            num_scalar_prefetch=1,
            grid=(columns // block,),
            in_specs=[
                part(width),
                pl.BlockSpec(guest.shape, lambda n, i: (0, 0, 0)),
                part(heads),
                part(heads),
                pl.BlockSpec((width, block), lambda n, i: (0, n)),
            ],
            out_specs=pl.BlockSpec((rows, block), lambda n, i: (0, n)),
            scratch_shapes=[pltpu.VMEM((rows, width), jnp.bfloat16)],
        ),
        out_shape=jax.ShapeDtypeStruct((rows, columns), jnp.bfloat16),
        compiler_params=params(),
        cost_estimate=pl.CostEstimate(
            flops=4 * rows * width * columns,
            bytes_accessed=2 * (2 * rows * width + width * columns + rows * columns),
            transcendentals=0,
        ),
        name="merge",
    )(inverse, own, guest, own_lse, guest_lse, w_out)


def exchange(value):
    return lax.all_to_all(value, "grp", split_axis=0, concat_axis=0, tiled=True)


def shards(
    tokens,
    w_query,
    w_key,
    w_value,
    w_out,
    own_cache,
    guest_cache,
    rec_hidden,
    deal_order,
    own_len,
    guest_len,
    rec_index,
):
    groups = lax.axis_size("grp")
    tp_size = lax.axis_size("tp")
    group_id = lax.axis_index("grp")
    tp_id = lax.axis_index("tp")
    partner_id = (group_id + groups // 2) % groups
    width = w_query.shape[1]
    heads = width // HEAD_DIM
    shard_rows = tokens.shape[1]
    span = shard_rows * groups
    piece = shard_rows // tp_size

    chunks = 2
    tp_index = tp_id.astype(jnp.int32)[None]
    tied = lax.optimization_barrier

    if piece % 16 == 0:
        own_rows, guest_rows = deal(tokens, deal_order, tp_index, piece)
    else:
        mine = lax.dynamic_slice_in_dim(tokens, tp_id * piece, piece, 1)
        normed = layer_norm(mine).astype(jnp.bfloat16)
        own_rows = jnp.take(normed, deal_order, axis=0)
        guest_rows = jnp.roll(own_rows, groups // 2, axis=0)

    def gathered(arrived):
        if tp_size == 2 and piece % 16 == 0:
            return (arrived, lax.ppermute(arrived, "tp", [(0, 1), (1, 0)]))
        arrived = lax.all_gather(arrived, "tp", axis=0)
        return (jnp.transpose(arrived, (1, 0, 2, 3)).reshape(span, -1),)

    def place(owner, helper):
        return own_len[owner] + guest_len[helper] + jnp.arange(span, dtype=jnp.int32)

    own_arrived = exchange(own_rows)
    own_tables = rope_tables(place(group_id, partner_id))
    guest_tables = rope_tables(place(partner_id, group_id))
    rec_tables = rope_tables(rec_index[0])
    rec_rows = layer_norm(rec_hidden[0]).astype(jnp.bfloat16)
    rec_keys, rec_values = project((rec_rows,), tp_index, rec_tables, (w_key, w_value), (True, False))
    cache = replace_rows(own_cache, jnp.stack([rec_keys, rec_values]), rec_index)
    cache, own_tables, guest_tables, own_arrived, guest_rows = tied(
        (cache, own_tables, guest_tables, own_arrived, guest_rows)
    )

    own_x = gathered(own_arrived)
    guest_arrived = exchange(guest_rows)
    queries, new_keys, new_values = project(
        own_x, tp_index, own_tables, (w_query, w_key, w_value), (True, True, False)
    )
    guest_arrived, queries = tied((guest_arrived, queries))
    guest_x = gathered(guest_arrived)
    own_out, own_lse = attend(
        own_len[group_id][None], groups, 1, queries, cache, new_keys, new_values
    )
    guest_x, own_out = tied((guest_x, own_out))

    own_part = exchange(own_out)
    (guest_queries,) = project(guest_x, tp_index, guest_tables, (w_query,), (True,))
    *guest_out, guest_lse = attend(
        guest_len[group_id][None], groups, chunks, guest_queries, guest_cache
    )
    stats = lax.all_gather(jnp.concatenate([own_lse, guest_lse])[:, 0], "grp", axis=0)
    stats = lax.dynamic_slice_in_dim(stats, group_id * shard_rows, shard_rows, 2)
    stats = jnp.transpose(stats, (0, 2, 1))
    own_stats, guest_stats = stats[..., :heads], stats[..., heads:]

    inverse = jnp.sum(
        jnp.where(
            deal_order[None, :] == jnp.arange(groups, dtype=deal_order.dtype)[:, None],
            jnp.arange(groups, dtype=jnp.int32)[None, :],
            0,
        ),
        axis=1,
    )
    mixed = []
    for chunk in range(chunks):
        guest_part = exchange(guest_out[chunk])
        if chunk + 1 < chunks:
            guest_part, guest_out[chunk + 1] = tied((guest_part, guest_out[chunk + 1]))
        partial = merge(inverse, chunk, own_part, guest_part, own_stats, guest_stats, w_out)
        summed = lax.psum_scatter(partial, "tp", scatter_dimension=1, tiled=True)
        mixed.append(summed.reshape(groups, shard_rows // chunks, -1))
    return jnp.concatenate(mixed, axis=1)


def solution(mesh):
    return jax.shard_map(
        shards,
        mesh=mesh,
        in_specs=(
            P(None, "grp", None),
            P(None, "tp"),
            P(None, "tp"),
            P(None, "tp"),
            P("tp", None),
            P("grp", None, None, "tp"),
            P("grp", None, None, "tp"),
            P("grp", None, None),
            P(),
            P(),
            P(),
            P("grp", None),
        ),
        out_specs=P(None, "grp", "tp"),
        check_vma=False,
    )
```

```python
import functools
import math

import jax
import jax.numpy as jnp
from jax import lax
from jax.experimental import pallas as pl
from jax.experimental.pallas import tpu as pltpu
from jax.sharding import PartitionSpec as P

HEAD_DIM = 128
KEY_BLOCK = 1024
ROW_BLOCK = 256
STATS = 128
VMEM_LIMIT = 50 * 1024 * 1024

rope_base = 10000.0
norm_eps = 1e-05
LOG2E = math.log2(math.e)
LOWEST = -1e30


def params():
    return pltpu.CompilerParams(vmem_limit_bytes=VMEM_LIMIT)


def layer_norm(token_rows):
    widened = token_rows.astype(jnp.float32)
    centred = widened - jnp.mean(widened, axis=-1, keepdims=True)
    variance = jnp.mean(centred * centred, axis=-1, keepdims=True)
    return centred * lax.rsqrt(variance + norm_eps)


def rope_tables(positions):
    half_dim = HEAD_DIM // 2
    frequency = jnp.exp(-jnp.log(rope_base) * jnp.arange(half_dim, dtype=jnp.float32) / half_dim)
    angles = positions.astype(jnp.float32)[:, None] * frequency[None, :]
    cosine = jnp.cos(angles)
    sine = jnp.sin(angles)
    return (
        jnp.concatenate([cosine, cosine], axis=-1),
        jnp.concatenate([-sine, sine], axis=-1),
    )


def deal_kernel(order_ref, tp_ref, x_ref, first_ref, second_ref, guest_ref):
    each, cut, _ = first_ref.shape
    start = pl.program_id(0) * each
    for at in range(each):
        normed = layer_norm(x_ref[order_ref[start + at]]).astype(jnp.bfloat16)
        first_ref[at] = normed[:cut]
        second_ref[at] = normed[cut:]
        guest_ref[at] = normed


def deal(tokens, deal_order, tp_index, piece):
    groups, _, width = tokens.shape
    each = 4
    steps = groups // each
    cut = piece // 2
    return pl.pallas_call(
        deal_kernel,
        grid_spec=pltpu.PrefetchScalarGridSpec(
            num_scalar_prefetch=2,
            grid=(steps,),
            in_specs=[pl.BlockSpec((groups, piece, width), lambda d, order, t: (0, t[0], 0))],
            out_specs=[
                pl.BlockSpec((each, cut, width), lambda d, order, t: (d, 0, 0)),
                pl.BlockSpec((each, cut, width), lambda d, order, t: (d, 0, 0)),
                pl.BlockSpec(
                    (each, piece, width), lambda d, order, t: ((d + steps // 2) % steps, 0, 0)
                ),
            ],
        ),
        out_shape=[
            jax.ShapeDtypeStruct((groups, rows, width), jnp.bfloat16) for rows in (cut, cut, piece)
        ],
        compiler_params=params(),
        name="deal",
    )(deal_order, tp_index, tokens)


def project_kernel(turned, heads, sources, tp_ref, *refs):
    if sources > 1:
        part_refs, (cos_ref, sin_ref, *refs, x_ref) = refs[:sources], refs[sources:]
        shards_in = part_refs[0].shape[0]
        half = x_ref.shape[0] // 2
        each = half // shards_in

        @pl.when(pl.program_id(0) == 0)
        def _():
            t = tp_ref[0]
            for shard in range(shards_in):
                at = shard * each
                for mine_ref, other_ref in zip(part_refs[::2], part_refs[1::2]):
                    piece = mine_ref.shape[1]
                    for part_ref, side in ((mine_ref, t), (other_ref, 1 - t)):
                        start = pl.multiple_of(side * half + at, piece)
                        x_ref[pl.ds(start, piece), :] = part_ref[shard]
                    at += piece
    else:
        x_ref, cos_ref, sin_ref, *refs = refs
    count = len(turned)
    step = min(256, x_ref.shape[0])
    for first in range(0, x_ref.shape[0], step):
        rows = slice(first, first + step)
        for w_ref, out_ref, turn in zip(refs[:count], refs[count:], turned):
            product = jnp.dot(x_ref[rows, :], w_ref[...], preferred_element_type=jnp.float32)
            if not turn:
                out_ref[rows, :] = product.astype(jnp.bfloat16)
                continue
            for head in range(heads):
                cut = slice(head * HEAD_DIM, (head + 1) * HEAD_DIM)
                part = product[:, cut]
                swapped = pltpu.roll(part, HEAD_DIM // 2, 1)
                out_ref[rows, cut] = (
                    part * cos_ref[rows, :] + swapped * sin_ref[rows, :]
                ).astype(jnp.bfloat16)


def project(x, tp_index, tables, weights, turned):
    depth = x[0].shape[-1]
    rows = sum(math.prod(part.shape[:-1]) for part in x)
    width = weights[0].shape[1]
    block = min(256, width)
    table = pl.BlockSpec((rows, HEAD_DIM), lambda n, t: (0, 0))
    count = len(weights)
    return pl.pallas_call(
        functools.partial(project_kernel, turned, block // HEAD_DIM, len(x)),
        grid_spec=pltpu.PrefetchScalarGridSpec(
            num_scalar_prefetch=1,
            grid=(width // block,),
            in_specs=[pl.BlockSpec(part.shape, lambda n, t, r=part.ndim: (0,) * r) for part in x]
            + [table, table]
            + [pl.BlockSpec((depth, block), lambda n, t: (0, n))] * count,
            out_specs=[pl.BlockSpec((rows, block), lambda n, t: (0, n))] * count,
            scratch_shapes=[pltpu.VMEM((rows, depth), jnp.bfloat16)] if len(x) > 1 else [],
        ),
        out_shape=[jax.ShapeDtypeStruct((rows, width), jnp.bfloat16)] * count,
        compiler_params=params(),
        cost_estimate=pl.CostEstimate(
            flops=2 * rows * depth * width * count,
            bytes_accessed=2 * (rows * depth + count * width * (rows + depth)),
            transcendentals=0,
        ),
        name="project",
    )(tp_index, *x, *tables, *weights)


def replace_kernel(block, index_ref, cache_ref, fresh_ref, out_ref):
    first = pl.program_id(1) * block
    count = index_ref.shape[1]
    row = first + lax.broadcasted_iota(jnp.int32, (block, count), 0)
    hits = jnp.where(row == index_ref[...], 1.0, 0.0)
    picked = jnp.dot(
        hits.astype(jnp.bfloat16), fresh_ref[0], preferred_element_type=jnp.float32
    )
    is_hit = jnp.sum(hits, axis=1, keepdims=True) > 0.5
    out_ref[0] = jnp.where(is_hit, picked, cache_ref[0, 0].astype(jnp.float32)).astype(jnp.bfloat16)


def replace_rows(cache, fresh, rec_index):
    _, _, rows, width = cache.shape
    count = rec_index.shape[1]
    block = 512
    return pl.pallas_call(
        functools.partial(replace_kernel, block),
        grid=(2, rows // block),
        in_specs=[
            pl.BlockSpec((1, count), lambda c, r: (0, 0)),
            pl.BlockSpec((1, 1, block, width), lambda c, r: (0, c, r, 0)),
            pl.BlockSpec((1, count, width), lambda c, r: (c, 0, 0)),
        ],
        out_specs=pl.BlockSpec((1, block, width), lambda c, r: (c, r, 0)),
        out_shape=jax.ShapeDtypeStruct((2, rows, width), jnp.bfloat16),
        compiler_params=params(),
        cost_estimate=pl.CostEstimate(
            flops=4 * rows * count * width, bytes_accessed=10 * rows * width, transcendentals=0
        ),
        name="replace_rows",
    )(rec_index, cache, fresh)


def fold_keys(jobs, m_ref, acc_ref):
    scale = HEAD_DIM**-0.5 * LOG2E

    def scores_of(job):
        _, queries, keys, _, mask = job
        scores = lax.dot_general(
            queries(), keys(), (((1,), (1,)), ((), ())), preferred_element_type=jnp.float32
        )
        return scores if mask is None else jnp.where(mask, scores, LOWEST)

    upcoming = scores_of(jobs[0])
    for at, (place, _, _, values, _) in enumerate(jobs):
        scores = upcoming
        if at + 1 < len(jobs):
            upcoming = scores_of(jobs[at + 1])
        old_max = m_ref[place]
        new_max = jnp.maximum(old_max, jnp.max(scores, axis=1, keepdims=True))
        factor = jnp.exp2((old_max - new_max) * scale)
        shift = new_max * scale
        tiles = scores.shape[1] // HEAD_DIM
        weights = jnp.exp2(scores * scale - jnp.concatenate([shift] * tiles, axis=1))
        seen = values()
        widened = jnp.concatenate([seen, jnp.ones(seen.shape, jnp.bfloat16)], axis=1)
        product = jnp.dot(
            weights.astype(jnp.bfloat16), widened, preferred_element_type=jnp.float32
        )
        acc_ref[place] = acc_ref[place] * jnp.concatenate([factor, factor], axis=1) + product
        m_ref[place] = new_max


def attend_kernel(causal, chunk, chunks, piece, count_ref, q_ref, k_ref, v_ref, *refs):
    if causal:
        nk_ref, nv_ref, *refs = refs
    o_ref, lse_ref, m_ref, acc_ref = refs
    scale = HEAD_DIM**-0.5 * LOG2E
    rows_in = q_ref.shape[0]
    per_step = q_ref.shape[1] // HEAD_DIM
    step = pl.program_id(0)
    used = count_ref[0]
    blocks = range(rows_in // ROW_BLOCK)
    places = [(head, block) for head in range(per_step) for block in blocks]
    m_ref[...] = jnp.full(m_ref.shape, LOWEST, jnp.float32)
    acc_ref[...] = jnp.zeros(acc_ref.shape, jnp.float32)
    k_all = k_ref.at[(0,) * (len(k_ref.shape) - 2)]
    v_all = v_ref.at[(0,) * (len(v_ref.shape) - 2)]

    def head_cut(head):
        return slice(head * HEAD_DIM, (head + 1) * HEAD_DIM)

    def rows_of(block):
        return slice(block * ROW_BLOCK, (block + 1) * ROW_BLOCK)

    def job(place, keys_ref, values_ref, picked, mask):
        head, block = place
        cut = head_cut(head)
        return (
            place,
            lambda: q_ref[rows_of(block), cut],
            lambda: keys_ref[picked, cut],
            lambda: values_ref[picked, cut],
            mask,
        )

    def visit(block, masked):
        start = pl.multiple_of(block * KEY_BLOCK, KEY_BLOCK)
        mask = None
        if masked:
            mask = lax.broadcasted_iota(jnp.int32, (1, KEY_BLOCK), 1) < used - start
        picked = pl.ds(start, KEY_BLOCK)
        fold_keys([job(place, k_all, v_all, picked, mask) for place in places], m_ref, acc_ref)

    full = used // KEY_BLOCK
    pl.loop(0, full)(lambda block: visit(block, False))

    @pl.when(used % KEY_BLOCK > 0)
    def _():
        visit(full, True)

    if causal:
        shards_each = ROW_BLOCK // piece
        jobs = []
        for place in places:
            row = lax.broadcasted_iota(jnp.int32, (ROW_BLOCK, ROW_BLOCK), 0)
            key = lax.broadcasted_iota(jnp.int32, (ROW_BLOCK, ROW_BLOCK), 1)
            row_shard, key_shard = row // piece, key // piece
            for key_chunk in range(chunks):
                same = key % piece <= row % piece if key_chunk == chunk else key_chunk < chunk
                mask = (key_shard < row_shard) | ((key_shard == row_shard) & same)
                first = key_chunk * rows_in
                for key_block in range(place[1] + 1):
                    at = first + key_block * ROW_BLOCK
                    picked = slice(at, at + ROW_BLOCK)
                    is_last = key_block == place[1]
                    jobs.append(job(place, nk_ref, nv_ref, picked, mask if is_last else None))
        fold_keys(jobs, m_ref, acc_ref)

    for head, block in places:
        rows = rows_of(block)
        total = acc_ref[head, block, :, HEAD_DIM:]
        seen = total > 0.0
        safe = jnp.where(seen, total, 1.0)
        out = (acc_ref[head, block, :, :HEAD_DIM] / safe).astype(jnp.bfloat16)
        column = step * per_step + head
        o_ref[rows, pl.ds(pl.multiple_of(column * HEAD_DIM, HEAD_DIM), HEAD_DIM)] = out
        lse = jnp.where(seen, m_ref[head, block] * scale + jnp.log2(safe), LOWEST)
        lane = lax.broadcasted_iota(jnp.int32, (ROW_BLOCK, STATS), 1)
        before = jnp.where(column == 0, 0.0, lse_ref[rows, :])
        lse_ref[rows, :] = jnp.where(lane == column, lse, before)

    @pl.when(step == pl.num_programs(0) - 1)
    def _():
        for block in blocks:
            rows = rows_of(block)
            left = lse_ref[rows, :]
            packed = jnp.zeros_like(left)
            for turn in range(3):
                part = left.astype(jnp.bfloat16).astype(jnp.float32)
                left = left - part
                packed = packed + (pltpu.roll(part, turn * STATS // 4, 1) if turn else part)
            o_ref[rows, o_ref.shape[1] - STATS :] = packed.astype(jnp.bfloat16)


def attend(count, groups, chunk, chunks, queries, cache, new_keys=None, new_values=None):
    span, width = queries.shape
    heads = width // HEAD_DIM
    per_step = 2
    rows = cache.shape[-2]
    causal = new_keys is not None
    rows_in = span // chunks
    lead = cache.ndim - 3
    shape = (1,) * (lead + 1) + (rows, per_step * HEAD_DIM)
    every = pl.BlockSpec((span, per_step * HEAD_DIM), lambda h, n: (0, h))

    def half(which):
        return pl.BlockSpec(shape, lambda h, n: (0,) * lead + (which, 0, h))

    keys_seen = rows + (span // 2 if causal else 0)
    out = pl.pallas_call(
        functools.partial(attend_kernel, causal, chunk, chunks, rows_in // groups),
        grid_spec=pltpu.PrefetchScalarGridSpec(
            num_scalar_prefetch=1,
            grid=(heads // per_step,),
            in_specs=[
                pl.BlockSpec((rows_in, per_step * HEAD_DIM), lambda h, n: (chunk, h)),
                half(0),
                half(1),
            ]
            + [every] * (2 if causal else 0),
            out_specs=pl.BlockSpec((rows_in, width + STATS), lambda h, n: (0, 0)),
            scratch_shapes=[
                pltpu.VMEM((rows_in, STATS), jnp.float32),
                pltpu.VMEM((per_step, rows_in // ROW_BLOCK, ROW_BLOCK, HEAD_DIM), jnp.float32),
                pltpu.VMEM((per_step, rows_in // ROW_BLOCK, ROW_BLOCK, 2 * HEAD_DIM), jnp.float32),
            ],
        ),
        out_shape=jax.ShapeDtypeStruct((rows_in, width + STATS), jnp.bfloat16),
        compiler_params=params(),
        cost_estimate=pl.CostEstimate(
            flops=16 * rows_in * keys_seen * width,
            bytes_accessed=4 * rows * width + 4 * rows_in * width,
            transcendentals=rows_in * keys_seen * heads,
        ),
        name="attend_own" if causal else "attend_guest",
    )(count, queries, cache, cache, *((new_keys, new_values) if causal else ()))
    return out.reshape(groups, rows_in // groups, width + STATS)


def merge_kernel(groups, heads, inverse_ref, tp_ref, own_ref, guest_ref, w_ref, *refs):
    *out_refs, att_ref = refs
    piece = own_ref.shape[1]
    width = heads * HEAD_DIM
    step = pl.program_id(0)

    def stats(part_ref, at):
        packed = part_ref[at, :, width:].astype(jnp.float32)
        return (
            packed
            + pltpu.roll(packed, STATS - STATS // 4, 1)
            + pltpu.roll(packed, STATS - STATS // 2, 1)
        )

    @pl.when(step == 0)
    def _():
        def one_request(request, carry):
            source = inverse_ref[request]
            helper = lax.rem(source + groups // 2, groups)
            own_lse = stats(own_ref, source)
            guest_lse = stats(guest_ref, helper)
            top = jnp.maximum(own_lse, guest_lse)
            own_share = jnp.exp2(own_lse - top)
            guest_share = jnp.exp2(guest_lse - top)
            total = own_share + guest_share
            own_share = own_share / total
            guest_share = guest_share / total
            rows = pl.ds(pl.multiple_of(request * piece, piece), piece)
            for head in range(heads):
                cut = slice(head * HEAD_DIM, (head + 1) * HEAD_DIM)
                merged = own_ref[source, :, cut].astype(jnp.float32) * own_share[
                    :, head : head + 1
                ] + guest_ref[helper, :, cut].astype(jnp.float32) * guest_share[:, head : head + 1]
                att_ref[rows, cut] = merged.astype(jnp.bfloat16)
            return carry

        lax.fori_loop(0, groups, one_request, 0)

    product = jnp.dot(att_ref[...], w_ref[...], preferred_element_type=jnp.float32).astype(
        jnp.bfloat16
    )
    each = pl.num_programs(0) // len(out_refs)
    for at, out_ref in enumerate(out_refs):
        pl.when(step // each == at)(functools.partial(out_ref.__setitem__, ..., product))


def merge(inverse, tp_index, splits, own, guest, w_out):
    groups, piece, padded = guest.shape
    width = w_out.shape[0]
    heads = width // HEAD_DIM
    columns = w_out.shape[1]
    block = 512
    rows = groups * piece
    steps = columns // block
    each = steps // splits

    def w_at(n, i, t):
        return (0, (n + each * (1 - t[0])) % steps if splits == 2 else n)

    def out_at(which):
        return lambda n, i, t: (0, jnp.clip(n - which * each, 0, each - 1))

    part = pl.BlockSpec(guest.shape, lambda n, i, t: (0, 0, 0))
    return pl.pallas_call(
        functools.partial(merge_kernel, groups, heads),
        grid_spec=pltpu.PrefetchScalarGridSpec(
            num_scalar_prefetch=2,
            grid=(steps,),
            in_specs=[part, part, pl.BlockSpec((width, block), w_at)],
            out_specs=[pl.BlockSpec((rows, block), out_at(which)) for which in range(splits)],
            scratch_shapes=[pltpu.VMEM((rows, width), jnp.bfloat16)],
        ),
        out_shape=[jax.ShapeDtypeStruct((rows, columns // splits), jnp.bfloat16)] * splits,
        compiler_params=params(),
        cost_estimate=pl.CostEstimate(
            flops=4 * rows * width * columns,
            bytes_accessed=2 * (2 * rows * padded + width * columns + rows * columns),
            transcendentals=0,
        ),
        name="merge",
    )(inverse, tp_index, own, guest, w_out)


def exchange(value):
    return lax.all_to_all(value, "grp", split_axis=0, concat_axis=0, tiled=True)


def shards(
    tokens,
    w_query,
    w_key,
    w_value,
    w_out,
    own_cache,
    guest_cache,
    rec_hidden,
    deal_order,
    own_len,
    guest_len,
    rec_index,
):
    groups = lax.axis_size("grp")
    tp_size = lax.axis_size("tp")
    group_id = lax.axis_index("grp")
    tp_id = lax.axis_index("tp")
    partner_id = (group_id + groups // 2) % groups
    width = w_query.shape[1]
    heads = width // HEAD_DIM
    shard_rows = tokens.shape[1]
    span = shard_rows * groups
    piece = shard_rows // tp_size

    chunks = 2
    chunk_rows = shard_rows // chunks
    paired = tp_size == 2 and piece % 32 == 0
    tp_index = tp_id.astype(jnp.int32)[None]
    tied = lax.optimization_barrier
    neighbour = [(0, 1), (1, 0)]

    if paired:
        *own_rows, guest_rows = deal(tokens, deal_order, tp_index, piece)
    else:
        mine = lax.dynamic_slice_in_dim(tokens, tp_id * piece, piece, 1)
        normed = layer_norm(mine).astype(jnp.bfloat16)
        own_rows = [jnp.take(normed, deal_order, axis=0)]
        guest_rows = jnp.roll(own_rows[0], groups // 2, axis=0)

    def gathered(arrived):
        if paired:
            return [arrived, lax.ppermute(arrived, "tp", neighbour)]
        arrived = lax.all_gather(arrived, "tp", axis=0)
        arrived = jnp.transpose(arrived, (1, 0, 2, 3)).reshape(groups, chunks, chunk_rows, -1)
        return [jnp.transpose(arrived, (1, 0, 2, 3)).reshape(span, -1)]

    def place(owner, helper):
        row = jnp.arange(span, dtype=jnp.int32).reshape(groups, chunks, chunk_rows)
        row = jnp.transpose(row, (1, 0, 2)).reshape(span)
        return own_len[owner] + guest_len[helper] + row

    own_x = gathered(exchange(own_rows[0]))
    if paired:
        own_x[0], own_rows[1] = tied((own_x[0], own_rows[1]))
        second = exchange(own_rows[1])
    own_tables = rope_tables(place(group_id, partner_id))
    guest_tables = rope_tables(place(partner_id, group_id))
    rec_tables = rope_tables(rec_index[0])
    rec_rows = layer_norm(rec_hidden[0]).astype(jnp.bfloat16)
    rec_keys, rec_values = project((rec_rows,), tp_index, rec_tables, (w_key, w_value), (True, False))
    cache = replace_rows(own_cache, jnp.stack([rec_keys, rec_values]), rec_index)
    if paired:
        second, cache, own_tables, guest_tables, own_x, guest_rows = tied(
            (second, cache, own_tables, guest_tables, own_x, guest_rows)
        )
        own_x = own_x + gathered(second)

    guest_arrived = exchange(guest_rows)
    queries, new_keys, new_values = project(
        own_x, tp_index, own_tables, (w_query, w_key, w_value), (True, True, False)
    )
    guest_arrived, queries = tied((guest_arrived, queries))
    guest_x = gathered(guest_arrived)

    def own_attend(chunk, seen):
        return attend(own_len[group_id][None], groups, chunk, chunks, seen, cache, new_keys, new_values)

    def guest_attend(chunk, seen):
        return attend(guest_len[group_id][None], groups, chunk, chunks, seen, guest_cache)

    own_out = [own_attend(0, queries)]
    own_out[0], queries = tied((own_out[0], queries))
    own_out.append(own_attend(1, queries))
    own_part = [exchange(own_out[0])]
    guest_x, own_out[1] = tied((guest_x, own_out[1]))
    (guest_queries,) = project(guest_x, tp_index, guest_tables, (w_query,), (True,))
    own_part[0], guest_queries, own_out[1] = tied((own_part[0], guest_queries, own_out[1]))
    own_part.append(exchange(own_out[1]))
    guest_out = [guest_attend(0, guest_queries)]
    guest_out[0], guest_queries = tied((guest_out[0], guest_queries))
    guest_out.append(guest_attend(1, guest_queries))
    own_part[1], guest_out = tied((own_part[1], guest_out))

    inverse = jnp.sum(
        jnp.where(
            deal_order[None, :] == jnp.arange(groups, dtype=deal_order.dtype)[:, None],
            jnp.arange(groups, dtype=jnp.int32)[None, :],
            0,
        ),
        axis=1,
    )
    guest_part = [exchange(guest_out[0])]
    guest_part[0], guest_out[1] = tied((guest_part[0], guest_out[1]))
    guest_part.append(exchange(guest_out[1]))
    mixed = []
    for chunk in range(chunks):
        partial = merge(
            inverse, tp_index, 2 if paired else 1, own_part[chunk], guest_part[chunk], w_out
        )
        if chunk == 0:
            partial, guest_part[1] = tied((partial, guest_part[1]))
        if paired:
            theirs, mine = partial
            arrived = lax.ppermute(theirs, "tp", neighbour).astype(jnp.float32)
            summed = (mine.astype(jnp.float32) + arrived).astype(jnp.bfloat16)
        else:
            summed = lax.psum_scatter(partial[0], "tp", scatter_dimension=1, tiled=True)
        mixed.append(summed.reshape(groups, chunk_rows, -1))
    return jnp.concatenate(mixed, axis=1)


def solution(mesh):
    return jax.shard_map(
        shards,
        mesh=mesh,
        in_specs=(
            P(None, "grp", None),
            P(None, "tp"),
            P(None, "tp"),
            P(None, "tp"),
            P("tp", None),
            P("grp", None, None, "tp"),
            P("grp", None, None, "tp"),
            P("grp", None, None),
            P(),
            P(),
            P(),
            P("grp", None),
        ),
        out_specs=P(None, "grp", "tp"),
        check_vma=False,
    )
```

```python
import functools
import math

import jax
import jax.numpy as jnp
from jax import lax
from jax.experimental import pallas as pl
from jax.experimental.pallas import tpu as pltpu
from jax.sharding import PartitionSpec as P

HEAD_DIM = 128
KEY_BLOCK = 1024
ROW_BLOCK = 256
STATS = 128
VMEM_LIMIT = 50 * 1024 * 1024
ATTEND_LIMIT = 60 * 1024 * 1024

rope_base = 10000.0
norm_eps = 1e-05
LOG2E = math.log2(math.e)
LOWEST = -1e30


def params(limit=VMEM_LIMIT):
    return pltpu.CompilerParams(vmem_limit_bytes=limit)


def layer_norm(token_rows):
    widened = token_rows.astype(jnp.float32)
    centred = widened - jnp.mean(widened, axis=-1, keepdims=True)
    variance = jnp.mean(centred * centred, axis=-1, keepdims=True)
    return centred * lax.rsqrt(variance + norm_eps)


def rope_tables(positions):
    half_dim = HEAD_DIM // 2
    frequency = jnp.exp(-jnp.log(rope_base) * jnp.arange(half_dim, dtype=jnp.float32) / half_dim)
    angles = positions.astype(jnp.float32)[:, None] * frequency[None, :]
    cosine = jnp.cos(angles)
    sine = jnp.sin(angles)
    return (
        jnp.concatenate([cosine, cosine], axis=-1),
        jnp.concatenate([-sine, sine], axis=-1),
    )


def deal_kernel(order_ref, tp_ref, x_ref, first_ref, second_ref, guest_ref):
    each, cut, _ = first_ref.shape
    start = pl.program_id(0) * each
    for at in range(each):
        normed = layer_norm(x_ref[order_ref[start + at]]).astype(jnp.bfloat16)
        first_ref[at] = normed[:cut]
        second_ref[at] = normed[cut:]
        guest_ref[at] = normed


def deal(tokens, deal_order, tp_index, piece):
    groups, _, width = tokens.shape
    each = 4
    steps = groups // each
    cut = piece // 2
    return pl.pallas_call(
        deal_kernel,
        grid_spec=pltpu.PrefetchScalarGridSpec(
            num_scalar_prefetch=2,
            grid=(steps,),
            in_specs=[pl.BlockSpec((groups, piece, width), lambda d, order, t: (0, t[0], 0))],
            out_specs=[
                pl.BlockSpec((each, cut, width), lambda d, order, t: (d, 0, 0)),
                pl.BlockSpec((each, cut, width), lambda d, order, t: (d, 0, 0)),
                pl.BlockSpec(
                    (each, piece, width), lambda d, order, t: ((d + steps // 2) % steps, 0, 0)
                ),
            ],
        ),
        out_shape=[
            jax.ShapeDtypeStruct((groups, rows, width), jnp.bfloat16) for rows in (cut, cut, piece)
        ],
        compiler_params=params(),
        name="deal",
    )(deal_order, tp_index, tokens)


def project_kernel(turned, heads, sources, cut, tp_ref, *refs):
    if sources > 1:
        mine_ref, other_ref, cos_ref, sin_ref, *refs, x_ref = refs
        shards_in, rows_each, _ = mine_ref.shape

        @pl.when(pl.program_id(0) == 0)
        def _():
            t = tp_ref[0]
            for piece in range(rows_each // cut):
                rows = slice(piece * cut, (piece + 1) * cut)
                for shard in range(shards_in):
                    at = (piece * shards_in + shard) * 2
                    for part_ref, side in ((mine_ref, t), (other_ref, 1 - t)):
                        start = pl.multiple_of((at + side) * cut, cut)
                        x_ref[pl.ds(start, cut), :] = part_ref[shard, rows, :]
    else:
        x_ref, cos_ref, sin_ref, *refs = refs
    count = len(turned)
    step = min(256, x_ref.shape[0])
    for first in range(0, x_ref.shape[0], step):
        rows = slice(first, first + step)
        for w_ref, out_ref, turn in zip(refs[:count], refs[count:], turned):
            product = jnp.dot(x_ref[rows, :], w_ref[...], preferred_element_type=jnp.float32)
            if not turn:
                out_ref[rows, :] = product.astype(jnp.bfloat16)
                continue
            for head in range(heads):
                cut = slice(head * HEAD_DIM, (head + 1) * HEAD_DIM)
                part = product[:, cut]
                swapped = pltpu.roll(part, HEAD_DIM // 2, 1)
                out_ref[rows, cut] = (
                    part * cos_ref[rows, :] + swapped * sin_ref[rows, :]
                ).astype(jnp.bfloat16)


def project(x, cut, tp_index, tables, weights, turned):
    depth = x[0].shape[-1]
    rows = sum(math.prod(part.shape[:-1]) for part in x)
    width = weights[0].shape[1]
    block = min(256, width)
    table = pl.BlockSpec((rows, HEAD_DIM), lambda n, t: (0, 0))
    count = len(weights)
    return pl.pallas_call(
        functools.partial(project_kernel, turned, block // HEAD_DIM, len(x), cut),
        grid_spec=pltpu.PrefetchScalarGridSpec(
            num_scalar_prefetch=1,
            grid=(width // block,),
            in_specs=[pl.BlockSpec(part.shape, lambda n, t, r=part.ndim: (0,) * r) for part in x]
            + [table, table]
            + [pl.BlockSpec((depth, block), lambda n, t: (0, n))] * count,
            out_specs=[pl.BlockSpec((rows, block), lambda n, t: (0, n))] * count,
            scratch_shapes=[pltpu.VMEM((rows, depth), jnp.bfloat16)] if len(x) > 1 else [],
        ),
        out_shape=[jax.ShapeDtypeStruct((rows, width), jnp.bfloat16)] * count,
        compiler_params=params(),
        cost_estimate=pl.CostEstimate(
            flops=2 * rows * depth * width * count,
            bytes_accessed=2 * (rows * depth + count * width * (rows + depth)),
            transcendentals=0,
        ),
        name="project",
    )(tp_index, *x, *tables, *weights)


def replace_kernel(block, index_ref, cache_ref, fresh_ref, out_ref):
    first = pl.program_id(1) * block
    count = index_ref.shape[1]
    row = first + lax.broadcasted_iota(jnp.int32, (block, count), 0)
    hits = jnp.where(row == index_ref[...], 1.0, 0.0)
    picked = jnp.dot(
        hits.astype(jnp.bfloat16), fresh_ref[0], preferred_element_type=jnp.float32
    )
    is_hit = jnp.sum(hits, axis=1, keepdims=True) > 0.5
    out_ref[0] = jnp.where(is_hit, picked, cache_ref[0, 0].astype(jnp.float32)).astype(jnp.bfloat16)


def replace_rows(cache, fresh, rec_index):
    _, _, rows, width = cache.shape
    count = rec_index.shape[1]
    block = 512
    return pl.pallas_call(
        functools.partial(replace_kernel, block),
        grid=(2, rows // block),
        in_specs=[
            pl.BlockSpec((1, count), lambda c, r: (0, 0)),
            pl.BlockSpec((1, 1, block, width), lambda c, r: (0, c, r, 0)),
            pl.BlockSpec((1, count, width), lambda c, r: (c, 0, 0)),
        ],
        out_specs=pl.BlockSpec((1, block, width), lambda c, r: (c, r, 0)),
        out_shape=jax.ShapeDtypeStruct((2, rows, width), jnp.bfloat16),
        compiler_params=params(),
        cost_estimate=pl.CostEstimate(
            flops=4 * rows * count * width, bytes_accessed=10 * rows * width, transcendentals=0
        ),
        name="replace_rows",
    )(rec_index, cache, fresh)


def fold_keys(jobs, m_ref, acc_ref):
    scale = HEAD_DIM**-0.5 * LOG2E

    def scores_of(job):
        _, queries, keys, _ = job
        parts = []
        for key_block, mask in keys():
            scores = lax.dot_general(
                queries(), key_block, (((1,), (1,)), ((), ())), preferred_element_type=jnp.float32
            )
            parts.append(scores if mask is None else jnp.where(mask, scores, LOWEST))
        return parts[0] if len(parts) == 1 else jnp.concatenate(parts, axis=1)

    upcoming = scores_of(jobs[0])
    for at, (place, _, _, values) in enumerate(jobs):
        scores = upcoming
        if at + 1 < len(jobs):
            upcoming = scores_of(jobs[at + 1])
        old_max = m_ref[place]
        new_max = jnp.maximum(old_max, jnp.max(scores, axis=1, keepdims=True))
        factor = jnp.exp2((old_max - new_max) * scale)
        shift = new_max * scale
        tiles = scores.shape[1] // HEAD_DIM
        weights = jnp.exp2(scores * scale - jnp.concatenate([shift] * tiles, axis=1))
        seen = values()
        widened = jnp.concatenate([seen, jnp.ones(seen.shape, jnp.bfloat16)], axis=1)
        product = jnp.dot(
            weights.astype(jnp.bfloat16), widened, preferred_element_type=jnp.float32
        )
        acc_ref[place] = acc_ref[place] * jnp.concatenate([factor, factor], axis=1) + product
        m_ref[place] = new_max


def attend_kernel(causal, chunk, chunks, piece, sides, count_ref, q_ref, k_ref, v_ref, *refs):
    if causal:
        new_refs, refs = refs[: 2 * chunks], refs[2 * chunks :]
    o_ref, lse_ref, m_ref, acc_ref = refs
    scale = HEAD_DIM**-0.5 * LOG2E
    rows_in = q_ref.shape[0]
    per_step = q_ref.shape[1] // HEAD_DIM
    step = pl.program_id(0)
    used = count_ref[0]
    blocks = range(rows_in // ROW_BLOCK)
    places = [(head, block) for head in range(per_step) for block in blocks]
    m_ref[...] = jnp.full(m_ref.shape, LOWEST, jnp.float32)
    acc_ref[...] = jnp.zeros(acc_ref.shape, jnp.float32)
    k_all = k_ref.at[(0,) * (len(k_ref.shape) - 2)]
    v_all = v_ref.at[(0,) * (len(v_ref.shape) - 2)]

    def head_cut(head):
        return slice(head * HEAD_DIM, (head + 1) * HEAD_DIM)

    def rows_of(block):
        return slice(block * ROW_BLOCK, (block + 1) * ROW_BLOCK)

    def job(place, picks):
        head, block = place
        cut = head_cut(head)

        def values():
            found = [values_ref[at, cut] for _, values_ref, at, _ in picks]
            return found[0] if len(found) == 1 else jnp.concatenate(found, axis=0)

        return (
            place,
            lambda: q_ref[rows_of(block), cut],
            lambda: [(keys_ref[at, cut], mask) for keys_ref, _, at, mask in picks],
            values,
        )

    def visit(block, masked):
        start = pl.multiple_of(block * KEY_BLOCK, KEY_BLOCK)
        mask = None
        if masked:
            mask = lax.broadcasted_iota(jnp.int32, (1, KEY_BLOCK), 1) < used - start
        picks = [(k_all, v_all, pl.ds(start, KEY_BLOCK), mask)]
        fold_keys([job(place, picks) for place in places], m_ref, acc_ref)

    full = used // KEY_BLOCK
    pl.loop(0, full)(lambda block: visit(block, False))

    @pl.when(used % KEY_BLOCK > 0)
    def _():
        visit(full, True)

    if causal:
        each = piece // sides
        row = lax.broadcasted_iota(jnp.int32, (ROW_BLOCK, ROW_BLOCK), 0)
        key = lax.broadcasted_iota(jnp.int32, (ROW_BLOCK, ROW_BLOCK), 1)

        def natural(at, of_chunk):
            within = at % piece
            inside = (within // each) * (each * chunks) + of_chunk * each + within % each
            return (at // piece) * (piece * chunks) + inside

        row_at = natural(row, chunk)
        masks = [natural(key, key_chunk) <= row_at for key_chunk in range(chunks)]
        jobs = []
        for place in places:
            picks = []
            for key_chunk in range(chunks):
                pair = new_refs[2 * key_chunk : 2 * key_chunk + 2]
                if place[1]:
                    picks.append((*pair, slice(0, place[1] * ROW_BLOCK), None))
                picks.append((*pair, rows_of(place[1]), masks[key_chunk]))
            jobs.append(job(place, picks))
        fold_keys(jobs, m_ref, acc_ref)

    for head, block in places:
        rows = rows_of(block)
        total = acc_ref[head, block, :, HEAD_DIM:]
        seen = total > 0.0
        safe = jnp.where(seen, total, 1.0)
        out = (acc_ref[head, block, :, :HEAD_DIM] / safe).astype(jnp.bfloat16)
        column = step * per_step + head
        o_ref[rows, pl.ds(pl.multiple_of(column * HEAD_DIM, HEAD_DIM), HEAD_DIM)] = out
        lse = jnp.where(seen, m_ref[head, block] * scale + jnp.log2(safe), LOWEST)
        lane = lax.broadcasted_iota(jnp.int32, (ROW_BLOCK, STATS), 1)
        before = jnp.where(column == 0, 0.0, lse_ref[rows, :])
        lse_ref[rows, :] = jnp.where(lane == column, lse, before)

    @pl.when(step == pl.num_programs(0) - 1)
    def _():
        for block in blocks:
            rows = rows_of(block)
            left = lse_ref[rows, :]
            packed = jnp.zeros_like(left)
            for turn in range(3):
                part = left.astype(jnp.bfloat16).astype(jnp.float32)
                left = left - part
                packed = packed + (pltpu.roll(part, turn * STATS // 4, 1) if turn else part)
            o_ref[rows, o_ref.shape[1] - STATS :] = packed.astype(jnp.bfloat16)


def attend(count, groups, chunk, chunks, sides, queries, q_at, cache, new=()):
    width = queries.shape[1]
    heads = width // HEAD_DIM
    per_step = 2
    rows = cache.shape[-2]
    causal = len(new) > 0
    rows_in = queries.shape[0] if causal else queries.shape[0] // chunks
    lead = cache.ndim - 3
    shape = (1,) * (lead + 1) + (rows, per_step * HEAD_DIM)
    every = pl.BlockSpec((rows_in, per_step * HEAD_DIM), lambda h, n: (0, h))

    def half(which):
        return pl.BlockSpec(shape, lambda h, n: (0,) * lead + (which, 0, h))

    keys_seen = rows + (rows_in if causal else 0)
    out = pl.pallas_call(
        functools.partial(attend_kernel, causal, chunk, chunks, rows_in // groups, sides),
        grid_spec=pltpu.PrefetchScalarGridSpec(
            num_scalar_prefetch=1,
            grid=(heads // per_step,),
            in_specs=[
                pl.BlockSpec((rows_in, per_step * HEAD_DIM), lambda h, n: (q_at, h)),
                half(0),
                half(1),
            ]
            + [every] * len(new),
            out_specs=pl.BlockSpec((rows_in, width + STATS), lambda h, n: (0, 0)),
            scratch_shapes=[
                pltpu.VMEM((rows_in, STATS), jnp.float32),
                pltpu.VMEM((per_step, rows_in // ROW_BLOCK, ROW_BLOCK, HEAD_DIM), jnp.float32),
                pltpu.VMEM((per_step, rows_in // ROW_BLOCK, ROW_BLOCK, 2 * HEAD_DIM), jnp.float32),
            ],
        ),
        out_shape=jax.ShapeDtypeStruct((rows_in, width + STATS), jnp.bfloat16),
        compiler_params=params(ATTEND_LIMIT),
        cost_estimate=pl.CostEstimate(
            flops=16 * rows_in * keys_seen * width,
            bytes_accessed=4 * rows * width + 4 * rows_in * width,
            transcendentals=rows_in * keys_seen * heads,
        ),
        name="attend_own" if causal else "attend_guest",
    )(count, queries, cache, cache, *new)
    return out.reshape(groups, rows_in // groups, width + STATS)


def merge_kernel(groups, heads, inverse_ref, tp_ref, own_ref, guest_ref, w_ref, *refs):
    *out_refs, att_ref = refs
    piece = own_ref.shape[1]
    width = heads * HEAD_DIM
    step = pl.program_id(0)

    def stats(part_ref, at):
        packed = part_ref[at, :, width:].astype(jnp.float32)
        return (
            packed
            + pltpu.roll(packed, STATS - STATS // 4, 1)
            + pltpu.roll(packed, STATS - STATS // 2, 1)
        )

    @pl.when(step == 0)
    def _():
        for request in range(groups):
            source = inverse_ref[request]
            helper = lax.rem(source + groups // 2, groups)
            own_lse = stats(own_ref, source)
            guest_lse = stats(guest_ref, helper)
            top = jnp.maximum(own_lse, guest_lse)
            own_share = jnp.exp2(own_lse - top)
            guest_share = jnp.exp2(guest_lse - top)
            total = own_share + guest_share
            own_share = own_share / total
            guest_share = guest_share / total
            rows = pl.ds(request * piece, piece)
            for head in range(heads):
                cut = slice(head * HEAD_DIM, (head + 1) * HEAD_DIM)
                merged = own_ref[source, :, cut].astype(jnp.float32) * own_share[
                    :, head : head + 1
                ] + guest_ref[helper, :, cut].astype(jnp.float32) * guest_share[:, head : head + 1]
                att_ref[rows, cut] = merged.astype(jnp.bfloat16)

    product = jnp.dot(att_ref[...], w_ref[...], preferred_element_type=jnp.float32).astype(
        jnp.bfloat16
    )
    each = pl.num_programs(0) // len(out_refs)
    for at, out_ref in enumerate(out_refs):
        pl.when(step // each == at)(functools.partial(out_ref.__setitem__, ..., product))


def merge(inverse, tp_index, splits, own, guest, w_out):
    groups, piece, padded = guest.shape
    width = w_out.shape[0]
    heads = width // HEAD_DIM
    columns = w_out.shape[1]
    block = 512
    rows = groups * piece
    steps = columns // block
    each = steps // splits

    def w_at(n, i, t):
        return (0, (n + each * (1 - t[0])) % steps if splits == 2 else n)

    def out_at(which):
        return lambda n, i, t: (0, jnp.clip(n - which * each, 0, each - 1))

    part = pl.BlockSpec(guest.shape, lambda n, i, t: (0, 0, 0))
    return pl.pallas_call(
        functools.partial(merge_kernel, groups, heads),
        grid_spec=pltpu.PrefetchScalarGridSpec(
            num_scalar_prefetch=2,
            grid=(steps,),
            in_specs=[part, part, pl.BlockSpec((width, block), w_at)],
            out_specs=[pl.BlockSpec((rows, block), out_at(which)) for which in range(splits)],
            scratch_shapes=[pltpu.VMEM((rows, width), jnp.bfloat16)],
        ),
        out_shape=[jax.ShapeDtypeStruct((rows, columns // splits), jnp.bfloat16)] * splits,
        compiler_params=params(),
        cost_estimate=pl.CostEstimate(
            flops=4 * rows * width * columns,
            bytes_accessed=2 * (2 * rows * padded + width * columns + rows * columns),
            transcendentals=0,
        ),
        name="merge",
    )(inverse, tp_index, own, guest, w_out)


def exchange(value):
    return lax.all_to_all(value, "grp", split_axis=0, concat_axis=0, tiled=True)


def shards(
    tokens,
    w_query,
    w_key,
    w_value,
    w_out,
    own_cache,
    guest_cache,
    rec_hidden,
    deal_order,
    own_len,
    guest_len,
    rec_index,
):
    groups = lax.axis_size("grp")
    tp_size = lax.axis_size("tp")
    group_id = lax.axis_index("grp")
    tp_id = lax.axis_index("tp")
    partner_id = (group_id + groups // 2) % groups
    width = w_query.shape[1]
    heads = width // HEAD_DIM
    shard_rows = tokens.shape[1]
    span = shard_rows * groups
    piece = shard_rows // tp_size

    chunks = 2
    chunk_rows = shard_rows // chunks
    paired = tp_size == 2 and piece % 32 == 0
    sides = 2 if paired else 1
    each = chunk_rows // sides
    tp_index = tp_id.astype(jnp.int32)[None]
    tied = lax.optimization_barrier
    neighbour = [(0, 1), (1, 0)]

    if paired:
        *own_rows, guest_rows = deal(tokens, deal_order, tp_index, piece)
    else:
        mine = lax.dynamic_slice_in_dim(tokens, tp_id * piece, piece, 1)
        normed = layer_norm(mine).astype(jnp.bfloat16)
        own_rows = [jnp.take(normed, deal_order, axis=0)]
        guest_rows = jnp.roll(own_rows[0], groups // 2, axis=0)

    def in_chunks(rows):
        rows = rows.reshape(groups, sides, chunks, each, -1)
        return jnp.transpose(rows, (2, 0, 1, 3, 4)).reshape(chunks, span // chunks, -1)

    def gathered(arrived):
        if paired:
            return [arrived, lax.ppermute(arrived, "tp", neighbour)]
        arrived = lax.all_gather(arrived, "tp", axis=0)
        return in_chunks(jnp.transpose(arrived, (1, 0, 2, 3)))

    row_order = in_chunks(jnp.arange(span, dtype=jnp.int32)).reshape(span)

    def place(owner, helper):
        return own_len[owner] + guest_len[helper] + row_order

    def projected(x, tables, weights, turned):
        return project(x, each, tp_index, tables, weights, turned)

    arrived = exchange(own_rows[0])
    own_tables = rope_tables(place(group_id, partner_id))
    guest_tables = rope_tables(place(partner_id, group_id))
    rec_tables = rope_tables(rec_index[0])
    rec_rows = layer_norm(rec_hidden[0]).astype(jnp.bfloat16)
    rec_parts = projected((rec_rows,), rec_tables, (w_key, w_value), (True, False))
    arrived, own_tables, guest_tables, rec_parts, own_rows = tied(
        (arrived, own_tables, guest_tables, rec_parts, own_rows)
    )

    own_x = [gathered(arrived)]
    cache = replace_rows(own_cache, jnp.stack(rec_parts), rec_index)
    if paired:
        arrived = exchange(own_rows[1])
        arrived, cache, own_x, guest_rows = tied((arrived, cache, own_x, guest_rows))
        own_x.append(gathered(arrived))
    else:
        own_x = [[part] for part in own_x[0]]

    guest_arrived = exchange(guest_rows)
    queries, new = [], []
    for chunk in range(chunks):
        rows = slice(chunk * span // chunks, (chunk + 1) * span // chunks)
        tables = [table[rows] for table in own_tables]
        made = projected(own_x[chunk], tables, (w_query, w_key, w_value), (True, True, False))
        queries.append(made[0])
        new += made[1:]
    guest_arrived, queries = tied((guest_arrived, queries))
    guest_x = gathered(guest_arrived)
    if not paired:
        guest_x = [guest_x.reshape(span, -1)]

    def own_attend(chunk, seen):
        count = own_len[group_id][None]
        return attend(count, groups, chunk, chunks, sides, seen, 0, cache, new)

    def guest_attend(chunk, seen):
        count = guest_len[group_id][None]
        return attend(count, groups, chunk, chunks, sides, seen, chunk, guest_cache)

    own_out = [own_attend(0, queries[0])]
    own_out[0], queries[1] = tied((own_out[0], queries[1]))
    own_out.append(own_attend(1, queries[1]))
    own_part = [exchange(own_out[0])]
    guest_x, own_out[1] = tied((guest_x, own_out[1]))
    (guest_queries,) = projected(guest_x, guest_tables, (w_query,), (True,))
    own_part[0], guest_queries, own_out[1] = tied((own_part[0], guest_queries, own_out[1]))
    own_part.append(exchange(own_out[1]))
    guest_out = [guest_attend(0, guest_queries)]
    own_part[1], guest_out[0], guest_queries = tied((own_part[1], guest_out[0], guest_queries))
    guest_out.append(guest_attend(1, guest_queries))

    inverse = jnp.sum(
        jnp.where(
            deal_order[None, :] == jnp.arange(groups, dtype=deal_order.dtype)[:, None],
            jnp.arange(groups, dtype=jnp.int32)[None, :],
            0,
        ),
        axis=1,
    )
    guest_part = [exchange(guest_out[0])]
    guest_part[0], guest_out[1] = tied((guest_part[0], guest_out[1]))
    guest_part.append(exchange(guest_out[1]))
    mixed = []
    for chunk in range(chunks):
        partial = merge(
            inverse, tp_index, 2 if paired else 1, own_part[chunk], guest_part[chunk], w_out
        )
        if chunk == 0:
            partial, guest_part[1] = tied((partial, guest_part[1]))
        if paired:
            theirs, mine = partial
            arrived = lax.ppermute(theirs, "tp", neighbour).astype(jnp.float32)
            summed = (mine.astype(jnp.float32) + arrived).astype(jnp.bfloat16)
        else:
            summed = lax.psum_scatter(partial[0], "tp", scatter_dimension=1, tiled=True)
        mixed.append(summed.reshape(groups, sides, 1, each, -1))
    return jnp.concatenate(mixed, axis=2).reshape(groups, shard_rows, -1)


def solution(mesh):
    return jax.shard_map(
        shards,
        mesh=mesh,
        in_specs=(
            P(None, "grp", None),
            P(None, "tp"),
            P(None, "tp"),
            P(None, "tp"),
            P("tp", None),
            P("grp", None, None, "tp"),
            P("grp", None, None, "tp"),
            P("grp", None, None),
            P(),
            P(),
            P(),
            P("grp", None),
        ),
        out_specs=P(None, "grp", "tp"),
        check_vma=False,
    )
```

```python
import functools
import math

import jax
import jax.numpy as jnp
from jax import lax
from jax.experimental import pallas as pl
from jax.experimental.pallas import tpu as pltpu
from jax.sharding import PartitionSpec as P

HEAD_DIM = 128
KEY_BLOCK = 1024
ROW_BLOCK = 256
STATS = 128
VMEM_LIMIT = 60 * 1024 * 1024

rope_base = 10000.0
norm_eps = 1e-05
LOG2E = math.log2(math.e)
LOWEST = -1e30


def params():
    return pltpu.CompilerParams(vmem_limit_bytes=VMEM_LIMIT)


def layer_norm(token_rows):
    widened = token_rows.astype(jnp.float32)
    centred = widened - jnp.mean(widened, axis=-1, keepdims=True)
    variance = jnp.mean(centred * centred, axis=-1, keepdims=True)
    return centred * lax.rsqrt(variance + norm_eps)


def rope_tables(positions):
    half_dim = HEAD_DIM // 2
    frequency = jnp.exp(-jnp.log(rope_base) * jnp.arange(half_dim, dtype=jnp.float32) / half_dim)
    angles = positions.astype(jnp.float32)[:, None] * frequency[None, :]
    cosine = jnp.cos(angles)
    sine = jnp.sin(angles)
    return (
        jnp.concatenate([cosine, cosine], axis=-1),
        jnp.concatenate([-sine, sine], axis=-1),
    )


def deal_kernel(order_ref, tp_ref, x_ref, *out_refs):
    each, cut, _ = out_refs[0].shape
    start = pl.program_id(0) * each
    for at in range(each):
        normed = layer_norm(x_ref[order_ref[start + at]]).astype(jnp.bfloat16)
        for which, out_ref in enumerate(out_refs):
            first = which % 2 * cut
            out_ref[at] = normed[first : first + cut]


def deal(tokens, deal_order, tp_index, piece):
    groups, _, width = tokens.shape
    each = 4
    steps = groups // each
    cut = piece // 2
    own = pl.BlockSpec((each, cut, width), lambda d, order, t: (d, 0, 0))
    guest = pl.BlockSpec((each, cut, width), lambda d, order, t: ((d + steps // 2) % steps, 0, 0))
    return pl.pallas_call(
        deal_kernel,
        grid_spec=pltpu.PrefetchScalarGridSpec(
            num_scalar_prefetch=2,
            grid=(steps,),
            in_specs=[pl.BlockSpec((groups, piece, width), lambda d, order, t: (0, t[0], 0))],
            out_specs=[own, own, guest, guest],
        ),
        out_shape=[jax.ShapeDtypeStruct((groups, cut, width), jnp.bfloat16)] * 4,
        compiler_params=params(),
        name="deal",
    )(deal_order, tp_index, tokens)


def project_kernel(turned, heads, sources, cut, tp_ref, *refs):
    if sources > 1:
        mine_ref, other_ref, cos_ref, sin_ref, *refs, x_ref = refs
        shards_in, rows_each, _ = mine_ref.shape

        @pl.when(pl.program_id(0) == 0)
        def _():
            t = tp_ref[0]
            for piece in range(rows_each // cut):
                rows = slice(piece * cut, (piece + 1) * cut)
                for shard in range(shards_in):
                    at = (piece * shards_in + shard) * 2
                    for part_ref, side in ((mine_ref, t), (other_ref, 1 - t)):
                        start = pl.multiple_of((at + side) * cut, cut)
                        x_ref[pl.ds(start, cut), :] = part_ref[shard, rows, :]
    else:
        x_ref, cos_ref, sin_ref, *refs = refs
    count = len(turned)
    step = min(512, x_ref.shape[0])
    for first in range(0, x_ref.shape[0], step):
        rows = slice(first, first + step)
        for w_ref, out_ref, turn in zip(refs[:count], refs[count:], turned):
            product = jnp.dot(x_ref[rows, :], w_ref[...], preferred_element_type=jnp.float32)
            if not turn:
                out_ref[rows, :] = product.astype(jnp.bfloat16)
                continue
            for head in range(heads):
                cut = slice(head * HEAD_DIM, (head + 1) * HEAD_DIM)
                part = product[:, cut]
                swapped = pltpu.roll(part, HEAD_DIM // 2, 1)
                out_ref[rows, cut] = (
                    part * cos_ref[rows, :] + swapped * sin_ref[rows, :]
                ).astype(jnp.bfloat16)


def project(x, cut, tp_index, tables, weights, turned):
    depth = x[0].shape[-1]
    rows = sum(math.prod(part.shape[:-1]) for part in x)
    width = weights[0].shape[1]
    block = min(256, width)
    table = pl.BlockSpec((rows, HEAD_DIM), lambda n, t: (0, 0))
    count = len(weights)
    return pl.pallas_call(
        functools.partial(project_kernel, turned, block // HEAD_DIM, len(x), cut),
        grid_spec=pltpu.PrefetchScalarGridSpec(
            num_scalar_prefetch=1,
            grid=(width // block,),
            in_specs=[pl.BlockSpec(part.shape, lambda n, t, r=part.ndim: (0,) * r) for part in x]
            + [table, table]
            + [pl.BlockSpec((depth, block), lambda n, t: (0, n))] * count,
            out_specs=[pl.BlockSpec((rows, block), lambda n, t: (0, n))] * count,
            scratch_shapes=[pltpu.VMEM((rows, depth), jnp.bfloat16)] if len(x) > 1 else [],
        ),
        out_shape=[jax.ShapeDtypeStruct((rows, width), jnp.bfloat16)] * count,
        compiler_params=params(),
        cost_estimate=pl.CostEstimate(
            flops=2 * rows * depth * width * count,
            bytes_accessed=2 * (rows * depth + count * width * (rows + depth)),
            transcendentals=0,
        ),
        name="project",
    )(tp_index, *x, *tables, *weights)


def replace_kernel(block, index_ref, cache_ref, fresh_ref, out_ref):
    first = pl.program_id(1) * block
    count = index_ref.shape[1]
    row = first + lax.broadcasted_iota(jnp.int32, (block, count), 0)
    hits = jnp.where(row == index_ref[...], 1.0, 0.0)
    picked = jnp.dot(
        hits.astype(jnp.bfloat16), fresh_ref[0], preferred_element_type=jnp.float32
    )
    is_hit = jnp.sum(hits, axis=1, keepdims=True) > 0.5
    out_ref[0] = jnp.where(is_hit, picked, cache_ref[0, 0].astype(jnp.float32)).astype(jnp.bfloat16)


def replace_rows(cache, fresh, rec_index):
    _, _, rows, width = cache.shape
    count = rec_index.shape[1]
    block = 512
    return pl.pallas_call(
        functools.partial(replace_kernel, block),
        grid=(2, rows // block),
        in_specs=[
            pl.BlockSpec((1, count), lambda c, r: (0, 0)),
            pl.BlockSpec((1, 1, block, width), lambda c, r: (0, c, r, 0)),
            pl.BlockSpec((1, count, width), lambda c, r: (c, 0, 0)),
        ],
        out_specs=pl.BlockSpec((1, block, width), lambda c, r: (c, r, 0)),
        out_shape=jax.ShapeDtypeStruct((2, rows, width), jnp.bfloat16),
        compiler_params=params(),
        cost_estimate=pl.CostEstimate(
            flops=4 * rows * count * width, bytes_accessed=10 * rows * width, transcendentals=0
        ),
        name="replace_rows",
    )(rec_index, cache, fresh)


def fold_keys(jobs, m_ref, acc_ref):
    scale = HEAD_DIM**-0.5 * LOG2E

    def scores_of(job):
        _, queries, keys, _ = job
        parts = []
        for key_block, mask in keys():
            scores = lax.dot_general(
                queries(), key_block, (((1,), (1,)), ((), ())), preferred_element_type=jnp.float32
            )
            parts.append(scores if mask is None else jnp.where(mask, scores, LOWEST))
        return parts[0] if len(parts) == 1 else jnp.concatenate(parts, axis=1)

    upcoming = scores_of(jobs[0])
    for at, (place, _, _, values) in enumerate(jobs):
        scores = upcoming
        if at + 1 < len(jobs):
            upcoming = scores_of(jobs[at + 1])
        old_max = m_ref[place]
        new_max = jnp.maximum(old_max, jnp.max(scores, axis=1, keepdims=True))
        factor = jnp.exp2((old_max - new_max) * scale)
        shift = new_max * scale
        tiles = scores.shape[1] // HEAD_DIM
        weights = jnp.exp2(scores * scale - jnp.concatenate([shift] * tiles, axis=1))
        seen = values()
        widened = jnp.concatenate([seen, jnp.ones(seen.shape, jnp.bfloat16)], axis=1)
        product = jnp.dot(
            weights.astype(jnp.bfloat16), widened, preferred_element_type=jnp.float32
        )
        acc_ref[place] = acc_ref[place] * jnp.concatenate([factor, factor], axis=1) + product
        m_ref[place] = new_max


def attend_kernel(causal, chunk, chunks, piece, sides, count_ref, q_ref, k_ref, v_ref, *refs):
    if causal:
        new_refs, refs = refs[: 2 * chunks], refs[2 * chunks :]
    o_ref, lse_ref, m_ref, acc_ref = refs
    scale = HEAD_DIM**-0.5 * LOG2E
    rows_in = q_ref.shape[0]
    per_step = q_ref.shape[1] // HEAD_DIM
    step = pl.program_id(0)
    used = count_ref[0]
    everything = slice(0, rows_in)
    blocks = [slice(at, at + ROW_BLOCK) for at in range(0, rows_in, ROW_BLOCK)]
    places = [(head, block) for head in range(per_step) for block in blocks]
    m_ref[...] = jnp.full(m_ref.shape, LOWEST, jnp.float32)
    acc_ref[...] = jnp.zeros(acc_ref.shape, jnp.float32)
    k_all = k_ref.at[(0,) * (len(k_ref.shape) - 2)]
    v_all = v_ref.at[(0,) * (len(v_ref.shape) - 2)]

    def head_cut(head):
        return slice(head * HEAD_DIM, (head + 1) * HEAD_DIM)

    def job(place, picks):
        head, block = place
        cut = head_cut(head)

        def values():
            found = [values_ref[at, cut] for _, values_ref, at, _ in picks]
            return found[0] if len(found) == 1 else jnp.concatenate(found, axis=0)

        return (
            place,
            lambda: q_ref[block, cut],
            lambda: [(keys_ref[at, cut], mask) for keys_ref, _, at, mask in picks],
            values,
        )

    def visit(block, masked):
        start = pl.multiple_of(block * KEY_BLOCK, KEY_BLOCK)
        mask = None
        if masked:
            mask = lax.broadcasted_iota(jnp.int32, (1, KEY_BLOCK), 1) < used - start
        picks = [(k_all, v_all, pl.ds(start, KEY_BLOCK), mask)]
        fold_keys([job((head, everything), picks) for head in range(per_step)], m_ref, acc_ref)

    full = used // KEY_BLOCK
    pl.loop(0, full)(lambda block: visit(block, False))

    @pl.when(used % KEY_BLOCK > 0)
    def _():
        visit(full, True)

    if causal:
        each = piece // sides
        row = lax.broadcasted_iota(jnp.int32, (ROW_BLOCK, ROW_BLOCK), 0)
        key = lax.broadcasted_iota(jnp.int32, (ROW_BLOCK, ROW_BLOCK), 1)

        def natural(at, of_chunk):
            within = at % piece
            inside = (within // each) * (each * chunks) + of_chunk * each + within % each
            return (at // piece) * (piece * chunks) + inside

        row_at = natural(row, chunk)
        masks = [natural(key, key_chunk) <= row_at for key_chunk in range(chunks)]
        jobs = []
        for place in places:
            picks = []
            for key_chunk in range(chunks):
                pair = new_refs[2 * key_chunk : 2 * key_chunk + 2]
                if place[1].start:
                    picks.append((*pair, slice(0, place[1].start), None))
                picks.append((*pair, place[1], masks[key_chunk]))
            jobs.append(job(place, picks))
        fold_keys(jobs, m_ref, acc_ref)

    for head, block in places:
        rows = block
        total = acc_ref[head, block, HEAD_DIM:]
        seen = total > 0.0
        safe = jnp.where(seen, total, 1.0)
        out = (acc_ref[head, block, :HEAD_DIM] / safe).astype(jnp.bfloat16)
        column = step * per_step + head
        o_ref[rows, pl.ds(pl.multiple_of(column * HEAD_DIM, HEAD_DIM), HEAD_DIM)] = out
        lse = jnp.where(seen, m_ref[head, block] * scale + jnp.log2(safe), LOWEST)
        lane = lax.broadcasted_iota(jnp.int32, (ROW_BLOCK, STATS), 1)
        before = jnp.where(column == 0, 0.0, lse_ref[rows, :])
        lse_ref[rows, :] = jnp.where(lane == column, lse, before)

    @pl.when(step == pl.num_programs(0) - 1)
    def _():
        for rows in blocks:
            left = lse_ref[rows, :]
            packed = jnp.zeros_like(left)
            for turn in range(3):
                part = left.astype(jnp.bfloat16).astype(jnp.float32)
                left = left - part
                packed = packed + (pltpu.roll(part, turn * STATS // 4, 1) if turn else part)
            o_ref[rows, o_ref.shape[1] - STATS :] = packed.astype(jnp.bfloat16)


def attend(count, groups, chunk, chunks, sides, queries, cache, new=()):
    width = queries.shape[1]
    heads = width // HEAD_DIM
    per_step = 2
    rows = cache.shape[-2]
    causal = len(new) > 0
    rows_in = queries.shape[0]
    lead = cache.ndim - 3
    shape = (1,) * (lead + 1) + (rows, per_step * HEAD_DIM)
    every = pl.BlockSpec((rows_in, per_step * HEAD_DIM), lambda h, n: (0, h))

    def half(which):
        return pl.BlockSpec(shape, lambda h, n: (0,) * lead + (which, 0, h))

    keys_seen = rows + (rows_in if causal else 0)
    out = pl.pallas_call(
        functools.partial(attend_kernel, causal, chunk, chunks, rows_in // groups, sides),
        grid_spec=pltpu.PrefetchScalarGridSpec(
            num_scalar_prefetch=1,
            grid=(heads // per_step,),
            in_specs=[
                every,
                half(0),
                half(1),
            ]
            + [every] * len(new),
            out_specs=pl.BlockSpec((rows_in, width + STATS), lambda h, n: (0, 0)),
            scratch_shapes=[
                pltpu.VMEM((rows_in, STATS), jnp.float32),
                pltpu.VMEM((per_step, rows_in, HEAD_DIM), jnp.float32),
                pltpu.VMEM((per_step, rows_in, 2 * HEAD_DIM), jnp.float32),
            ],
        ),
        out_shape=jax.ShapeDtypeStruct((rows_in, width + STATS), jnp.bfloat16),
        compiler_params=params(),
        cost_estimate=pl.CostEstimate(
            flops=16 * rows_in * keys_seen * width,
            bytes_accessed=4 * rows * width + 4 * rows_in * width,
            transcendentals=rows_in * keys_seen * heads,
        ),
        name="attend_own" if causal else "attend_guest",
    )(count, queries, cache, cache, *new)
    return out.reshape(groups, rows_in // groups, width + STATS)


def merge_kernel(groups, heads, inverse_ref, tp_ref, own_ref, guest_ref, w_ref, *refs):
    *out_refs, att_ref = refs
    piece = own_ref.shape[1]
    width = heads * HEAD_DIM
    step = pl.program_id(0)

    def stats(part_ref, at):
        packed = part_ref[at, :, width:].astype(jnp.float32)
        return (
            packed
            + pltpu.roll(packed, STATS - STATS // 4, 1)
            + pltpu.roll(packed, STATS - STATS // 2, 1)
        )

    @pl.when(step == 0)
    def _():
        for request in range(groups):
            source = inverse_ref[request]
            helper = lax.rem(source + groups // 2, groups)
            own_lse = stats(own_ref, source)
            guest_lse = stats(guest_ref, helper)
            top = jnp.maximum(own_lse, guest_lse)
            own_share = jnp.exp2(own_lse - top)
            guest_share = jnp.exp2(guest_lse - top)
            total = own_share + guest_share
            own_share = own_share / total
            guest_share = guest_share / total
            rows = pl.ds(request * piece, piece)
            for head in range(heads):
                cut = slice(head * HEAD_DIM, (head + 1) * HEAD_DIM)
                merged = own_ref[source, :, cut].astype(jnp.float32) * own_share[
                    :, head : head + 1
                ] + guest_ref[helper, :, cut].astype(jnp.float32) * guest_share[:, head : head + 1]
                att_ref[rows, cut] = merged.astype(jnp.bfloat16)

    product = jnp.dot(att_ref[...], w_ref[...], preferred_element_type=jnp.float32).astype(
        jnp.bfloat16
    )
    each = pl.num_programs(0) // len(out_refs)
    for at, out_ref in enumerate(out_refs):
        pl.when(step // each == at)(functools.partial(out_ref.__setitem__, ..., product))


def merge(inverse, tp_index, splits, own, guest, w_out):
    groups, piece, padded = guest.shape
    width = w_out.shape[0]
    heads = width // HEAD_DIM
    columns = w_out.shape[1]
    block = 512
    rows = groups * piece
    steps = columns // block
    each = steps // splits

    def w_at(n, i, t):
        return (0, (n + each * (1 - t[0])) % steps if splits == 2 else n)

    def out_at(which):
        return lambda n, i, t: (0, jnp.clip(n - which * each, 0, each - 1))

    part = pl.BlockSpec(guest.shape, lambda n, i, t: (0, 0, 0))
    return pl.pallas_call(
        functools.partial(merge_kernel, groups, heads),
        grid_spec=pltpu.PrefetchScalarGridSpec(
            num_scalar_prefetch=2,
            grid=(steps,),
            in_specs=[part, part, pl.BlockSpec((width, block), w_at)],
            out_specs=[pl.BlockSpec((rows, block), out_at(which)) for which in range(splits)],
            scratch_shapes=[pltpu.VMEM((rows, width), jnp.bfloat16)],
        ),
        out_shape=[jax.ShapeDtypeStruct((rows, columns // splits), jnp.bfloat16)] * splits,
        compiler_params=params(),
        cost_estimate=pl.CostEstimate(
            flops=4 * rows * width * columns,
            bytes_accessed=2 * (2 * rows * padded + width * columns + rows * columns),
            transcendentals=0,
        ),
        name="merge",
    )(inverse, tp_index, own, guest, w_out)


def exchange(value):
    return lax.all_to_all(value, "grp", split_axis=0, concat_axis=0, tiled=True)


def shards(
    tokens,
    w_query,
    w_key,
    w_value,
    w_out,
    own_cache,
    guest_cache,
    rec_hidden,
    deal_order,
    own_len,
    guest_len,
    rec_index,
):
    groups = lax.axis_size("grp")
    tp_size = lax.axis_size("tp")
    group_id = lax.axis_index("grp")
    tp_id = lax.axis_index("tp")
    partner_id = (group_id + groups // 2) % groups
    width = w_query.shape[1]
    heads = width // HEAD_DIM
    shard_rows = tokens.shape[1]
    span = shard_rows * groups
    piece = shard_rows // tp_size

    chunks = 2
    chunk_rows = shard_rows // chunks
    paired = tp_size == 2 and piece % 32 == 0
    sides = 2 if paired else 1
    each = chunk_rows // sides
    tp_index = tp_id.astype(jnp.int32)[None]
    tied = lax.optimization_barrier
    neighbour = [(0, 1), (1, 0)]

    if paired:
        dealt = deal(tokens, deal_order, tp_index, piece)
        own_rows, guest_rows = dealt[:2], dealt[2:]
    else:
        mine = lax.dynamic_slice_in_dim(tokens, tp_id * piece, piece, 1)
        normed = layer_norm(mine).astype(jnp.bfloat16)
        own_rows = jnp.take(normed, deal_order, axis=0)
        guest_rows = jnp.roll(own_rows, groups // 2, axis=0)

    def in_chunks(rows):
        rows = rows.reshape(groups, sides, chunks, each, -1)
        return jnp.transpose(rows, (2, 0, 1, 3, 4)).reshape(chunks, span // chunks, -1)

    def with_other(arrived):
        return [arrived, lax.ppermute(arrived, "tp", neighbour)]

    def gathered(rows):
        arrived = lax.all_gather(exchange(rows), "tp", axis=0)
        parts = in_chunks(jnp.transpose(arrived, (1, 0, 2, 3)))
        return [[part] for part in parts]

    row_order = in_chunks(jnp.arange(span, dtype=jnp.int32)).reshape(span)

    def place(owner, helper):
        return own_len[owner] + guest_len[helper] + row_order

    def projected(x, tables, chunk, weights, turned):
        if chunk is not None:
            rows = slice(chunk * span // chunks, (chunk + 1) * span // chunks)
            tables = [table[rows] for table in tables]
        return project(x, each, tp_index, tables, weights, turned)

    def own_project(chunk):
        return projected(
            own_x[chunk], own_tables, chunk, (w_query, w_key, w_value), (True, True, False)
        )

    def own_attend(chunk, queries):
        count = own_len[group_id][None]
        return attend(count, groups, chunk, chunks, sides, queries, cache, new)

    def guest_attend(chunk):
        (queries,) = projected(guest_x[chunk], guest_tables, chunk, (w_query,), (True,))
        count = guest_len[group_id][None]
        return attend(count, groups, chunk, chunks, sides, queries, guest_cache)

    own_tables = rope_tables(place(group_id, partner_id))
    guest_tables = rope_tables(place(partner_id, group_id))
    rec_tables = rope_tables(rec_index[0])
    rec_rows = layer_norm(rec_hidden[0]).astype(jnp.bfloat16)
    rec_parts = projected((rec_rows,), rec_tables, None, (w_key, w_value), (True, False))

    if paired:
        arrived = exchange(guest_rows[0])
        arrived, own_tables, guest_tables, rec_parts, own_rows = tied(
            (arrived, own_tables, guest_tables, rec_parts, own_rows)
        )
        guest_x = [with_other(arrived)]
        cache = replace_rows(own_cache, jnp.stack(rec_parts), rec_index)
        arrived = exchange(own_rows[0])
        arrived, cache, guest_x, own_rows = tied((arrived, cache, guest_x, own_rows))
        own_x = [with_other(arrived)]
        guest_out = [guest_attend(0)]
        arrived = exchange(own_rows[1])
        arrived, own_x, guest_out, guest_rows = tied((arrived, own_x, guest_out, guest_rows))
        own_x.append(with_other(arrived))
        arrived = exchange(guest_rows[1])
        made = [own_project(chunk) for chunk in range(chunks)]
        arrived, guest_out, made = tied((arrived, guest_out, made))
        guest_x.append(with_other(arrived))
    else:
        cache = replace_rows(own_cache, jnp.stack(rec_parts), rec_index)
        own_x = gathered(own_rows)
        guest_x = gathered(guest_rows)
        guest_out = [guest_attend(0)]
        made = [own_project(chunk) for chunk in range(chunks)]
    new = [part for parts in made for part in parts[1:]]
    inverse = jnp.sum(
        jnp.where(
            deal_order[None, :] == jnp.arange(groups, dtype=deal_order.dtype)[:, None],
            jnp.arange(groups, dtype=jnp.int32)[None, :],
            0,
        ),
        axis=1,
    )

    guest_part = [exchange(guest_out[0])]
    own_out = [own_attend(0, made[0][0])]
    guest_part, own_out, query = tied((guest_part, own_out, made[1][0]))
    own_part = [exchange(own_out[0])]
    own_out.append(own_attend(1, query))
    own_part, own_out, guest_x = tied((own_part, own_out, guest_x))
    own_part.append(exchange(own_out[1]))
    guest_out.append(guest_attend(1))

    def merged(chunk):
        splits = 2 if paired else 1
        return merge(inverse, tp_index, splits, own_part[chunk], guest_part[chunk], w_out)

    def summed(partial):
        if paired:
            theirs, mine = partial
            arrived = lax.ppermute(theirs, "tp", neighbour).astype(jnp.float32)
            total = (mine.astype(jnp.float32) + arrived).astype(jnp.bfloat16)
        else:
            total = lax.psum_scatter(partial[0], "tp", scatter_dimension=1, tiled=True)
        return total.reshape(groups, sides, 1, each, -1)

    partial = merged(0)
    own_part[1], guest_out[1], partial = tied((own_part[1], guest_out[1], partial))
    mixed = [summed(partial)]
    guest_part.append(exchange(guest_out[1]))
    guest_part[1], mixed = tied((guest_part[1], mixed))
    mixed.append(summed(merged(1)))
    return jnp.concatenate(mixed, axis=2).reshape(groups, shard_rows, -1)


def solution(mesh):
    return jax.shard_map(
        shards,
        mesh=mesh,
        in_specs=(
            P(None, "grp", None),
            P(None, "tp"),
            P(None, "tp"),
            P(None, "tp"),
            P("tp", None),
            P("grp", None, None, "tp"),
            P("grp", None, None, "tp"),
            P("grp", None, None),
            P(),
            P(),
            P(),
            P("grp", None),
        ),
        out_specs=P(None, "grp", "tp"),
        check_vma=False,
    )
```

```python
import functools
import math

import jax
import jax.numpy as jnp
from jax import lax
from jax.experimental import pallas as pl
from jax.experimental.pallas import tpu as pltpu
from jax.sharding import PartitionSpec as P

HEAD_DIM = 128
KEY_BLOCK = 1024
ROW_BLOCK = 256
STATS = 128
PIECE = 256
MIB = 1024 * 1024

rope_base = 10000.0
norm_eps = 1e-05
LOG2E = math.log2(math.e)
LOWEST = -1e30


def params(mib):
    return pltpu.CompilerParams(vmem_limit_bytes=mib * MIB)


def layer_norm(token_rows):
    widened = token_rows.astype(jnp.float32)
    centred = widened - jnp.mean(widened, axis=-1, keepdims=True)
    variance = jnp.mean(centred * centred, axis=-1, keepdims=True)
    return centred * lax.rsqrt(variance + norm_eps)


def rope_tables(positions):
    half_dim = HEAD_DIM // 2
    frequency = jnp.exp(-jnp.log(rope_base) * jnp.arange(half_dim, dtype=jnp.float32) / half_dim)
    angles = positions.astype(jnp.float32)[:, None] * frequency[None, :]
    cosine = jnp.cos(angles)
    sine = jnp.sin(angles)
    return (
        jnp.concatenate([cosine, cosine], axis=-1),
        jnp.concatenate([-sine, sine], axis=-1),
    )


def deal_kernel(order_ref, tp_ref, x_ref, first_ref, second_ref, guest_ref):
    each, cut, _ = first_ref.shape
    start = pl.program_id(0) * each
    for at in range(each):
        normed = layer_norm(x_ref[order_ref[start + at]]).astype(jnp.bfloat16)
        first_ref[at] = normed[:cut]
        second_ref[at] = normed[cut:]
        guest_ref[at] = normed


def deal(tokens, deal_order, tp_index, piece):
    groups, _, width = tokens.shape
    each = 4
    steps = groups // each
    cut = piece // 2
    own = pl.BlockSpec((each, cut, width), lambda d, order, t: (d, 0, 0))
    guest = pl.BlockSpec((each, piece, width), lambda d, order, t: ((d + steps // 2) % steps, 0, 0))
    return pl.pallas_call(
        deal_kernel,
        grid_spec=pltpu.PrefetchScalarGridSpec(
            num_scalar_prefetch=2,
            grid=(steps,),
            in_specs=[pl.BlockSpec((groups, piece, width), lambda d, order, t: (0, t[0], 0))],
            out_specs=[own, own, guest],
        ),
        out_shape=[
            jax.ShapeDtypeStruct((groups, rows, width), jnp.bfloat16) for rows in (cut, cut, piece)
        ],
        compiler_params=params(20),
        name="deal",
    )(deal_order, tp_index, tokens)


def project_kernel(turned, heads, sources, cut, tp_ref, *refs):
    if sources > 1:
        mine_ref, other_ref, cos_ref, sin_ref, *refs, x_ref = refs
        shards_in, rows_each, _ = mine_ref.shape

        @pl.when(pl.program_id(0) == 0)
        def _():
            t = tp_ref[0]
            for piece in range(rows_each // cut):
                rows = slice(piece * cut, (piece + 1) * cut)
                for shard in range(shards_in):
                    at = (piece * shards_in + shard) * 2
                    for part_ref, side in ((mine_ref, t), (other_ref, 1 - t)):
                        start = pl.multiple_of((at + side) * cut, cut)
                        x_ref[pl.ds(start, cut), :] = part_ref[shard, rows, :]
    else:
        x_ref, cos_ref, sin_ref, *refs = refs
    count = len(turned)
    step = min(512, x_ref.shape[0])
    for first in range(0, x_ref.shape[0], step):
        rows = slice(first, first + step)
        for w_ref, out_ref, turn in zip(refs[:count], refs[count:], turned):
            product = jnp.dot(x_ref[rows, :], w_ref[...], preferred_element_type=jnp.float32)
            if not turn:
                out_ref[rows, :] = product.astype(jnp.bfloat16)
                continue
            for head in range(heads):
                cut = slice(head * HEAD_DIM, (head + 1) * HEAD_DIM)
                part = product[:, cut]
                swapped = pltpu.roll(part, HEAD_DIM // 2, 1)
                out_ref[rows, cut] = (
                    part * cos_ref[rows, :] + swapped * sin_ref[rows, :]
                ).astype(jnp.bfloat16)


def project(x, cut, tp_index, tables, weights, turned):
    depth = x[0].shape[-1]
    rows = sum(math.prod(part.shape[:-1]) for part in x)
    width = weights[0].shape[1]
    block = min(256, width)
    table = pl.BlockSpec((rows, HEAD_DIM), lambda n, t: (0, 0))
    count = len(weights)
    return pl.pallas_call(
        functools.partial(project_kernel, turned, block // HEAD_DIM, len(x), cut),
        grid_spec=pltpu.PrefetchScalarGridSpec(
            num_scalar_prefetch=1,
            grid=(width // block,),
            in_specs=[pl.BlockSpec(part.shape, lambda n, t, r=part.ndim: (0,) * r) for part in x]
            + [table, table]
            + [pl.BlockSpec((depth, block), lambda n, t: (0, n))] * count,
            out_specs=[pl.BlockSpec((rows, block), lambda n, t: (0, n))] * count,
            scratch_shapes=[pltpu.VMEM((rows, depth), jnp.bfloat16)] if len(x) > 1 else [],
        ),
        out_shape=[jax.ShapeDtypeStruct((rows, width), jnp.bfloat16)] * count,
        compiler_params=params(24),
        cost_estimate=pl.CostEstimate(
            flops=2 * rows * depth * width * count,
            bytes_accessed=2 * (rows * depth + count * width * (rows + depth)),
            transcendentals=0,
        ),
        name="project",
    )(tp_index, *x, *tables, *weights)


def replace_kernel(block, index_ref, cache_ref, fresh_ref, out_ref):
    first = pl.program_id(1) * block
    count = index_ref.shape[1]
    row = first + lax.broadcasted_iota(jnp.int32, (block, count), 0)
    hits = jnp.where(row == index_ref[...], 1.0, 0.0)
    picked = jnp.dot(
        hits.astype(jnp.bfloat16), fresh_ref[0], preferred_element_type=jnp.float32
    )
    is_hit = jnp.sum(hits, axis=1, keepdims=True) > 0.5
    out_ref[0] = jnp.where(is_hit, picked, cache_ref[0, 0].astype(jnp.float32)).astype(jnp.bfloat16)


def replace_rows(cache, fresh, rec_index):
    _, _, rows, width = cache.shape
    count = rec_index.shape[1]
    block = 512
    return pl.pallas_call(
        functools.partial(replace_kernel, block),
        grid=(2, rows // block),
        in_specs=[
            pl.BlockSpec((1, count), lambda c, r: (0, 0)),
            pl.BlockSpec((1, 1, block, width), lambda c, r: (0, c, r, 0)),
            pl.BlockSpec((1, count, width), lambda c, r: (c, 0, 0)),
        ],
        out_specs=pl.BlockSpec((1, block, width), lambda c, r: (c, r, 0)),
        out_shape=jax.ShapeDtypeStruct((2, rows, width), jnp.bfloat16),
        compiler_params=params(20),
        cost_estimate=pl.CostEstimate(
            flops=4 * rows * count * width, bytes_accessed=10 * rows * width, transcendentals=0
        ),
        name="replace_rows",
    )(rec_index, cache, fresh)


def fold_keys(jobs, m_ref, acc_ref):
    scale = HEAD_DIM**-0.5 * LOG2E

    def scores_of(job):
        _, queries, keys, _ = job
        for key_block, mask in keys():
            for at in range(0, key_block.shape[0], PIECE):
                scores = lax.dot_general(
                    queries(),
                    key_block[at : at + PIECE],
                    (((1,), (1,)), ((), ())),
                    preferred_element_type=jnp.float32,
                )
                if mask is not None:
                    scores = jnp.where(mask[:, at : at + PIECE], scores, LOWEST)
                yield scores

    upcoming = list(scores_of(jobs[0]))
    for at, (place, _, _, values) in enumerate(jobs):
        scores = upcoming
        ahead = scores_of(jobs[at + 1]) if at + 1 < len(jobs) else iter(())
        upcoming = []
        old_max = m_ref[place]
        widest = functools.reduce(jnp.maximum, scores)
        new_max = jnp.maximum(old_max, jnp.max(widest, axis=1, keepdims=True))
        factor = jnp.exp2((old_max - new_max) * scale)
        shift = new_max * scale
        shift = jnp.concatenate([shift] * (PIECE // HEAD_DIM), axis=1)
        weights = []
        for part in scores:
            upcoming += [found for _, found in zip(range(1), ahead)]
            weights.append(jnp.exp2(part * scale - shift).astype(jnp.bfloat16))
        upcoming += list(ahead)
        seen = values()
        widened = jnp.concatenate([seen, jnp.ones(seen.shape, jnp.bfloat16)], axis=1)
        product = jnp.dot(
            jnp.concatenate(weights, axis=1), widened, preferred_element_type=jnp.float32
        )
        acc_ref[place] = acc_ref[place] * jnp.concatenate([factor, factor], axis=1) + product
        m_ref[place] = new_max


def attend_kernel(causal, chunk, chunks, piece, sides, count_ref, q_ref, k_ref, v_ref, *refs):
    if causal:
        new_refs, refs = refs[: 2 * chunks], refs[2 * chunks :]
    o_ref, lse_ref, m_ref, acc_ref = refs
    scale = HEAD_DIM**-0.5 * LOG2E
    rows_in = q_ref.shape[0]
    per_step = q_ref.shape[1] // HEAD_DIM
    step = pl.program_id(0)
    used = count_ref[0]
    blocks = [slice(at, at + ROW_BLOCK) for at in range(0, rows_in, ROW_BLOCK)]
    places = [(head, block) for head in range(per_step) for block in blocks]
    m_ref[...] = jnp.full(m_ref.shape, LOWEST, jnp.float32)
    acc_ref[...] = jnp.zeros(acc_ref.shape, jnp.float32)
    k_all = k_ref.at[(0,) * (len(k_ref.shape) - 2)]
    v_all = v_ref.at[(0,) * (len(v_ref.shape) - 2)]

    def head_cut(head):
        return slice(head * HEAD_DIM, (head + 1) * HEAD_DIM)

    def job(place, picks):
        head, block = place
        cut = head_cut(head)

        def values():
            found = [values_ref[at, cut] for _, values_ref, at, _ in picks]
            return found[0] if len(found) == 1 else jnp.concatenate(found, axis=0)

        return (
            place,
            lambda: q_ref[block, cut],
            lambda: [(keys_ref[at, cut], mask) for keys_ref, _, at, mask in picks],
            values,
        )

    def visit(block, masked):
        start = pl.multiple_of(block * KEY_BLOCK, KEY_BLOCK)
        mask = None
        if masked:
            mask = lax.broadcasted_iota(jnp.int32, (1, KEY_BLOCK), 1) < used - start
        picks = [(k_all, v_all, pl.ds(start, KEY_BLOCK), mask)]
        fold_keys([job(place, picks) for place in places], m_ref, acc_ref)

    full = used // KEY_BLOCK
    pl.loop(0, full)(lambda block: visit(block, False))

    @pl.when(used % KEY_BLOCK > 0)
    def _():
        visit(full, True)

    if causal:
        each = piece // sides
        row = lax.broadcasted_iota(jnp.int32, (ROW_BLOCK, ROW_BLOCK), 0)
        key = lax.broadcasted_iota(jnp.int32, (ROW_BLOCK, ROW_BLOCK), 1)

        def natural(at, of_chunk):
            within = at % piece
            inside = (within // each) * (each * chunks) + of_chunk * each + within % each
            return (at // piece) * (piece * chunks) + inside

        row_at = natural(row, chunk)
        masks = [natural(key, key_chunk) <= row_at for key_chunk in range(chunks)]
        jobs = []
        for place in places:
            picks = []
            for key_chunk in range(chunks):
                pair = new_refs[2 * key_chunk : 2 * key_chunk + 2]
                if place[1].start:
                    picks.append((*pair, slice(0, place[1].start), None))
                picks.append((*pair, place[1], masks[key_chunk]))
            jobs.append(job(place, picks))
        fold_keys(jobs, m_ref, acc_ref)

    for head, block in places:
        rows = block
        total = acc_ref[head, block, HEAD_DIM:]
        seen = total > 0.0
        safe = jnp.where(seen, total, 1.0)
        out = (acc_ref[head, block, :HEAD_DIM] / safe).astype(jnp.bfloat16)
        column = step * per_step + head
        o_ref[rows, pl.ds(pl.multiple_of(column * HEAD_DIM, HEAD_DIM), HEAD_DIM)] = out
        lse = jnp.where(seen, m_ref[head, block] * scale + jnp.log2(safe), LOWEST)
        lane = lax.broadcasted_iota(jnp.int32, (ROW_BLOCK, STATS), 1)
        before = jnp.where(column == 0, 0.0, lse_ref[rows, :])
        lse_ref[rows, :] = jnp.where(lane == column, lse, before)

    @pl.when(step == pl.num_programs(0) - 1)
    def _():
        for rows in blocks:
            left = lse_ref[rows, :]
            packed = jnp.zeros_like(left)
            for turn in range(3):
                part = left.astype(jnp.bfloat16).astype(jnp.float32)
                left = left - part
                packed = packed + (pltpu.roll(part, turn * STATS // 4, 1) if turn else part)
            o_ref[rows, o_ref.shape[1] - STATS :] = packed.astype(jnp.bfloat16)


def attend(count, groups, chunk, chunks, sides, queries, cache, new=()):
    width = queries.shape[1]
    heads = width // HEAD_DIM
    per_step = 2
    rows = cache.shape[-2]
    causal = len(new) > 0
    rows_in = queries.shape[0]
    lead = cache.ndim - 3
    shape = (1,) * (lead + 1) + (rows, per_step * HEAD_DIM)
    every = pl.BlockSpec((rows_in, per_step * HEAD_DIM), lambda h, n: (0, h))

    def half(which):
        return pl.BlockSpec(shape, lambda h, n: (0,) * lead + (which, 0, h))

    keys_seen = rows + (rows_in if causal else 0)
    out = pl.pallas_call(
        functools.partial(attend_kernel, causal, chunk, chunks, rows_in // groups, sides),
        grid_spec=pltpu.PrefetchScalarGridSpec(
            num_scalar_prefetch=1,
            grid=(heads // per_step,),
            in_specs=[
                every,
                half(0),
                half(1),
            ]
            + [every] * len(new),
            out_specs=pl.BlockSpec((rows_in, width + STATS), lambda h, n: (0, 0)),
            scratch_shapes=[
                pltpu.VMEM((rows_in, STATS), jnp.float32),
                pltpu.VMEM((per_step, rows_in, HEAD_DIM), jnp.float32),
                pltpu.VMEM((per_step, rows_in, 2 * HEAD_DIM), jnp.float32),
            ],
        ),
        out_shape=jax.ShapeDtypeStruct((rows_in, width + STATS), jnp.bfloat16),
        compiler_params=params(30),
        cost_estimate=pl.CostEstimate(
            flops=16 * rows_in * keys_seen * width,
            bytes_accessed=4 * rows * width + 4 * rows_in * width,
            transcendentals=rows_in * keys_seen * heads,
        ),
        name="attend_own" if causal else "attend_guest",
    )(count, queries, cache, cache, *new)
    return out.reshape(groups, rows_in // groups, width + STATS)


def merge_kernel(groups, heads, inverse_ref, tp_ref, own_ref, guest_ref, w_ref, *refs):
    *out_refs, att_ref, share_ref = refs
    piece = own_ref.shape[1]
    width = heads * HEAD_DIM
    step = pl.program_id(0)

    def stats(part_ref, at):
        packed = part_ref[at, :, width:].astype(jnp.float32)
        return (
            packed
            + pltpu.roll(packed, STATS - STATS // 4, 1)
            + pltpu.roll(packed, STATS - STATS // 2, 1)
        )

    @pl.when(step == 0)
    def _():
        lane = lax.broadcasted_iota(jnp.int32, (piece, STATS), 1)
        rows = [pl.ds(request * piece, piece) for request in range(groups)]
        for request in range(groups):
            source = inverse_ref[request]
            helper = lax.rem(source + groups // 2, groups)
            ahead = stats(guest_ref, helper) - stats(own_ref, source)
            share = jnp.where(lane < heads, 1.0 / (1.0 + jnp.exp2(ahead)), 0.0)
            high = share.astype(jnp.bfloat16).astype(jnp.float32)
            rest = pltpu.roll(share - high, STATS // 4, 1)
            share_ref[rows[request], :] = (high + rest).astype(jnp.bfloat16)
        lane = lax.broadcasted_iota(jnp.int32, (STATS, width), 0)
        head = lax.broadcasted_iota(jnp.int32, (STATS, width), 1) // HEAD_DIM
        spread = jnp.where((lane == head) | (lane == head + STATS // 4), 1.0, 0.0)
        shares = jnp.dot(
            share_ref[...], spread.astype(jnp.bfloat16), preferred_element_type=jnp.float32
        )
        for request in range(groups):
            source = inverse_ref[request]
            helper = lax.rem(source + groups // 2, groups)
            own = own_ref[source, :, :width].astype(jnp.float32)
            guest = guest_ref[helper, :, :width].astype(jnp.float32)
            share = shares[request * piece : (request + 1) * piece]
            att_ref[rows[request], :] = (guest + share * (own - guest)).astype(jnp.bfloat16)

    product = jnp.dot(att_ref[...], w_ref[...], preferred_element_type=jnp.float32).astype(
        jnp.bfloat16
    )
    each = pl.num_programs(0) // len(out_refs)
    for at, out_ref in enumerate(out_refs):
        pl.when(step // each == at)(functools.partial(out_ref.__setitem__, ..., product))


def merge(inverse, tp_index, splits, own, guest, w_out):
    groups, piece, _ = guest.shape
    width = w_out.shape[0]
    heads = width // HEAD_DIM
    columns = w_out.shape[1]
    block = 512
    rows = groups * piece
    steps = columns // block
    each = steps // splits

    def w_at(n, i, t):
        return (0, (n + each * (1 - t[0])) % steps if splits == 2 else n)

    def out_at(which):
        return lambda n, i, t: (0, jnp.clip(n - which * each, 0, each - 1))

    part = pl.BlockSpec(guest.shape, lambda n, i, t: (0, 0, 0))
    return pl.pallas_call(
        functools.partial(merge_kernel, groups, heads),
        grid_spec=pltpu.PrefetchScalarGridSpec(
            num_scalar_prefetch=2,
            grid=(steps,),
            in_specs=[part, part, pl.BlockSpec((width, block), w_at)],
            out_specs=[pl.BlockSpec((rows, block), out_at(which)) for which in range(splits)],
            scratch_shapes=[
                pltpu.VMEM((rows, width), jnp.bfloat16),
                pltpu.VMEM((rows, STATS), jnp.bfloat16),
            ],
        ),
        out_shape=[jax.ShapeDtypeStruct((rows, columns // splits), jnp.bfloat16)] * splits,
        compiler_params=params(20),
        cost_estimate=pl.CostEstimate(
            flops=rows * width * columns,
            bytes_accessed=rows * columns,
            transcendentals=0,
        ),
        name="merge",
    )(inverse, tp_index, own, guest, w_out)


def exchange(value):
    return lax.all_to_all(value, "grp", split_axis=0, concat_axis=0, tiled=True)


def shards(
    tokens,
    w_query,
    w_key,
    w_value,
    w_out,
    own_cache,
    guest_cache,
    rec_hidden,
    deal_order,
    own_len,
    guest_len,
    rec_index,
):
    groups = lax.axis_size("grp")
    tp_size = lax.axis_size("tp")
    group_id = lax.axis_index("grp")
    tp_id = lax.axis_index("tp")
    partner_id = (group_id + groups // 2) % groups
    width = w_query.shape[1]
    heads = width // HEAD_DIM
    shard_rows = tokens.shape[1]
    span = shard_rows * groups
    piece = shard_rows // tp_size

    chunks = 2
    chunk_rows = shard_rows // chunks
    paired = tp_size == 2 and piece % 32 == 0
    sides = 2 if paired else 1
    each = chunk_rows // sides
    tp_index = tp_id.astype(jnp.int32)[None]
    tied = lax.optimization_barrier
    neighbour = [(0, 1), (1, 0)]

    if paired:
        dealt = deal(tokens, deal_order, tp_index, piece)
        own_rows, guest_rows = dealt[:2], dealt[2]
    else:
        mine = lax.dynamic_slice_in_dim(tokens, tp_id * piece, piece, 1)
        normed = layer_norm(mine).astype(jnp.bfloat16)
        own_rows = jnp.take(normed, deal_order, axis=0)
        guest_rows = jnp.roll(own_rows, groups // 2, axis=0)

    def in_chunks(rows):
        rows = rows.reshape(groups, sides, chunks, each, -1)
        return jnp.transpose(rows, (2, 0, 1, 3, 4)).reshape(chunks, span // chunks, -1)

    def with_other(arrived):
        return [arrived, lax.ppermute(arrived, "tp", neighbour)]

    def gathered(rows):
        arrived = lax.all_gather(exchange(rows), "tp", axis=0)
        parts = in_chunks(jnp.transpose(arrived, (1, 0, 2, 3)))
        return [[part] for part in parts]

    row_order = in_chunks(jnp.arange(span, dtype=jnp.int32)).reshape(span)

    def place(owner, helper):
        return own_len[owner] + guest_len[helper] + row_order

    def projected(x, tables, chunk, weights, turned):
        if chunk is not None:
            rows = slice(chunk * span // chunks, (chunk + 1) * span // chunks)
            tables = [table[rows] for table in tables]
        return project(x, each, tp_index, tables, weights, turned)

    def own_project(chunk):
        return projected(
            own_x[chunk], own_tables, chunk, (w_query, w_key, w_value), (True, True, False)
        )

    def own_attend(chunk, queries):
        count = own_len[group_id][None]
        return attend(count, groups, chunk, chunks, sides, queries, cache, new)

    def guest_attend(chunk, queries):
        count = guest_len[group_id][None]
        return attend(count, groups, chunk, chunks, sides, queries, guest_cache)

    def guest_project():
        if paired:
            (queries,) = projected(guest_x, guest_tables, None, (w_query,), (True,))
            return [queries[: span // chunks], queries[span // chunks :]]
        return [
            projected(guest_x[chunk], guest_tables, chunk, (w_query,), (True,))[0]
            for chunk in range(chunks)
        ]

    own_tables = rope_tables(place(group_id, partner_id))
    guest_tables = rope_tables(place(partner_id, group_id))
    rec_tables = rope_tables(rec_index[0])
    rec_rows = layer_norm(rec_hidden[0]).astype(jnp.bfloat16)
    rec_parts = projected((rec_rows,), rec_tables, None, (w_key, w_value), (True, False))

    if paired:
        arrived = exchange(own_rows[0])
        arrived, own_tables, guest_tables, rec_parts, own_rows = tied(
            (arrived, own_tables, guest_tables, rec_parts, own_rows)
        )
        own_x = [with_other(arrived)]
        cache = replace_rows(own_cache, jnp.stack(rec_parts), rec_index)
        arrived = exchange(own_rows[1])
        arrived, cache, own_x, guest_rows = tied((arrived, cache, own_x, guest_rows))
        own_x.append(with_other(arrived))
        arrived = exchange(guest_rows)
        made = [own_project(chunk) for chunk in range(chunks)]
        arrived, made = tied((arrived, made))
        guest_x = with_other(arrived)
    else:
        cache = replace_rows(own_cache, jnp.stack(rec_parts), rec_index)
        own_x = gathered(own_rows)
        guest_x = gathered(guest_rows)
        made = [own_project(chunk) for chunk in range(chunks)]
    new = [part for parts in made for part in parts[1:]]
    inverse = jnp.sum(
        jnp.where(
            deal_order[None, :] == jnp.arange(groups, dtype=deal_order.dtype)[:, None],
            jnp.arange(groups, dtype=jnp.int32)[None, :],
            0,
        ),
        axis=1,
    )

    own_out = [own_attend(0, made[0][0])]
    own_out, query = tied((own_out, made[1][0]))
    own_part = [exchange(own_out[0])]
    own_out.append(own_attend(1, query))
    own_part, own_out, guest_x = tied((own_part, own_out, guest_x))
    own_part.append(exchange(own_out[1]))
    queries = guest_project()
    guest_out = [guest_attend(0, queries[0])]
    own_part, guest_out, query = tied((own_part, guest_out, queries[1]))
    guest_part = [exchange(guest_out[0])]
    guest_out.append(guest_attend(1, query))
    guest_part, guest_out = tied((guest_part, guest_out))
    guest_part.append(exchange(guest_out[1]))

    def merged(chunk):
        splits = 2 if paired else 1
        return merge(inverse, tp_index, splits, own_part[chunk], guest_part[chunk], w_out)

    def summed(partial):
        if paired:
            theirs, mine = partial
            arrived = lax.ppermute(theirs, "tp", neighbour).astype(jnp.float32)
            total = (mine.astype(jnp.float32) + arrived).astype(jnp.bfloat16)
        else:
            total = lax.psum_scatter(partial[0], "tp", scatter_dimension=1, tiled=True)
        return total.reshape(groups, sides, 1, each, -1)

    partial = merged(0)
    guest_part[1], partial = tied((guest_part[1], partial))
    mixed = [summed(partial), summed(merged(1))]
    return jnp.concatenate(mixed, axis=2).reshape(groups, shard_rows, -1)


def solution(mesh):
    return jax.shard_map(
        shards,
        mesh=mesh,
        in_specs=(
            P(None, "grp", None),
            P(None, "tp"),
            P(None, "tp"),
            P(None, "tp"),
            P("tp", None),
            P("grp", None, None, "tp"),
            P("grp", None, None, "tp"),
            P("grp", None, None),
            P(),
            P(),
            P(),
            P("grp", None),
        ),
        out_specs=P(None, "grp", "tp"),
        check_vma=False,
    )
```

```python
import functools
import math

import jax
import jax.numpy as jnp
from jax import lax
from jax.experimental import pallas as pl
from jax.experimental.pallas import tpu as pltpu
from jax.sharding import PartitionSpec as P

HEAD_DIM = 128
KEY_BLOCK = 1024
ROW_BLOCK = 256
STATS = 128
PIECE = 256
VMEM_LIMIT = 60 * 1024 * 1024

rope_base = 10000.0
norm_eps = 1e-05
LOG2E = math.log2(math.e)
LOWEST = -1e30


def params():
    return pltpu.CompilerParams(vmem_limit_bytes=VMEM_LIMIT)


def layer_norm(token_rows):
    widened = token_rows.astype(jnp.float32)
    centred = widened - jnp.mean(widened, axis=-1, keepdims=True)
    variance = jnp.mean(centred * centred, axis=-1, keepdims=True)
    return centred * lax.rsqrt(variance + norm_eps)


def rope_tables(positions):
    half_dim = HEAD_DIM // 2
    frequency = jnp.exp(-jnp.log(rope_base) * jnp.arange(half_dim, dtype=jnp.float32) / half_dim)
    angles = positions.astype(jnp.float32)[:, None] * frequency[None, :]
    cosine = jnp.cos(angles)
    sine = jnp.sin(angles)
    return (
        jnp.concatenate([cosine, cosine], axis=-1),
        jnp.concatenate([-sine, sine], axis=-1),
    )


def deal_kernel(order_ref, tp_ref, x_ref, first_ref, second_ref, guest_ref):
    each, cut, _ = first_ref.shape
    start = pl.program_id(0) * each
    for at in range(each):
        normed = layer_norm(x_ref[order_ref[start + at]]).astype(jnp.bfloat16)
        first_ref[at] = normed[:cut]
        second_ref[at] = normed[cut:]
        guest_ref[at] = normed


def deal(tokens, deal_order, tp_index, piece):
    groups, _, width = tokens.shape
    each = 4
    steps = groups // each
    cut = piece // 2
    own = pl.BlockSpec((each, cut, width), lambda d, order, t: (d, 0, 0))
    guest = pl.BlockSpec((each, piece, width), lambda d, order, t: ((d + steps // 2) % steps, 0, 0))
    return pl.pallas_call(
        deal_kernel,
        grid_spec=pltpu.PrefetchScalarGridSpec(
            num_scalar_prefetch=2,
            grid=(steps,),
            in_specs=[pl.BlockSpec((groups, piece, width), lambda d, order, t: (0, t[0], 0))],
            out_specs=[own, own, guest],
        ),
        out_shape=[
            jax.ShapeDtypeStruct((groups, rows, width), jnp.bfloat16) for rows in (cut, cut, piece)
        ],
        compiler_params=params(),
        name="deal",
    )(deal_order, tp_index, tokens)


def project_kernel(turned, heads, sources, cut, tp_ref, *refs):
    if sources > 1:
        mine_ref, other_ref, cos_ref, sin_ref, *refs, x_ref = refs
        shards_in, rows_each, _ = mine_ref.shape

        @pl.when(pl.program_id(0) == 0)
        def _():
            t = tp_ref[0]
            for piece in range(rows_each // cut):
                rows = slice(piece * cut, (piece + 1) * cut)
                for shard in range(shards_in):
                    at = (piece * shards_in + shard) * 2
                    for part_ref, side in ((mine_ref, t), (other_ref, 1 - t)):
                        start = pl.multiple_of((at + side) * cut, cut)
                        x_ref[pl.ds(start, cut), :] = part_ref[shard, rows, :]
    else:
        x_ref, cos_ref, sin_ref, *refs = refs
    count = len(turned)
    step = min(512, x_ref.shape[0])
    for first in range(0, x_ref.shape[0], step):
        rows = slice(first, first + step)
        for w_ref, out_ref, turn in zip(refs[:count], refs[count:], turned):
            product = jnp.dot(x_ref[rows, :], w_ref[...], preferred_element_type=jnp.float32)
            if not turn:
                out_ref[rows, :] = product.astype(jnp.bfloat16)
                continue
            for head in range(heads):
                cut = slice(head * HEAD_DIM, (head + 1) * HEAD_DIM)
                part = product[:, cut]
                swapped = pltpu.roll(part, HEAD_DIM // 2, 1)
                out_ref[rows, cut] = (
                    part * cos_ref[rows, :] + swapped * sin_ref[rows, :]
                ).astype(jnp.bfloat16)


def project(x, cut, tp_index, tables, table_at, weights, turned):
    depth = x[0].shape[-1]
    rows = sum(math.prod(part.shape[:-1]) for part in x)
    width = weights[0].shape[1]
    block = min(256, width)
    table = pl.BlockSpec((rows, HEAD_DIM), lambda n, t: (table_at, 0))
    count = len(weights)
    return pl.pallas_call(
        functools.partial(project_kernel, turned, block // HEAD_DIM, len(x), cut),
        grid_spec=pltpu.PrefetchScalarGridSpec(
            num_scalar_prefetch=1,
            grid=(width // block,),
            in_specs=[pl.BlockSpec(part.shape, lambda n, t, r=part.ndim: (0,) * r) for part in x]
            + [table, table]
            + [pl.BlockSpec((depth, block), lambda n, t: (0, n))] * count,
            out_specs=[pl.BlockSpec((rows, block), lambda n, t: (0, n))] * count,
            scratch_shapes=[pltpu.VMEM((rows, depth), jnp.bfloat16)] if len(x) > 1 else [],
        ),
        out_shape=[jax.ShapeDtypeStruct((rows, width), jnp.bfloat16)] * count,
        compiler_params=params(),
        cost_estimate=pl.CostEstimate(
            flops=rows * depth * width,
            bytes_accessed=rows * depth,
            transcendentals=0,
        ),
        name="project",
    )(tp_index, *x, *tables, *weights)


def replace_kernel(block, index_ref, cache_ref, keys_ref, values_ref, out_ref):
    first = pl.program_id(1) * block
    count = index_ref.shape[1]

    def fill(fresh_ref):
        row = first + lax.broadcasted_iota(jnp.int32, (block, count), 0)
        hits = jnp.where(row == index_ref[...], 1.0, 0.0)
        picked = jnp.dot(
            hits.astype(jnp.bfloat16), fresh_ref[...], preferred_element_type=jnp.float32
        )
        is_hit = jnp.sum(hits, axis=1, keepdims=True) > 0.5
        out_ref[0] = jnp.where(is_hit, picked, cache_ref[0, 0].astype(jnp.float32)).astype(
            jnp.bfloat16
        )

    for which, fresh_ref in enumerate((keys_ref, values_ref)):
        pl.when(pl.program_id(0) == which)(functools.partial(fill, fresh_ref))


def replace_rows(cache, keys, values, rec_index):
    _, _, rows, width = cache.shape
    count = rec_index.shape[1]
    block = 512
    return pl.pallas_call(
        functools.partial(replace_kernel, block),
        grid=(2, rows // block),
        in_specs=[
            pl.BlockSpec((1, count), lambda c, r: (0, 0)),
            pl.BlockSpec((1, 1, block, width), lambda c, r: (0, c, r, 0)),
            pl.BlockSpec((count, width), lambda c, r: (0, 0)),
            pl.BlockSpec((count, width), lambda c, r: (0, 0)),
        ],
        out_specs=pl.BlockSpec((1, block, width), lambda c, r: (c, r, 0)),
        out_shape=jax.ShapeDtypeStruct((2, rows, width), jnp.bfloat16),
        compiler_params=params(),
        cost_estimate=pl.CostEstimate(
            flops=4 * rows * count * width, bytes_accessed=10 * rows * width, transcendentals=0
        ),
        name="replace_rows",
    )(rec_index, cache, keys, values)


def fold_keys(jobs, m_ref, acc_ref):
    scale = HEAD_DIM**-0.5 * LOG2E

    def scores_of(job):
        _, queries, keys, _ = job
        for key_block, mask in keys():
            for at in range(0, key_block.shape[0], PIECE):
                scores = lax.dot_general(
                    queries(),
                    key_block[at : at + PIECE],
                    (((1,), (1,)), ((), ())),
                    preferred_element_type=jnp.float32,
                )
                if mask is not None:
                    scores = jnp.where(mask[:, at : at + PIECE], scores, LOWEST)
                yield scores

    upcoming = list(scores_of(jobs[0]))
    for at, (place, _, _, values) in enumerate(jobs):
        scores = upcoming
        ahead = scores_of(jobs[at + 1]) if at + 1 < len(jobs) else iter(())
        upcoming = []
        old_max = m_ref[place]
        widest = functools.reduce(jnp.maximum, scores)
        new_max = jnp.maximum(old_max, jnp.max(widest, axis=1, keepdims=True))
        factor = jnp.exp2((old_max - new_max) * scale)
        shift = new_max * scale
        shift = jnp.concatenate([shift] * (PIECE // HEAD_DIM), axis=1)
        weights = []
        for part in scores:
            upcoming += [found for _, found in zip(range(1), ahead)]
            weights.append(jnp.exp2(part * scale - shift).astype(jnp.bfloat16))
        upcoming += list(ahead)
        seen = values()
        widened = jnp.concatenate([seen, jnp.ones(seen.shape, jnp.bfloat16)], axis=1)
        product = jnp.dot(
            jnp.concatenate(weights, axis=1), widened, preferred_element_type=jnp.float32
        )
        acc_ref[place] = acc_ref[place] * jnp.concatenate([factor, factor], axis=1) + product
        m_ref[place] = new_max


def attend_kernel(causal, chunk, chunks, piece, sides, count_ref, q_ref, k_ref, v_ref, *refs):
    if causal:
        new_refs, refs = refs[: 2 * chunks], refs[2 * chunks :]
    o_ref, lse_ref, m_ref, acc_ref = refs
    scale = HEAD_DIM**-0.5 * LOG2E
    rows_in = q_ref.shape[0]
    per_step = q_ref.shape[1] // HEAD_DIM
    step = pl.program_id(0)
    used = count_ref[0]
    blocks = [slice(at, at + ROW_BLOCK) for at in range(0, rows_in, ROW_BLOCK)]
    places = [(head, block) for head in range(per_step) for block in blocks]
    m_ref[...] = jnp.full(m_ref.shape, LOWEST, jnp.float32)
    acc_ref[...] = jnp.zeros(acc_ref.shape, jnp.float32)
    k_all = k_ref.at[(0,) * (len(k_ref.shape) - 2)]
    v_all = v_ref.at[(0,) * (len(v_ref.shape) - 2)]

    def head_cut(head):
        return slice(head * HEAD_DIM, (head + 1) * HEAD_DIM)

    def job(place, picks):
        head, block = place
        cut = head_cut(head)

        def values():
            found = [values_ref[at, cut] for _, values_ref, at, _ in picks]
            return found[0] if len(found) == 1 else jnp.concatenate(found, axis=0)

        return (
            place,
            lambda: q_ref[block, cut],
            lambda: [(keys_ref[at, cut], mask) for keys_ref, _, at, mask in picks],
            values,
        )

    def visit(block, masked):
        start = pl.multiple_of(block * KEY_BLOCK, KEY_BLOCK)
        mask = None
        if masked:
            mask = lax.broadcasted_iota(jnp.int32, (1, KEY_BLOCK), 1) < used - start
        picks = [(k_all, v_all, pl.ds(start, KEY_BLOCK), mask)]
        fold_keys([job(place, picks) for place in places], m_ref, acc_ref)

    full = used // KEY_BLOCK
    pl.loop(0, full)(lambda block: visit(block, False))

    @pl.when(used % KEY_BLOCK > 0)
    def _():
        visit(full, True)

    if causal:
        each = piece // sides
        row = lax.broadcasted_iota(jnp.int32, (ROW_BLOCK, ROW_BLOCK), 0)
        key = lax.broadcasted_iota(jnp.int32, (ROW_BLOCK, ROW_BLOCK), 1)

        def natural(at, of_chunk):
            within = at % piece
            inside = (within // each) * (each * chunks) + of_chunk * each + within % each
            return (at // piece) * (piece * chunks) + inside

        row_at = natural(row, chunk)
        masks = [natural(key, key_chunk) <= row_at for key_chunk in range(chunks)]
        jobs = []
        for place in places:
            picks = []
            for key_chunk in range(chunks):
                pair = new_refs[2 * key_chunk : 2 * key_chunk + 2]
                if place[1].start:
                    picks.append((*pair, slice(0, place[1].start), None))
                picks.append((*pair, place[1], masks[key_chunk]))
            jobs.append(job(place, picks))
        fold_keys(jobs, m_ref, acc_ref)

    for head, block in places:
        rows = block
        total = acc_ref[head, block, HEAD_DIM:]
        seen = total > 0.0
        safe = jnp.where(seen, total, 1.0)
        out = (acc_ref[head, block, :HEAD_DIM] / safe).astype(jnp.bfloat16)
        column = step * per_step + head
        o_ref[rows, pl.ds(pl.multiple_of(column * HEAD_DIM, HEAD_DIM), HEAD_DIM)] = out
        lse = jnp.where(seen, m_ref[head, block] * scale + jnp.log2(safe), LOWEST)
        lane = lax.broadcasted_iota(jnp.int32, (ROW_BLOCK, STATS), 1)
        before = jnp.where(column == 0, 0.0, lse_ref[rows, :])
        lse_ref[rows, :] = jnp.where(lane == column, lse, before)

    @pl.when(step == pl.num_programs(0) - 1)
    def _():
        for rows in blocks:
            left = lse_ref[rows, :]
            packed = jnp.zeros_like(left)
            for turn in range(3):
                part = left.astype(jnp.bfloat16).astype(jnp.float32)
                left = left - part
                packed = packed + (pltpu.roll(part, turn * STATS // 4, 1) if turn else part)
            o_ref[rows, o_ref.shape[1] - STATS :] = packed.astype(jnp.bfloat16)


def attend(count, rows_in, groups, chunk, chunks, sides, query, cache, new=()):
    queries, q_at = query
    width = queries.shape[1]
    heads = width // HEAD_DIM
    per_step = 2
    rows = cache.shape[-2]
    causal = len(new) > 0
    lead = cache.ndim - 3
    shape = (1,) * (lead + 1) + (rows, per_step * HEAD_DIM)
    every = pl.BlockSpec((rows_in, per_step * HEAD_DIM), lambda h, n: (0, h))

    def half(which):
        return pl.BlockSpec(shape, lambda h, n: (0,) * lead + (which, 0, h))

    keys_seen = rows + (rows_in if causal else 0)
    out = pl.pallas_call(
        functools.partial(attend_kernel, causal, chunk, chunks, rows_in // groups, sides),
        grid_spec=pltpu.PrefetchScalarGridSpec(
            num_scalar_prefetch=1,
            grid=(heads // per_step,),
            in_specs=[
                pl.BlockSpec((rows_in, per_step * HEAD_DIM), lambda h, n: (q_at, h)),
                half(0),
                half(1),
            ]
            + [every] * len(new),
            out_specs=pl.BlockSpec((rows_in, width + STATS), lambda h, n: (0, 0)),
            scratch_shapes=[
                pltpu.VMEM((rows_in, STATS), jnp.float32),
                pltpu.VMEM((per_step, rows_in, HEAD_DIM), jnp.float32),
                pltpu.VMEM((per_step, rows_in, 2 * HEAD_DIM), jnp.float32),
            ],
        ),
        out_shape=jax.ShapeDtypeStruct((rows_in, width + STATS), jnp.bfloat16),
        compiler_params=params(),
        cost_estimate=pl.CostEstimate(
            flops=2 * rows_in * keys_seen * width,
            bytes_accessed=4 * rows_in * width,
            transcendentals=0,
        ),
        name="attend_own" if causal else "attend_guest",
    )(count, queries, cache, cache, *new)
    return out.reshape(groups, rows_in // groups, width + STATS)


def merge_kernel(groups, heads, inverse_ref, tp_ref, own_ref, guest_ref, w_ref, *refs):
    *out_refs, att_ref, share_ref = refs
    piece = own_ref.shape[1]
    width = heads * HEAD_DIM
    step = pl.program_id(0)

    def stats(part_ref, at):
        packed = part_ref[at, :, width:].astype(jnp.float32)
        return (
            packed
            + pltpu.roll(packed, STATS - STATS // 4, 1)
            + pltpu.roll(packed, STATS - STATS // 2, 1)
        )

    @pl.when(step == 0)
    def _():
        lane = lax.broadcasted_iota(jnp.int32, (piece, STATS), 1)
        rows = [pl.ds(request * piece, piece) for request in range(groups)]
        for request in range(groups):
            source = inverse_ref[request]
            helper = lax.rem(source + groups // 2, groups)
            ahead = stats(guest_ref, helper) - stats(own_ref, source)
            share = jnp.where(lane < heads, 1.0 / (1.0 + jnp.exp2(ahead)), 0.0)
            high = share.astype(jnp.bfloat16).astype(jnp.float32)
            rest = pltpu.roll(share - high, STATS // 4, 1)
            share_ref[rows[request], :] = (high + rest).astype(jnp.bfloat16)
        lane = lax.broadcasted_iota(jnp.int32, (STATS, width), 0)
        head = lax.broadcasted_iota(jnp.int32, (STATS, width), 1) // HEAD_DIM
        spread = jnp.where((lane == head) | (lane == head + STATS // 4), 1.0, 0.0)
        shares = jnp.dot(
            share_ref[...], spread.astype(jnp.bfloat16), preferred_element_type=jnp.float32
        )
        for request in range(groups):
            source = inverse_ref[request]
            helper = lax.rem(source + groups // 2, groups)
            own = own_ref[source, :, :width].astype(jnp.float32)
            guest = guest_ref[helper, :, :width].astype(jnp.float32)
            share = shares[request * piece : (request + 1) * piece]
            att_ref[rows[request], :] = (guest + share * (own - guest)).astype(jnp.bfloat16)

    product = jnp.dot(att_ref[...], w_ref[...], preferred_element_type=jnp.float32).astype(
        jnp.bfloat16
    )
    each = pl.num_programs(0) // len(out_refs)
    for at, out_ref in enumerate(out_refs):
        pl.when(step // each == at)(functools.partial(out_ref.__setitem__, ..., product))


def merge(inverse, tp_index, splits, own, guest, w_out):
    groups, piece, _ = guest.shape
    width = w_out.shape[0]
    heads = width // HEAD_DIM
    columns = w_out.shape[1]
    block = 512
    rows = groups * piece
    steps = columns // block
    each = steps // splits

    def w_at(n, i, t):
        return (0, (n + each * (1 - t[0])) % steps if splits == 2 else n)

    def out_at(which):
        return lambda n, i, t: (0, jnp.clip(n - which * each, 0, each - 1))

    part = pl.BlockSpec(guest.shape, lambda n, i, t: (0, 0, 0))
    return pl.pallas_call(
        functools.partial(merge_kernel, groups, heads),
        grid_spec=pltpu.PrefetchScalarGridSpec(
            num_scalar_prefetch=2,
            grid=(steps,),
            in_specs=[part, part, pl.BlockSpec((width, block), w_at)],
            out_specs=[pl.BlockSpec((rows, block), out_at(which)) for which in range(splits)],
            scratch_shapes=[
                pltpu.VMEM((rows, width), jnp.bfloat16),
                pltpu.VMEM((rows, STATS), jnp.bfloat16),
            ],
        ),
        out_shape=[jax.ShapeDtypeStruct((rows, columns // splits), jnp.bfloat16)] * splits,
        compiler_params=params(),
        cost_estimate=pl.CostEstimate(
            flops=rows * width * columns,
            bytes_accessed=rows * columns,
            transcendentals=0,
        ),
        name="merge",
    )(inverse, tp_index, own, guest, w_out)


def exchange(value):
    return lax.all_to_all(value, "grp", split_axis=0, concat_axis=0, tiled=True)


def shards(
    tokens,
    w_query,
    w_key,
    w_value,
    w_out,
    own_cache,
    guest_cache,
    rec_hidden,
    deal_order,
    own_len,
    guest_len,
    rec_index,
):
    groups = lax.axis_size("grp")
    tp_size = lax.axis_size("tp")
    group_id = lax.axis_index("grp")
    tp_id = lax.axis_index("tp")
    partner_id = (group_id + groups // 2) % groups
    width = w_query.shape[1]
    heads = width // HEAD_DIM
    shard_rows = tokens.shape[1]
    span = shard_rows * groups
    piece = shard_rows // tp_size

    chunks = 2
    chunk_rows = shard_rows // chunks
    paired = tp_size == 2 and piece % 32 == 0
    sides = 2 if paired else 1
    each = chunk_rows // sides
    tp_index = tp_id.astype(jnp.int32)[None]
    tied = lax.optimization_barrier
    neighbour = [(0, 1), (1, 0)]

    if paired:
        dealt = deal(tokens, deal_order, tp_index, piece)
        own_rows, guest_rows = dealt[:2], dealt[2]
    else:
        mine = lax.dynamic_slice_in_dim(tokens, tp_id * piece, piece, 1)
        normed = layer_norm(mine).astype(jnp.bfloat16)
        own_rows = jnp.take(normed, deal_order, axis=0)
        guest_rows = jnp.roll(own_rows, groups // 2, axis=0)

    def in_chunks(rows):
        rows = rows.reshape(groups, sides, chunks, each, -1)
        return jnp.transpose(rows, (2, 0, 1, 3, 4)).reshape(chunks, span // chunks, -1)

    def with_other(arrived):
        return [arrived, lax.ppermute(arrived, "tp", neighbour)]

    def gathered(rows):
        arrived = lax.all_gather(exchange(rows), "tp", axis=0)
        parts = in_chunks(jnp.transpose(arrived, (1, 0, 2, 3)))
        return [[part] for part in parts]

    row_order = in_chunks(jnp.arange(span, dtype=jnp.int32)).reshape(span)

    def place(owner, helper):
        return own_len[owner] + guest_len[helper] + row_order

    def projected(x, tables, chunk, weights, turned):
        return project(x, each, tp_index, tables, chunk, weights, turned)

    def own_project(chunk):
        return projected(
            own_x[chunk], own_tables, chunk, (w_query, w_key, w_value), (True, True, False)
        )

    def own_attend(chunk, queries):
        count = own_len[group_id][None]
        rows_in = span // chunks
        return attend(count, rows_in, groups, chunk, chunks, sides, (queries, 0), cache, new)

    def guest_attend(chunk, query):
        count = guest_len[group_id][None]
        rows_in = span // chunks
        return attend(count, rows_in, groups, chunk, chunks, sides, query, guest_cache)

    def guest_project():
        if paired:
            (queries,) = projected(guest_x, guest_tables, 0, (w_query,), (True,))
            return [(queries, 0), (queries, 1)]
        return [
            (projected(guest_x[chunk], guest_tables, chunk, (w_query,), (True,))[0], 0)
            for chunk in range(chunks)
        ]

    own_tables = rope_tables(place(group_id, partner_id))
    guest_tables = rope_tables(place(partner_id, group_id))
    rec_tables = rope_tables(rec_index[0])
    rec_rows = layer_norm(rec_hidden[0]).astype(jnp.bfloat16)
    rec_parts = projected((rec_rows,), rec_tables, 0, (w_key, w_value), (True, False))

    if paired:
        arrived = exchange(own_rows[0])
        arrived, own_tables, guest_tables, rec_parts, own_rows = tied(
            (arrived, own_tables, guest_tables, rec_parts, own_rows)
        )
        own_x = [with_other(arrived)]
        cache = replace_rows(own_cache, *rec_parts, rec_index)
        arrived = exchange(own_rows[1])
        arrived, cache, own_x, guest_rows = tied((arrived, cache, own_x, guest_rows))
        own_x.append(with_other(arrived))
        arrived = exchange(guest_rows)
        made = [own_project(chunk) for chunk in range(chunks)]
        arrived, made = tied((arrived, made))
        guest_x = with_other(arrived)
    else:
        cache = replace_rows(own_cache, *rec_parts, rec_index)
        own_x = gathered(own_rows)
        guest_x = gathered(guest_rows)
        made = [own_project(chunk) for chunk in range(chunks)]
    new = [part for parts in made for part in parts[1:]]
    inverse = jnp.sum(
        jnp.where(
            deal_order[None, :] == jnp.arange(groups, dtype=deal_order.dtype)[:, None],
            jnp.arange(groups, dtype=jnp.int32)[None, :],
            0,
        ),
        axis=1,
    )

    own_out = [own_attend(0, made[0][0])]
    own_out, query = tied((own_out, made[1][0]))
    own_part = [exchange(own_out[0])]
    own_out.append(own_attend(1, query))
    own_part, own_out = tied((own_part, own_out))
    own_part.append(exchange(own_out[1]))
    guest_x, own_out = tied((guest_x, own_out))
    queries = guest_project()
    guest_out = [guest_attend(0, queries[0])]
    own_part, guest_out, query = tied((own_part, guest_out, queries[1][0]))
    guest_part = [exchange(guest_out[0])]
    guest_out.append(guest_attend(1, (query, queries[1][1])))
    guest_part, guest_out = tied((guest_part, guest_out))
    guest_part.append(exchange(guest_out[1]))

    def merged(chunk):
        splits = 2 if paired and chunk else 1
        return merge(inverse, tp_index, splits, own_part[chunk], guest_part[chunk], w_out)

    def summed(partial, split):
        if split:
            theirs, mine = partial
            arrived = lax.ppermute(theirs, "tp", neighbour).astype(jnp.float32)
            total = (mine.astype(jnp.float32) + arrived).astype(jnp.bfloat16)
        else:
            total = lax.psum_scatter(partial[0], "tp", scatter_dimension=1, tiled=True)
        return total.reshape(groups, sides, 1, each, -1)

    partial = merged(0)
    guest_part[1], partial = tied((guest_part[1], partial))
    mixed = [summed(partial, False), summed(merged(1), paired)]
    return jnp.concatenate(mixed, axis=2).reshape(groups, shard_rows, -1)


def solution(mesh):
    return jax.shard_map(
        shards,
        mesh=mesh,
        in_specs=(
            P(None, "grp", None),
            P(None, "tp"),
            P(None, "tp"),
            P(None, "tp"),
            P("tp", None),
            P("grp", None, None, "tp"),
            P("grp", None, None, "tp"),
            P("grp", None, None),
            P(),
            P(),
            P(),
            P("grp", None),
        ),
        out_specs=P(None, "grp", "tp"),
        check_vma=False,
    )
```

```python
import functools
import math

import jax
import jax.numpy as jnp
from jax import lax
from jax.experimental import pallas as pl
from jax.experimental.pallas import tpu as pltpu
from jax.sharding import PartitionSpec as P

HEAD_DIM = 128
KEY_BLOCK = 1024
ROW_BLOCK = 256
STATS = 128
PIECE = 256
VMEM_LIMIT = 60 * 1024 * 1024

rope_base = 10000.0
norm_eps = 1e-05
LOG2E = math.log2(math.e)
LOWEST = -1e30


def params():
    return pltpu.CompilerParams(vmem_limit_bytes=VMEM_LIMIT)


def layer_norm(token_rows):
    widened = token_rows.astype(jnp.float32)
    centred = widened - jnp.mean(widened, axis=-1, keepdims=True)
    variance = jnp.mean(centred * centred, axis=-1, keepdims=True)
    return centred * lax.rsqrt(variance + norm_eps)


def rope_tables(positions):
    half_dim = HEAD_DIM // 2
    frequency = jnp.exp(-jnp.log(rope_base) * jnp.arange(half_dim, dtype=jnp.float32) / half_dim)
    angles = positions.astype(jnp.float32)[:, None] * frequency[None, :]
    cosine = jnp.cos(angles)
    sine = jnp.sin(angles)
    return (
        jnp.concatenate([cosine, cosine], axis=-1),
        jnp.concatenate([-sine, sine], axis=-1),
    )


def deal_kernel(order_ref, tp_ref, x_ref, first_ref, second_ref, guest_ref):
    each, cut, _ = first_ref.shape
    start = pl.program_id(0) * each
    for at in range(each):
        normed = layer_norm(x_ref[order_ref[start + at]]).astype(jnp.bfloat16)
        first_ref[at] = normed[:cut]
        second_ref[at] = normed[cut:]
        guest_ref[at] = normed


def deal(tokens, deal_order, tp_index, piece):
    groups, _, width = tokens.shape
    each = 4
    steps = groups // each
    cut = piece // 2
    own = pl.BlockSpec((each, cut, width), lambda d, order, t: (d, 0, 0))
    guest = pl.BlockSpec((each, piece, width), lambda d, order, t: ((d + steps // 2) % steps, 0, 0))
    return pl.pallas_call(
        deal_kernel,
        grid_spec=pltpu.PrefetchScalarGridSpec(
            num_scalar_prefetch=2,
            grid=(steps,),
            in_specs=[pl.BlockSpec((groups, piece, width), lambda d, order, t: (0, t[0], 0))],
            out_specs=[own, own, guest],
        ),
        out_shape=[
            jax.ShapeDtypeStruct((groups, rows, width), jnp.bfloat16) for rows in (cut, cut, piece)
        ],
        compiler_params=params(),
        name="deal",
    )(deal_order, tp_index, tokens)


def project_kernel(turned, heads, sources, cut, tp_ref, *refs):
    if sources > 1:
        mine_ref, other_ref, cos_ref, sin_ref, *refs, x_ref = refs
        shards_in, rows_each, _ = mine_ref.shape

        @pl.when(pl.program_id(0) == 0)
        def _():
            t = tp_ref[0]
            for piece in range(rows_each // cut):
                rows = slice(piece * cut, (piece + 1) * cut)
                for shard in range(shards_in):
                    at = (piece * shards_in + shard) * 2
                    for part_ref, side in ((mine_ref, t), (other_ref, 1 - t)):
                        start = pl.multiple_of((at + side) * cut, cut)
                        x_ref[pl.ds(start, cut), :] = part_ref[shard, rows, :]
    else:
        x_ref, cos_ref, sin_ref, *refs = refs
    count = len(turned)
    step = min(512, x_ref.shape[0])
    for first in range(0, x_ref.shape[0], step):
        rows = slice(first, first + step)
        for w_ref, out_ref, turn in zip(refs[:count], refs[count:], turned):
            product = jnp.dot(x_ref[rows, :], w_ref[...], preferred_element_type=jnp.float32)
            if not turn:
                out_ref[rows, :] = product.astype(jnp.bfloat16)
                continue
            for head in range(heads):
                cut = slice(head * HEAD_DIM, (head + 1) * HEAD_DIM)
                part = product[:, cut]
                swapped = pltpu.roll(part, HEAD_DIM // 2, 1)
                out_ref[rows, cut] = (
                    part * cos_ref[rows, :] + swapped * sin_ref[rows, :]
                ).astype(jnp.bfloat16)


def project(x, cut, tp_index, tables, table_at, weights, turned):
    depth = x[0].shape[-1]
    rows = sum(math.prod(part.shape[:-1]) for part in x)
    width = weights[0].shape[1]
    block = min(256, width)
    table = pl.BlockSpec((rows, HEAD_DIM), lambda n, t: (table_at, 0))
    count = len(weights)
    return pl.pallas_call(
        functools.partial(project_kernel, turned, block // HEAD_DIM, len(x), cut),
        grid_spec=pltpu.PrefetchScalarGridSpec(
            num_scalar_prefetch=1,
            grid=(width // block,),
            in_specs=[pl.BlockSpec(part.shape, lambda n, t, r=part.ndim: (0,) * r) for part in x]
            + [table, table]
            + [pl.BlockSpec((depth, block), lambda n, t: (0, n))] * count,
            out_specs=[pl.BlockSpec((rows, block), lambda n, t: (0, n))] * count,
            scratch_shapes=[pltpu.VMEM((rows, depth), jnp.bfloat16)] if len(x) > 1 else [],
        ),
        out_shape=[jax.ShapeDtypeStruct((rows, width), jnp.bfloat16)] * count,
        compiler_params=params(),
        cost_estimate=pl.CostEstimate(
            flops=2 * rows * depth * width * count,
            bytes_accessed=2 * (rows * depth + count * width * (rows + depth)),
            transcendentals=0,
        ),
        name="project",
    )(tp_index, *x, *tables, *weights)


def replace_kernel(block, index_ref, cache_ref, keys_ref, values_ref, out_ref):
    first = pl.program_id(1) * block
    count = index_ref.shape[1]

    def fill(fresh_ref):
        row = first + lax.broadcasted_iota(jnp.int32, (block, count), 0)
        hits = jnp.where(row == index_ref[...], 1.0, 0.0)
        picked = jnp.dot(
            hits.astype(jnp.bfloat16), fresh_ref[...], preferred_element_type=jnp.float32
        )
        is_hit = jnp.sum(hits, axis=1, keepdims=True) > 0.5
        out_ref[0] = jnp.where(is_hit, picked, cache_ref[0, 0].astype(jnp.float32)).astype(
            jnp.bfloat16
        )

    for which, fresh_ref in enumerate((keys_ref, values_ref)):
        pl.when(pl.program_id(0) == which)(functools.partial(fill, fresh_ref))


def replace_rows(cache, keys, values, rec_index):
    _, _, rows, width = cache.shape
    count = rec_index.shape[1]
    block = 512
    return pl.pallas_call(
        functools.partial(replace_kernel, block),
        grid=(2, rows // block),
        in_specs=[
            pl.BlockSpec((1, count), lambda c, r: (0, 0)),
            pl.BlockSpec((1, 1, block, width), lambda c, r: (0, c, r, 0)),
            pl.BlockSpec((count, width), lambda c, r: (0, 0)),
            pl.BlockSpec((count, width), lambda c, r: (0, 0)),
        ],
        out_specs=pl.BlockSpec((1, block, width), lambda c, r: (c, r, 0)),
        out_shape=jax.ShapeDtypeStruct((2, rows, width), jnp.bfloat16),
        compiler_params=params(),
        cost_estimate=pl.CostEstimate(
            flops=4 * rows * count * width, bytes_accessed=10 * rows * width, transcendentals=0
        ),
        name="replace_rows",
    )(rec_index, cache, keys, values)


def fold_keys(jobs, m_ref, acc_ref):
    scale = HEAD_DIM**-0.5 * LOG2E

    def scores_of(job):
        _, queries, keys, _ = job
        for key_block, mask in keys():
            for at in range(0, key_block.shape[0], PIECE):
                scores = lax.dot_general(
                    queries(),
                    key_block[at : at + PIECE],
                    (((1,), (1,)), ((), ())),
                    preferred_element_type=jnp.float32,
                )
                if mask is not None:
                    scores = jnp.where(mask[:, at : at + PIECE], scores, LOWEST)
                yield scores

    upcoming = list(scores_of(jobs[0]))
    for at, (place, _, _, values) in enumerate(jobs):
        scores = upcoming
        ahead = scores_of(jobs[at + 1]) if at + 1 < len(jobs) else iter(())
        upcoming = []
        old_max = m_ref[place]
        widest = functools.reduce(jnp.maximum, scores)
        new_max = jnp.maximum(old_max, jnp.max(widest, axis=1, keepdims=True))
        factor = jnp.exp2((old_max - new_max) * scale)
        shift = new_max * scale
        shift = jnp.concatenate([shift] * (PIECE // HEAD_DIM), axis=1)
        weights = []
        for part in scores:
            upcoming += [found for _, found in zip(range(1), ahead)]
            weights.append(jnp.exp2(part * scale - shift).astype(jnp.bfloat16))
        upcoming += list(ahead)
        seen = values()
        widened = jnp.concatenate([seen, jnp.ones(seen.shape, jnp.bfloat16)], axis=1)
        product = jnp.dot(
            jnp.concatenate(weights, axis=1), widened, preferred_element_type=jnp.float32
        )
        acc_ref[place] = acc_ref[place] * jnp.concatenate([factor, factor], axis=1) + product
        m_ref[place] = new_max


def attend_kernel(causal, chunk, chunks, piece, sides, count_ref, q_ref, k_ref, v_ref, *refs):
    if causal:
        new_refs, refs = refs[: 2 * chunks], refs[2 * chunks :]
    o_ref, lse_ref, m_ref, acc_ref = refs
    scale = HEAD_DIM**-0.5 * LOG2E
    rows_in = q_ref.shape[0]
    per_step = q_ref.shape[1] // HEAD_DIM
    step = pl.program_id(0)
    used = count_ref[0]
    blocks = [slice(at, at + ROW_BLOCK) for at in range(0, rows_in, ROW_BLOCK)]
    places = [(head, block) for head in range(per_step) for block in blocks]
    m_ref[...] = jnp.full(m_ref.shape, LOWEST, jnp.float32)
    acc_ref[...] = jnp.zeros(acc_ref.shape, jnp.float32)
    k_all = k_ref.at[(0,) * (len(k_ref.shape) - 2)]
    v_all = v_ref.at[(0,) * (len(v_ref.shape) - 2)]

    def head_cut(head):
        return slice(head * HEAD_DIM, (head + 1) * HEAD_DIM)

    def job(place, picks):
        head, block = place
        cut = head_cut(head)

        def values():
            found = [values_ref[at, cut] for _, values_ref, at, _ in picks]
            return found[0] if len(found) == 1 else jnp.concatenate(found, axis=0)

        return (
            place,
            lambda: q_ref[block, cut],
            lambda: [(keys_ref[at, cut], mask) for keys_ref, _, at, mask in picks],
            values,
        )

    def visit(block, masked):
        start = pl.multiple_of(block * KEY_BLOCK, KEY_BLOCK)
        mask = None
        if masked:
            mask = lax.broadcasted_iota(jnp.int32, (1, KEY_BLOCK), 1) < used - start
        picks = [(k_all, v_all, pl.ds(start, KEY_BLOCK), mask)]
        fold_keys([job(place, picks) for place in places], m_ref, acc_ref)

    full = used // KEY_BLOCK
    pl.loop(0, full)(lambda block: visit(block, False))

    @pl.when(used % KEY_BLOCK > 0)
    def _():
        visit(full, True)

    if causal:
        each = piece // sides
        row = lax.broadcasted_iota(jnp.int32, (ROW_BLOCK, ROW_BLOCK), 0)
        key = lax.broadcasted_iota(jnp.int32, (ROW_BLOCK, ROW_BLOCK), 1)

        def natural(at, of_chunk):
            within = at % piece
            inside = (within // each) * (each * chunks) + of_chunk * each + within % each
            return (at // piece) * (piece * chunks) + inside

        row_at = natural(row, chunk)
        masks = [natural(key, key_chunk) <= row_at for key_chunk in range(chunks)]
        jobs = []
        for place in places:
            picks = []
            for key_chunk in range(chunks):
                pair = new_refs[2 * key_chunk : 2 * key_chunk + 2]
                if place[1].start:
                    picks.append((*pair, slice(0, place[1].start), None))
                picks.append((*pair, place[1], masks[key_chunk]))
            jobs.append(job(place, picks))
        fold_keys(jobs, m_ref, acc_ref)

    for head, block in places:
        rows = block
        total = acc_ref[head, block, HEAD_DIM:]
        seen = total > 0.0
        safe = jnp.where(seen, total, 1.0)
        out = (acc_ref[head, block, :HEAD_DIM] / safe).astype(jnp.bfloat16)
        column = step * per_step + head
        o_ref[rows, pl.ds(pl.multiple_of(column * HEAD_DIM, HEAD_DIM), HEAD_DIM)] = out
        lse = jnp.where(seen, m_ref[head, block] * scale + jnp.log2(safe), LOWEST)
        lane = lax.broadcasted_iota(jnp.int32, (ROW_BLOCK, STATS), 1)
        before = jnp.where(column == 0, 0.0, lse_ref[rows, :])
        lse_ref[rows, :] = jnp.where(lane == column, lse, before)

    @pl.when(step == pl.num_programs(0) - 1)
    def _():
        for rows in blocks:
            left = lse_ref[rows, :]
            packed = jnp.zeros_like(left)
            for turn in range(3):
                part = left.astype(jnp.bfloat16).astype(jnp.float32)
                left = left - part
                packed = packed + (pltpu.roll(part, turn * STATS // 4, 1) if turn else part)
            o_ref[rows, o_ref.shape[1] - STATS :] = packed.astype(jnp.bfloat16)


def attend(count, groups, chunk, chunks, sides, queries, cache, new=()):
    width = queries.shape[1]
    heads = width // HEAD_DIM
    per_step = 2
    rows = cache.shape[-2]
    causal = len(new) > 0
    rows_in = queries.shape[0]
    lead = cache.ndim - 3
    shape = (1,) * (lead + 1) + (rows, per_step * HEAD_DIM)
    every = pl.BlockSpec((rows_in, per_step * HEAD_DIM), lambda h, n: (0, h))

    def half(which):
        return pl.BlockSpec(shape, lambda h, n: (0,) * lead + (which, 0, h))

    keys_seen = rows + (rows_in if causal else 0)
    out = pl.pallas_call(
        functools.partial(attend_kernel, causal, chunk, chunks, rows_in // groups, sides),
        grid_spec=pltpu.PrefetchScalarGridSpec(
            num_scalar_prefetch=1,
            grid=(heads // per_step,),
            in_specs=[
                pl.BlockSpec((rows_in, per_step * HEAD_DIM), lambda h, n: (0, h)),
                half(0),
                half(1),
            ]
            + [every] * len(new),
            out_specs=pl.BlockSpec((rows_in, width + STATS), lambda h, n: (0, 0)),
            scratch_shapes=[
                pltpu.VMEM((rows_in, STATS), jnp.float32),
                pltpu.VMEM((per_step, rows_in, HEAD_DIM), jnp.float32),
                pltpu.VMEM((per_step, rows_in, 2 * HEAD_DIM), jnp.float32),
            ],
        ),
        out_shape=jax.ShapeDtypeStruct((rows_in, width + STATS), jnp.bfloat16),
        compiler_params=params(),
        cost_estimate=pl.CostEstimate(
            flops=16 * rows_in * keys_seen * width,
            bytes_accessed=4 * rows * width + 4 * rows_in * width,
            transcendentals=0,
        ),
        name="attend_own" if causal else "attend_guest",
    )(count, queries, cache, cache, *new)
    return out.reshape(groups, rows_in // groups, width + STATS)


def merge_kernel(groups, heads, inverse_ref, tp_ref, own_ref, guest_ref, w_ref, *refs):
    *out_refs, att_ref, share_ref = refs
    piece = own_ref.shape[1]
    width = heads * HEAD_DIM
    step = pl.program_id(0)

    def stats(part_ref, at):
        packed = part_ref[at, :, width:].astype(jnp.float32)
        return (
            packed
            + pltpu.roll(packed, STATS - STATS // 4, 1)
            + pltpu.roll(packed, STATS - STATS // 2, 1)
        )

    @pl.when(step == 0)
    def _():
        lane = lax.broadcasted_iota(jnp.int32, (piece, STATS), 1)
        rows = [pl.ds(request * piece, piece) for request in range(groups)]
        for request in range(groups):
            source = inverse_ref[request]
            helper = lax.rem(source + groups // 2, groups)
            ahead = stats(guest_ref, helper) - stats(own_ref, source)
            share = jnp.where(lane < heads, 1.0 / (1.0 + jnp.exp2(ahead)), 0.0)
            high = share.astype(jnp.bfloat16).astype(jnp.float32)
            rest = pltpu.roll(share - high, STATS // 4, 1)
            share_ref[rows[request], :] = (high + rest).astype(jnp.bfloat16)
        lane = lax.broadcasted_iota(jnp.int32, (STATS, width), 0)
        head = lax.broadcasted_iota(jnp.int32, (STATS, width), 1) // HEAD_DIM
        spread = jnp.where((lane == head) | (lane == head + STATS // 4), 1.0, 0.0)
        shares = jnp.dot(
            share_ref[...], spread.astype(jnp.bfloat16), preferred_element_type=jnp.float32
        )
        for request in range(groups):
            source = inverse_ref[request]
            helper = lax.rem(source + groups // 2, groups)
            own = own_ref[source, :, :width].astype(jnp.float32)
            guest = guest_ref[helper, :, :width].astype(jnp.float32)
            share = shares[request * piece : (request + 1) * piece]
            att_ref[rows[request], :] = (guest + share * (own - guest)).astype(jnp.bfloat16)

    product = jnp.dot(att_ref[...], w_ref[...], preferred_element_type=jnp.float32).astype(
        jnp.bfloat16
    )
    each = pl.num_programs(0) // len(out_refs)
    for at, out_ref in enumerate(out_refs):
        pl.when(step // each == at)(functools.partial(out_ref.__setitem__, ..., product))


def merge(inverse, tp_index, splits, own, guest, w_out):
    groups, piece, _ = guest.shape
    width = w_out.shape[0]
    heads = width // HEAD_DIM
    columns = w_out.shape[1]
    block = 512
    rows = groups * piece
    steps = columns // block
    each = steps // splits

    def w_at(n, i, t):
        return (0, (n + each * (1 - t[0])) % steps if splits == 2 else n)

    def out_at(which):
        return lambda n, i, t: (0, jnp.clip(n - which * each, 0, each - 1))

    part = pl.BlockSpec(guest.shape, lambda n, i, t: (0, 0, 0))
    return pl.pallas_call(
        functools.partial(merge_kernel, groups, heads),
        grid_spec=pltpu.PrefetchScalarGridSpec(
            num_scalar_prefetch=2,
            grid=(steps,),
            in_specs=[part, part, pl.BlockSpec((width, block), w_at)],
            out_specs=[pl.BlockSpec((rows, block), out_at(which)) for which in range(splits)],
            scratch_shapes=[
                pltpu.VMEM((rows, width), jnp.bfloat16),
                pltpu.VMEM((rows, STATS), jnp.bfloat16),
            ],
        ),
        out_shape=[jax.ShapeDtypeStruct((rows, columns // splits), jnp.bfloat16)] * splits,
        compiler_params=params(),
        cost_estimate=pl.CostEstimate(
            flops=rows * width * columns,
            bytes_accessed=rows * columns,
            transcendentals=0,
        ),
        name="merge",
    )(inverse, tp_index, own, guest, w_out)


def exchange(value):
    return lax.all_to_all(value, "grp", split_axis=0, concat_axis=0, tiled=True)


def shards(
    tokens,
    w_query,
    w_key,
    w_value,
    w_out,
    own_cache,
    guest_cache,
    rec_hidden,
    deal_order,
    own_len,
    guest_len,
    rec_index,
):
    groups = lax.axis_size("grp")
    tp_size = lax.axis_size("tp")
    group_id = lax.axis_index("grp")
    tp_id = lax.axis_index("tp")
    partner_id = (group_id + groups // 2) % groups
    width = w_query.shape[1]
    heads = width // HEAD_DIM
    shard_rows = tokens.shape[1]
    span = shard_rows * groups
    piece = shard_rows // tp_size

    chunks = 2
    chunk_rows = shard_rows // chunks
    paired = tp_size == 2 and piece % 32 == 0
    sides = 2 if paired else 1
    each = chunk_rows // sides
    tp_index = tp_id.astype(jnp.int32)[None]
    tied = lax.optimization_barrier
    neighbour = [(0, 1), (1, 0)]

    if paired:
        dealt = deal(tokens, deal_order, tp_index, piece)
        own_rows, guest_rows = dealt[:2], dealt[2]
    else:
        mine = lax.dynamic_slice_in_dim(tokens, tp_id * piece, piece, 1)
        normed = layer_norm(mine).astype(jnp.bfloat16)
        own_rows = jnp.take(normed, deal_order, axis=0)
        guest_rows = jnp.roll(own_rows, groups // 2, axis=0)

    def in_chunks(rows):
        rows = rows.reshape(groups, sides, chunks, each, -1)
        return jnp.transpose(rows, (2, 0, 1, 3, 4)).reshape(chunks, span // chunks, -1)

    def with_other(arrived):
        return [arrived, lax.ppermute(arrived, "tp", neighbour)]

    def gathered(rows):
        arrived = lax.all_gather(exchange(rows), "tp", axis=0)
        parts = in_chunks(jnp.transpose(arrived, (1, 0, 2, 3)))
        return [[part] for part in parts]

    row_order = in_chunks(jnp.arange(span, dtype=jnp.int32)).reshape(span)

    def place(owner, helper):
        return own_len[owner] + guest_len[helper] + row_order

    def projected(x, tables, chunk, weights, turned):
        return project(x, each, tp_index, tables, chunk, weights, turned)

    def own_project(chunk):
        return projected(
            own_x[chunk], own_tables, chunk, (w_query, w_key, w_value), (True, True, False)
        )

    def own_attend(chunk, queries):
        count = own_len[group_id][None]
        return attend(count, groups, chunk, chunks, sides, queries, cache, new)

    def guest_attend(chunk, x):
        (queries,) = projected(x, guest_tables, chunk, (w_query,), (True,))
        count = guest_len[group_id][None]
        return attend(count, groups, chunk, chunks, sides, queries, guest_cache)

    own_tables = rope_tables(place(group_id, partner_id))
    guest_tables = rope_tables(place(partner_id, group_id))
    rec_tables = rope_tables(rec_index[0])
    rec_rows = layer_norm(rec_hidden[0]).astype(jnp.bfloat16)
    rec_parts = projected((rec_rows,), rec_tables, 0, (w_key, w_value), (True, False))

    if paired:
        arrived = exchange(own_rows[0])
        arrived, own_tables, guest_tables, rec_parts, own_rows = tied(
            (arrived, own_tables, guest_tables, rec_parts, own_rows)
        )
        own_x = [with_other(arrived)]
        cache = replace_rows(own_cache, *rec_parts, rec_index)
        arrived = exchange(own_rows[1])
        arrived, cache, own_x, guest_rows = tied((arrived, cache, own_x, guest_rows))
        own_x.append(with_other(arrived))
        arrived = exchange(guest_rows)
        made = [own_project(chunk) for chunk in range(chunks)]
        arrived, made = tied((arrived, made))
        guest_x = [with_other(arrived[:, :each])]
        guest_x, arrived = tied((guest_x, arrived[:, each:]))
        guest_x.append(with_other(arrived))
    else:
        cache = replace_rows(own_cache, *rec_parts, rec_index)
        own_x = gathered(own_rows)
        guest_x = gathered(guest_rows)
        made = [own_project(chunk) for chunk in range(chunks)]
    new = [part for parts in made for part in parts[1:]]
    inverse = jnp.sum(
        jnp.where(
            deal_order[None, :] == jnp.arange(groups, dtype=deal_order.dtype)[:, None],
            jnp.arange(groups, dtype=jnp.int32)[None, :],
            0,
        ),
        axis=1,
    )

    first, second = guest_x
    own_out = own_attend(0, made[0][0])
    own_out, query, first = tied((own_out, made[1][0], first))
    own_part = [exchange(own_out)]
    guest_out = guest_attend(0, first)
    own_part, guest_out, query = tied((own_part, guest_out, query))
    guest_part = [exchange(guest_out)]
    own_out = own_attend(1, query)
    guest_part, own_out, second = tied((guest_part, own_out, second))
    own_part.append(exchange(own_out))
    guest_out = guest_attend(1, second)
    own_part, guest_out = tied((own_part, guest_out))
    guest_part.append(exchange(guest_out))

    def merged(chunk):
        splits = 2 if paired else 1
        return merge(inverse, tp_index, splits, own_part[chunk], guest_part[chunk], w_out)

    def summed(partial):
        if paired:
            theirs, mine = partial
            arrived = lax.ppermute(theirs, "tp", neighbour).astype(jnp.float32)
            total = (mine.astype(jnp.float32) + arrived).astype(jnp.bfloat16)
        else:
            total = lax.psum_scatter(partial[0], "tp", scatter_dimension=1, tiled=True)
        return total.reshape(groups, sides, 1, each, -1)

    mixed = [summed(merged(0))]
    guest_part[1], mixed = tied((guest_part[1], mixed))
    mixed.append(summed(merged(1)))
    return jnp.concatenate(mixed, axis=2).reshape(groups, shard_rows, -1)


def solution(mesh):
    return jax.shard_map(
        shards,
        mesh=mesh,
        in_specs=(
            P(None, "grp", None),
            P(None, "tp"),
            P(None, "tp"),
            P(None, "tp"),
            P("tp", None),
            P("grp", None, None, "tp"),
            P("grp", None, None, "tp"),
            P("grp", None, None),
            P(),
            P(),
            P(),
            P("grp", None),
        ),
        out_specs=P(None, "grp", "tp"),
        check_vma=False,
    )
```

```python
import functools
import math

import jax
import jax.numpy as jnp
from jax import lax
from jax.experimental import pallas as pl
from jax.experimental.pallas import tpu as pltpu
from jax.sharding import PartitionSpec as P

HEAD_DIM = 128
KEY_BLOCK = 1024
ROW_BLOCK = 256
STATS = 128
PIECE = 256
VMEM_LIMIT = 60 * 1024 * 1024

rope_base = 10000.0
norm_eps = 1e-05
LOG2E = math.log2(math.e)
LOWEST = -1e30


def params():
    return pltpu.CompilerParams(vmem_limit_bytes=VMEM_LIMIT)


def layer_norm(token_rows):
    widened = token_rows.astype(jnp.float32)
    centred = widened - jnp.mean(widened, axis=-1, keepdims=True)
    variance = jnp.mean(centred * centred, axis=-1, keepdims=True)
    return centred * lax.rsqrt(variance + norm_eps)


def rope_tables(positions):
    half_dim = HEAD_DIM // 2
    frequency = jnp.exp(-jnp.log(rope_base) * jnp.arange(half_dim, dtype=jnp.float32) / half_dim)
    angles = positions.astype(jnp.float32)[:, None] * frequency[None, :]
    cosine = jnp.cos(angles)
    sine = jnp.sin(angles)
    return (
        jnp.concatenate([cosine, cosine], axis=-1),
        jnp.concatenate([-sine, sine], axis=-1),
    )


def deal_kernel(order_ref, tp_ref, x_ref, first_ref, second_ref, guest_ref):
    each, cut, _ = first_ref.shape
    start = pl.program_id(0) * each
    for at in range(each):
        normed = layer_norm(x_ref[order_ref[start + at]]).astype(jnp.bfloat16)
        first_ref[at] = normed[:cut]
        second_ref[at] = normed[cut:]
        guest_ref[at] = normed


def deal(tokens, deal_order, tp_index, piece):
    groups, _, width = tokens.shape
    each = 4
    steps = groups // each
    cut = piece // 2
    own = pl.BlockSpec((each, cut, width), lambda d, order, t: (d, 0, 0))
    guest = pl.BlockSpec((each, piece, width), lambda d, order, t: ((d + steps // 2) % steps, 0, 0))
    return pl.pallas_call(
        deal_kernel,
        grid_spec=pltpu.PrefetchScalarGridSpec(
            num_scalar_prefetch=2,
            grid=(steps,),
            in_specs=[pl.BlockSpec((groups, piece, width), lambda d, order, t: (0, t[0], 0))],
            out_specs=[own, own, guest],
        ),
        out_shape=[
            jax.ShapeDtypeStruct((groups, rows, width), jnp.bfloat16) for rows in (cut, cut, piece)
        ],
        compiler_params=params(),
        name="deal",
    )(deal_order, tp_index, tokens)


def project_kernel(turned, heads, sources, cut, tp_ref, *refs):
    if sources > 1:
        mine_ref, other_ref, cos_ref, sin_ref, *refs, x_ref = refs
        shards_in, rows_each, _ = mine_ref.shape

        @pl.when(pl.program_id(0) == 0)
        def _():
            t = tp_ref[0]
            for piece in range(rows_each // cut):
                rows = slice(piece * cut, (piece + 1) * cut)
                for shard in range(shards_in):
                    at = (piece * shards_in + shard) * 2
                    for part_ref, side in ((mine_ref, t), (other_ref, 1 - t)):
                        start = pl.multiple_of((at + side) * cut, cut)
                        x_ref[pl.ds(start, cut), :] = part_ref[shard, rows, :]
    else:
        x_ref, cos_ref, sin_ref, *refs = refs
    count = len(turned)
    step = min(512, x_ref.shape[0])
    for first in range(0, x_ref.shape[0], step):
        rows = slice(first, first + step)
        for w_ref, out_ref, turn in zip(refs[:count], refs[count:], turned):
            product = jnp.dot(x_ref[rows, :], w_ref[...], preferred_element_type=jnp.float32)
            if not turn:
                out_ref[rows, :] = product.astype(jnp.bfloat16)
                continue
            for head in range(heads):
                cut = slice(head * HEAD_DIM, (head + 1) * HEAD_DIM)
                part = product[:, cut]
                swapped = pltpu.roll(part, HEAD_DIM // 2, 1)
                out_ref[rows, cut] = (
                    part * cos_ref[rows, :] + swapped * sin_ref[rows, :]
                ).astype(jnp.bfloat16)


def project(x, cut, tp_index, tables, table_at, weights, turned):
    depth = x[0].shape[-1]
    rows = sum(math.prod(part.shape[:-1]) for part in x)
    width = weights[0].shape[1]
    block = min(256, width)
    table = pl.BlockSpec((rows, HEAD_DIM), lambda n, t: (table_at, 0))
    count = len(weights)
    return pl.pallas_call(
        functools.partial(project_kernel, turned, block // HEAD_DIM, len(x), cut),
        grid_spec=pltpu.PrefetchScalarGridSpec(
            num_scalar_prefetch=1,
            grid=(width // block,),
            in_specs=[pl.BlockSpec(part.shape, lambda n, t, r=part.ndim: (0,) * r) for part in x]
            + [table, table]
            + [pl.BlockSpec((depth, block), lambda n, t: (0, n))] * count,
            out_specs=[pl.BlockSpec((rows, block), lambda n, t: (0, n))] * count,
            scratch_shapes=[pltpu.VMEM((rows, depth), jnp.bfloat16)] if len(x) > 1 else [],
        ),
        out_shape=[jax.ShapeDtypeStruct((rows, width), jnp.bfloat16)] * count,
        compiler_params=params(),
        cost_estimate=pl.CostEstimate(
            flops=2 * rows * depth * width * count,
            bytes_accessed=2 * (rows * depth + count * width * (rows + depth)),
            transcendentals=0,
        ),
        name="project",
    )(tp_index, *x, *tables, *weights)


def replace_kernel(block, index_ref, cache_ref, keys_ref, values_ref, out_ref):
    first = pl.program_id(1) * block
    count = index_ref.shape[1]

    def fill(fresh_ref):
        row = first + lax.broadcasted_iota(jnp.int32, (block, count), 0)
        hits = jnp.where(row == index_ref[...], 1.0, 0.0)
        picked = jnp.dot(
            hits.astype(jnp.bfloat16), fresh_ref[...], preferred_element_type=jnp.float32
        )
        is_hit = jnp.sum(hits, axis=1, keepdims=True) > 0.5
        out_ref[0] = jnp.where(is_hit, picked, cache_ref[0, 0].astype(jnp.float32)).astype(
            jnp.bfloat16
        )

    for which, fresh_ref in enumerate((keys_ref, values_ref)):
        pl.when(pl.program_id(0) == which)(functools.partial(fill, fresh_ref))


def replace_rows(cache, keys, values, rec_index):
    _, _, rows, width = cache.shape
    count = rec_index.shape[1]
    block = 512
    return pl.pallas_call(
        functools.partial(replace_kernel, block),
        grid=(2, rows // block),
        in_specs=[
            pl.BlockSpec((1, count), lambda c, r: (0, 0)),
            pl.BlockSpec((1, 1, block, width), lambda c, r: (0, c, r, 0)),
            pl.BlockSpec((count, width), lambda c, r: (0, 0)),
            pl.BlockSpec((count, width), lambda c, r: (0, 0)),
        ],
        out_specs=pl.BlockSpec((1, block, width), lambda c, r: (c, r, 0)),
        out_shape=jax.ShapeDtypeStruct((2, rows, width), jnp.bfloat16),
        compiler_params=params(),
        cost_estimate=pl.CostEstimate(
            flops=4 * rows * count * width, bytes_accessed=10 * rows * width, transcendentals=0
        ),
        name="replace_rows",
    )(rec_index, cache, keys, values)


def fold_keys(jobs, m_ref, acc_ref):
    scale = HEAD_DIM**-0.5 * LOG2E

    def scores_of(job):
        _, queries, keys, _ = job
        for key_block, mask in keys():
            for at in range(0, key_block.shape[0], PIECE):
                scores = lax.dot_general(
                    queries(),
                    key_block[at : at + PIECE],
                    (((1,), (1,)), ((), ())),
                    preferred_element_type=jnp.float32,
                )
                if mask is not None:
                    scores = jnp.where(mask[:, at : at + PIECE], scores, LOWEST)
                yield scores

    upcoming = list(scores_of(jobs[0]))
    for at, (place, _, _, values) in enumerate(jobs):
        scores = upcoming
        ahead = scores_of(jobs[at + 1]) if at + 1 < len(jobs) else iter(())
        upcoming = []
        old_max = m_ref[place]
        widest = functools.reduce(jnp.maximum, scores)
        new_max = jnp.maximum(old_max, jnp.max(widest, axis=1, keepdims=True))
        factor = jnp.exp2((old_max - new_max) * scale)
        shift = new_max * scale
        shift = jnp.concatenate([shift] * (PIECE // HEAD_DIM), axis=1)
        weights = []
        for part in scores:
            upcoming += [found for _, found in zip(range(1), ahead)]
            weights.append(jnp.exp2((part * scale - shift).astype(jnp.bfloat16)))
        upcoming += list(ahead)
        seen = values()
        widened = jnp.concatenate([seen, jnp.ones(seen.shape, jnp.bfloat16)], axis=1)
        product = jnp.dot(
            jnp.concatenate(weights, axis=1), widened, preferred_element_type=jnp.float32
        )
        acc_ref[place] = acc_ref[place] * jnp.concatenate([factor, factor], axis=1) + product
        m_ref[place] = new_max


def attend_kernel(causal, chunk, chunks, piece, sides, count_ref, q_ref, k_ref, v_ref, *refs):
    if causal:
        new_refs, refs = refs[: 2 * chunks], refs[2 * chunks :]
    o_ref, lse_ref, m_ref, acc_ref = refs
    scale = HEAD_DIM**-0.5 * LOG2E
    rows_in = q_ref.shape[0]
    per_step = q_ref.shape[1] // HEAD_DIM
    step = pl.program_id(0)
    used = count_ref[0]
    blocks = [slice(at, at + ROW_BLOCK) for at in range(0, rows_in, ROW_BLOCK)]
    places = [(head, block) for head in range(per_step) for block in blocks]
    m_ref[...] = jnp.full(m_ref.shape, LOWEST, jnp.float32)
    acc_ref[...] = jnp.zeros(acc_ref.shape, jnp.float32)
    k_all = k_ref.at[(0,) * (len(k_ref.shape) - 2)]
    v_all = v_ref.at[(0,) * (len(v_ref.shape) - 2)]

    def head_cut(head):
        return slice(head * HEAD_DIM, (head + 1) * HEAD_DIM)

    def job(place, picks):
        head, block = place
        cut = head_cut(head)

        def values():
            found = [values_ref[at, cut] for _, values_ref, at, _ in picks]
            return found[0] if len(found) == 1 else jnp.concatenate(found, axis=0)

        return (
            place,
            lambda: q_ref[block, cut],
            lambda: [(keys_ref[at, cut], mask) for keys_ref, _, at, mask in picks],
            values,
        )

    def visit(block, masked):
        start = pl.multiple_of(block * KEY_BLOCK, KEY_BLOCK)
        mask = None
        if masked:
            mask = lax.broadcasted_iota(jnp.int32, (1, KEY_BLOCK), 1) < used - start
        picks = [(k_all, v_all, pl.ds(start, KEY_BLOCK), mask)]
        fold_keys([job(place, picks) for place in places], m_ref, acc_ref)

    def visit_two(pair):
        start = pl.multiple_of(pair * 2 * KEY_BLOCK, 2 * KEY_BLOCK)
        picks = [(k_all, v_all, pl.ds(start, 2 * KEY_BLOCK), None)]
        fold_keys([job(place, picks) for place in places], m_ref, acc_ref)

    full = used // KEY_BLOCK
    pl.loop(0, full // 2)(visit_two)

    @pl.when(full % 2 > 0)
    def _():
        visit(full - 1, False)

    @pl.when(used % KEY_BLOCK > 0)
    def _():
        visit(full, True)

    if causal:
        each = piece // sides
        row = lax.broadcasted_iota(jnp.int32, (ROW_BLOCK, ROW_BLOCK), 0)
        key = lax.broadcasted_iota(jnp.int32, (ROW_BLOCK, ROW_BLOCK), 1)

        def natural(at, of_chunk):
            within = at % piece
            inside = (within // each) * (each * chunks) + of_chunk * each + within % each
            return (at // piece) * (piece * chunks) + inside

        row_at = natural(row, chunk)
        masks = [natural(key, key_chunk) <= row_at for key_chunk in range(chunks)]
        jobs = []
        for place in places:
            picks = []
            for key_chunk in range(chunks):
                pair = new_refs[2 * key_chunk : 2 * key_chunk + 2]
                if place[1].start:
                    picks.append((*pair, slice(0, place[1].start), None))
                picks.append((*pair, place[1], masks[key_chunk]))
            jobs.append(job(place, picks))
        fold_keys(jobs, m_ref, acc_ref)

    for head, block in places:
        rows = block
        total = acc_ref[head, block, HEAD_DIM:]
        seen = total > 0.0
        safe = jnp.where(seen, total, 1.0)
        out = (acc_ref[head, block, :HEAD_DIM] / safe).astype(jnp.bfloat16)
        column = step * per_step + head
        o_ref[rows, pl.ds(pl.multiple_of(column * HEAD_DIM, HEAD_DIM), HEAD_DIM)] = out
        lse = jnp.where(seen, m_ref[head, block] * scale + jnp.log2(safe), LOWEST)
        lane = lax.broadcasted_iota(jnp.int32, (ROW_BLOCK, STATS), 1)
        before = jnp.where(column == 0, 0.0, lse_ref[rows, :])
        lse_ref[rows, :] = jnp.where(lane == column, lse, before)

    @pl.when(step == pl.num_programs(0) - 1)
    def _():
        for rows in blocks:
            left = lse_ref[rows, :]
            packed = jnp.zeros_like(left)
            for turn in range(3):
                part = left.astype(jnp.bfloat16).astype(jnp.float32)
                left = left - part
                packed = packed + (pltpu.roll(part, turn * STATS // 4, 1) if turn else part)
            o_ref[rows, o_ref.shape[1] - STATS :] = packed.astype(jnp.bfloat16)


def attend(count, groups, chunk, chunks, sides, queries, cache, new=()):
    width = queries.shape[1]
    heads = width // HEAD_DIM
    per_step = 2
    rows = cache.shape[-2]
    causal = len(new) > 0
    rows_in = queries.shape[0]
    lead = cache.ndim - 3
    shape = (1,) * (lead + 1) + (rows, per_step * HEAD_DIM)
    every = pl.BlockSpec((rows_in, per_step * HEAD_DIM), lambda h, n: (0, h))

    def half(which):
        return pl.BlockSpec(shape, lambda h, n: (0,) * lead + (which, 0, h))

    keys_seen = rows + (rows_in if causal else 0)
    out = pl.pallas_call(
        functools.partial(attend_kernel, causal, chunk, chunks, rows_in // groups, sides),
        grid_spec=pltpu.PrefetchScalarGridSpec(
            num_scalar_prefetch=1,
            grid=(heads // per_step,),
            in_specs=[
                pl.BlockSpec((rows_in, per_step * HEAD_DIM), lambda h, n: (0, h)),
                half(0),
                half(1),
            ]
            + [every] * len(new),
            out_specs=pl.BlockSpec((rows_in, width + STATS), lambda h, n: (0, 0)),
            scratch_shapes=[
                pltpu.VMEM((rows_in, STATS), jnp.float32),
                pltpu.VMEM((per_step, rows_in, HEAD_DIM), jnp.float32),
                pltpu.VMEM((per_step, rows_in, 2 * HEAD_DIM), jnp.float32),
            ],
        ),
        out_shape=jax.ShapeDtypeStruct((rows_in, width + STATS), jnp.bfloat16),
        compiler_params=params(),
        cost_estimate=pl.CostEstimate(
            flops=16 * rows_in * keys_seen * width,
            bytes_accessed=4 * rows * width + 4 * rows_in * width,
            transcendentals=0,
        ),
        name="attend_own" if causal else "attend_guest",
    )(count, queries, cache, cache, *new)
    return out.reshape(groups, rows_in // groups, width + STATS)


def merge_kernel(groups, heads, inverse_ref, tp_ref, own_ref, guest_ref, w_ref, *refs):
    *out_refs, att_ref, share_ref = refs
    piece = own_ref.shape[1]
    width = heads * HEAD_DIM
    step = pl.program_id(0)

    def stats(part_ref, at):
        packed = part_ref[at, :, width:].astype(jnp.float32)
        return (
            packed
            + pltpu.roll(packed, STATS - STATS // 4, 1)
            + pltpu.roll(packed, STATS - STATS // 2, 1)
        )

    @pl.when(step == 0)
    def _():
        lane = lax.broadcasted_iota(jnp.int32, (piece, STATS), 1)
        rows = [pl.ds(request * piece, piece) for request in range(groups)]
        for request in range(groups):
            source = inverse_ref[request]
            helper = lax.rem(source + groups // 2, groups)
            ahead = stats(guest_ref, helper) - stats(own_ref, source)
            share = jnp.where(lane < heads, 1.0 / (1.0 + jnp.exp2(ahead)), 0.0)
            high = share.astype(jnp.bfloat16).astype(jnp.float32)
            rest = pltpu.roll(share - high, STATS // 4, 1)
            share_ref[rows[request], :] = (high + rest).astype(jnp.bfloat16)
        lane = lax.broadcasted_iota(jnp.int32, (STATS, width), 0)
        head = lax.broadcasted_iota(jnp.int32, (STATS, width), 1) // HEAD_DIM
        spread = jnp.where((lane == head) | (lane == head + STATS // 4), 1.0, 0.0)
        shares = jnp.dot(
            share_ref[...], spread.astype(jnp.bfloat16), preferred_element_type=jnp.float32
        )
        for request in range(groups):
            source = inverse_ref[request]
            helper = lax.rem(source + groups // 2, groups)
            own = own_ref[source, :, :width].astype(jnp.float32)
            guest = guest_ref[helper, :, :width].astype(jnp.float32)
            share = shares[request * piece : (request + 1) * piece]
            att_ref[rows[request], :] = (guest + share * (own - guest)).astype(jnp.bfloat16)

    product = jnp.dot(att_ref[...], w_ref[...], preferred_element_type=jnp.float32).astype(
        jnp.bfloat16
    )
    each = pl.num_programs(0) // len(out_refs)
    for at, out_ref in enumerate(out_refs):
        pl.when(step // each == at)(functools.partial(out_ref.__setitem__, ..., product))


def merge(inverse, tp_index, splits, own, guest, w_out):
    groups, piece, _ = guest.shape
    width = w_out.shape[0]
    heads = width // HEAD_DIM
    columns = w_out.shape[1]
    block = 512
    rows = groups * piece
    steps = columns // block
    each = steps // splits

    def w_at(n, i, t):
        return (0, (n + each * (1 - t[0])) % steps if splits == 2 else n)

    def out_at(which):
        return lambda n, i, t: (0, jnp.clip(n - which * each, 0, each - 1))

    part = pl.BlockSpec(guest.shape, lambda n, i, t: (0, 0, 0))
    return pl.pallas_call(
        functools.partial(merge_kernel, groups, heads),
        grid_spec=pltpu.PrefetchScalarGridSpec(
            num_scalar_prefetch=2,
            grid=(steps,),
            in_specs=[part, part, pl.BlockSpec((width, block), w_at)],
            out_specs=[pl.BlockSpec((rows, block), out_at(which)) for which in range(splits)],
            scratch_shapes=[
                pltpu.VMEM((rows, width), jnp.bfloat16),
                pltpu.VMEM((rows, STATS), jnp.bfloat16),
            ],
        ),
        out_shape=[jax.ShapeDtypeStruct((rows, columns // splits), jnp.bfloat16)] * splits,
        compiler_params=params(),
        cost_estimate=pl.CostEstimate(
            flops=rows * width * columns,
            bytes_accessed=rows * columns,
            transcendentals=0,
        ),
        name="merge",
    )(inverse, tp_index, own, guest, w_out)


def exchange(value):
    return lax.all_to_all(value, "grp", split_axis=0, concat_axis=0, tiled=True)


def shards(
    tokens,
    w_query,
    w_key,
    w_value,
    w_out,
    own_cache,
    guest_cache,
    rec_hidden,
    deal_order,
    own_len,
    guest_len,
    rec_index,
):
    groups = lax.axis_size("grp")
    tp_size = lax.axis_size("tp")
    group_id = lax.axis_index("grp")
    tp_id = lax.axis_index("tp")
    partner_id = (group_id + groups // 2) % groups
    width = w_query.shape[1]
    heads = width // HEAD_DIM
    shard_rows = tokens.shape[1]
    span = shard_rows * groups
    piece = shard_rows // tp_size

    chunks = 2
    chunk_rows = shard_rows // chunks
    paired = tp_size == 2 and piece % 32 == 0
    sides = 2 if paired else 1
    each = chunk_rows // sides
    tp_index = tp_id.astype(jnp.int32)[None]
    tied = lax.optimization_barrier
    neighbour = [(0, 1), (1, 0)]

    if paired:
        dealt = deal(tokens, deal_order, tp_index, piece)
        own_rows, guest_rows = dealt[:2], dealt[2]
    else:
        mine = lax.dynamic_slice_in_dim(tokens, tp_id * piece, piece, 1)
        normed = layer_norm(mine).astype(jnp.bfloat16)
        own_rows = jnp.take(normed, deal_order, axis=0)
        guest_rows = jnp.roll(own_rows, groups // 2, axis=0)

    def in_chunks(rows):
        rows = rows.reshape(groups, sides, chunks, each, -1)
        return jnp.transpose(rows, (2, 0, 1, 3, 4)).reshape(chunks, span // chunks, -1)

    def with_other(arrived):
        return [arrived, lax.ppermute(arrived, "tp", neighbour)]

    def gathered(rows):
        arrived = lax.all_gather(exchange(rows), "tp", axis=0)
        parts = in_chunks(jnp.transpose(arrived, (1, 0, 2, 3)))
        return [[part] for part in parts]

    row_order = in_chunks(jnp.arange(span, dtype=jnp.int32)).reshape(span)

    def place(owner, helper):
        return own_len[owner] + guest_len[helper] + row_order

    def projected(x, tables, chunk, weights, turned):
        return project(x, each, tp_index, tables, chunk, weights, turned)

    def own_project(chunk):
        return projected(
            own_x[chunk], own_tables, chunk, (w_query, w_key, w_value), (True, True, False)
        )

    def own_attend(chunk, queries):
        count = own_len[group_id][None]
        return attend(count, groups, chunk, chunks, sides, queries, cache, new)

    def guest_attend(chunk, x):
        (queries,) = projected(x, guest_tables, chunk, (w_query,), (True,))
        count = guest_len[group_id][None]
        return attend(count, groups, chunk, chunks, sides, queries, guest_cache)

    own_tables = rope_tables(place(group_id, partner_id))
    guest_tables = rope_tables(place(partner_id, group_id))
    rec_tables = rope_tables(rec_index[0])
    rec_rows = layer_norm(rec_hidden[0]).astype(jnp.bfloat16)
    rec_parts = projected((rec_rows,), rec_tables, 0, (w_key, w_value), (True, False))

    if paired:
        arrived = exchange(own_rows[0])
        arrived, own_tables, guest_tables, rec_parts, own_rows = tied(
            (arrived, own_tables, guest_tables, rec_parts, own_rows)
        )
        own_x = [with_other(arrived)]
        cache = replace_rows(own_cache, *rec_parts, rec_index)
        arrived = exchange(own_rows[1])
        arrived, cache, own_x, guest_rows = tied((arrived, cache, own_x, guest_rows))
        own_x.append(with_other(arrived))
        arrived = exchange(guest_rows)
        made = [own_project(chunk) for chunk in range(chunks)]
        arrived, made = tied((arrived, made))
        guest_x = [with_other(arrived[:, :each])]
        guest_x, arrived = tied((guest_x, arrived[:, each:]))
        guest_x.append(with_other(arrived))
    else:
        cache = replace_rows(own_cache, *rec_parts, rec_index)
        own_x = gathered(own_rows)
        guest_x = gathered(guest_rows)
        made = [own_project(chunk) for chunk in range(chunks)]
    new = [part for parts in made for part in parts[1:]]
    inverse = jnp.sum(
        jnp.where(
            deal_order[None, :] == jnp.arange(groups, dtype=deal_order.dtype)[:, None],
            jnp.arange(groups, dtype=jnp.int32)[None, :],
            0,
        ),
        axis=1,
    )

    first, second = guest_x
    own_out = own_attend(0, made[0][0])
    own_out, query, first = tied((own_out, made[1][0], first))
    own_part = [exchange(own_out)]
    guest_out = guest_attend(0, first)
    own_part, guest_out, query = tied((own_part, guest_out, query))
    guest_part = [exchange(guest_out)]
    own_out = own_attend(1, query)
    guest_part, own_out, second = tied((guest_part, own_out, second))
    own_part.append(exchange(own_out))
    guest_out = guest_attend(1, second)
    own_part, guest_out = tied((own_part, guest_out))
    guest_part.append(exchange(guest_out))

    def merged(chunk):
        splits = 2 if paired else 1
        return merge(inverse, tp_index, splits, own_part[chunk], guest_part[chunk], w_out)

    def summed(mine, arrived):
        total = (mine.astype(jnp.float32) + arrived.astype(jnp.float32)).astype(jnp.bfloat16)
        return total.reshape(groups, sides, 1, each, -1)

    if paired:
        theirs, mine = merged(0)
        middle = theirs.shape[0] * 3 // 4
        upper = lax.ppermute(theirs[:middle], "tp", neighbour)
        upper, lower = tied((upper, theirs[middle:]))
        guest_part[1], upper = tied((guest_part[1], upper))
        lower = lax.ppermute(lower, "tp", neighbour)
        mixed = [summed(mine, jnp.concatenate([upper, lower]))]
        theirs, mine = merged(1)
        mixed.append(summed(mine, lax.ppermute(theirs, "tp", neighbour)))
    else:
        mixed = []
        for chunk in range(chunks):
            partial = lax.psum_scatter(merged(chunk)[0], "tp", scatter_dimension=1, tiled=True)
            mixed.append(partial.reshape(groups, sides, 1, each, -1))
    return jnp.concatenate(mixed, axis=2).reshape(groups, shard_rows, -1)


def solution(mesh):
    return jax.shard_map(
        shards,
        mesh=mesh,
        in_specs=(
            P(None, "grp", None),
            P(None, "tp"),
            P(None, "tp"),
            P(None, "tp"),
            P("tp", None),
            P("grp", None, None, "tp"),
            P("grp", None, None, "tp"),
            P("grp", None, None),
            P(),
            P(),
            P(),
            P("grp", None),
        ),
        out_specs=P(None, "grp", "tp"),
        check_vma=False,
    )
```

```python
import functools
import math

import jax
import jax.numpy as jnp
from jax import lax
from jax.experimental import pallas as pl
from jax.experimental.pallas import tpu as pltpu
from jax.sharding import PartitionSpec as P

HEAD_DIM = 128
KEY_BLOCK = 1024
ROW_BLOCK = 256
STATS = 128
VMEM_LIMIT = 60 * 1024 * 1024

rope_base = 10000.0
norm_eps = 1e-05
LOG2E = math.log2(math.e)
LOWEST = -1e30


def params():
    return pltpu.CompilerParams(vmem_limit_bytes=VMEM_LIMIT)


def layer_norm(token_rows):
    widened = token_rows.astype(jnp.float32)
    centred = widened - jnp.mean(widened, axis=-1, keepdims=True)
    variance = jnp.mean(centred * centred, axis=-1, keepdims=True)
    return centred * lax.rsqrt(variance + norm_eps)


def rope_tables(positions):
    half_dim = HEAD_DIM // 2
    frequency = jnp.exp(-jnp.log(rope_base) * jnp.arange(half_dim, dtype=jnp.float32) / half_dim)
    angles = positions.astype(jnp.float32)[:, None] * frequency[None, :]
    cosine = jnp.cos(angles)
    sine = jnp.sin(angles)
    return (
        jnp.concatenate([cosine, cosine], axis=-1),
        jnp.concatenate([-sine, sine], axis=-1),
    )


def deal_kernel(order_ref, tp_ref, x_ref, first_ref, second_ref, guest_ref):
    each, cut, _ = first_ref.shape
    start = pl.program_id(0) * each
    for at in range(each):
        normed = layer_norm(x_ref[order_ref[start + at]]).astype(jnp.bfloat16)
        first_ref[at] = normed[:cut]
        second_ref[at] = normed[cut:]
        guest_ref[at] = normed


def deal(tokens, deal_order, tp_index, piece):
    groups, _, width = tokens.shape
    each = 4
    steps = groups // each
    cut = piece // 2
    own = pl.BlockSpec((each, cut, width), lambda d, order, t: (d, 0, 0))
    guest = pl.BlockSpec((each, piece, width), lambda d, order, t: ((d + steps // 2) % steps, 0, 0))
    return pl.pallas_call(
        deal_kernel,
        grid_spec=pltpu.PrefetchScalarGridSpec(
            num_scalar_prefetch=2,
            grid=(steps,),
            in_specs=[pl.BlockSpec((groups, piece, width), lambda d, order, t: (0, t[0], 0))],
            out_specs=[own, own, guest],
        ),
        out_shape=[
            jax.ShapeDtypeStruct((groups, rows, width), jnp.bfloat16) for rows in (cut, cut, piece)
        ],
        compiler_params=params(),
        name="deal",
    )(deal_order, tp_index, tokens)


def project_kernel(turned, heads, sources, cut, tp_ref, *refs):
    if sources > 1:
        mine_ref, other_ref, cos_ref, sin_ref, *refs, x_ref = refs
        shards_in, rows_each, _ = mine_ref.shape

        @pl.when(pl.program_id(0) == 0)
        def _():
            t = tp_ref[0]
            for piece in range(rows_each // cut):
                rows = slice(piece * cut, (piece + 1) * cut)
                for shard in range(shards_in):
                    at = (piece * shards_in + shard) * 2
                    for part_ref, side in ((mine_ref, t), (other_ref, 1 - t)):
                        start = pl.multiple_of((at + side) * cut, cut)
                        x_ref[pl.ds(start, cut), :] = part_ref[shard, rows, :]
    else:
        x_ref, cos_ref, sin_ref, *refs = refs
    count = len(turned)
    step = min(512, x_ref.shape[0])
    for first in range(0, x_ref.shape[0], step):
        rows = slice(first, first + step)
        for w_ref, out_ref, turn in zip(refs[:count], refs[count:], turned):
            product = jnp.dot(x_ref[rows, :], w_ref[...], preferred_element_type=jnp.float32)
            if not turn:
                out_ref[rows, :] = product.astype(jnp.bfloat16)
                continue
            for head in range(heads):
                cut = slice(head * HEAD_DIM, (head + 1) * HEAD_DIM)
                part = product[:, cut]
                swapped = pltpu.roll(part, HEAD_DIM // 2, 1)
                out_ref[rows, cut] = (
                    part * cos_ref[rows, :] + swapped * sin_ref[rows, :]
                ).astype(jnp.bfloat16)


def project(x, cut, tp_index, tables, table_at, weights, turned):
    depth = x[0].shape[-1]
    rows = sum(math.prod(part.shape[:-1]) for part in x)
    width = weights[0].shape[1]
    block = min(256, width)
    table = pl.BlockSpec((rows, HEAD_DIM), lambda n, t: (table_at, 0))
    count = len(weights)
    return pl.pallas_call(
        functools.partial(project_kernel, turned, block // HEAD_DIM, len(x), cut),
        grid_spec=pltpu.PrefetchScalarGridSpec(
            num_scalar_prefetch=1,
            grid=(width // block,),
            in_specs=[pl.BlockSpec(part.shape, lambda n, t, r=part.ndim: (0,) * r) for part in x]
            + [table, table]
            + [pl.BlockSpec((depth, block), lambda n, t: (0, n))] * count,
            out_specs=[pl.BlockSpec((rows, block), lambda n, t: (0, n))] * count,
            scratch_shapes=[pltpu.VMEM((rows, depth), jnp.bfloat16)] if len(x) > 1 else [],
        ),
        out_shape=[jax.ShapeDtypeStruct((rows, width), jnp.bfloat16)] * count,
        compiler_params=params(),
        cost_estimate=pl.CostEstimate(
            flops=2 * rows * depth * width * count,
            bytes_accessed=2 * (rows * depth + count * width * (rows + depth)),
            transcendentals=0,
        ),
        name="project",
    )(tp_index, *x, *tables, *weights)


def replace_kernel(block, index_ref, cache_ref, keys_ref, values_ref, out_ref):
    first = pl.program_id(1) * block
    count = index_ref.shape[1]

    def fill(fresh_ref):
        row = first + lax.broadcasted_iota(jnp.int32, (block, count), 0)
        hits = jnp.where(row == index_ref[...], 1.0, 0.0)
        picked = jnp.dot(
            hits.astype(jnp.bfloat16), fresh_ref[...], preferred_element_type=jnp.float32
        )
        is_hit = jnp.sum(hits, axis=1, keepdims=True) > 0.5
        out_ref[0] = jnp.where(is_hit, picked, cache_ref[0, 0].astype(jnp.float32)).astype(
            jnp.bfloat16
        )

    for which, fresh_ref in enumerate((keys_ref, values_ref)):
        pl.when(pl.program_id(0) == which)(functools.partial(fill, fresh_ref))


def replace_rows(cache, keys, values, rec_index):
    _, _, rows, width = cache.shape
    count = rec_index.shape[1]
    block = 512
    return pl.pallas_call(
        functools.partial(replace_kernel, block),
        grid=(2, rows // block),
        in_specs=[
            pl.BlockSpec((1, count), lambda c, r: (0, 0)),
            pl.BlockSpec((1, 1, block, width), lambda c, r: (0, c, r, 0)),
            pl.BlockSpec((count, width), lambda c, r: (0, 0)),
            pl.BlockSpec((count, width), lambda c, r: (0, 0)),
        ],
        out_specs=pl.BlockSpec((1, block, width), lambda c, r: (c, r, 0)),
        out_shape=jax.ShapeDtypeStruct((2, rows, width), jnp.bfloat16),
        compiler_params=params(),
        cost_estimate=pl.CostEstimate(
            flops=4 * rows * count * width, bytes_accessed=10 * rows * width, transcendentals=0
        ),
        name="replace_rows",
    )(rec_index, cache, keys, values)


def fold_keys(jobs, m_ref, acc_ref):
    scale = HEAD_DIM**-0.5 * LOG2E

    def scores_of(job):
        _, queries, keys, _ = job
        parts = []
        for key_block, mask in keys():
            scores = lax.dot_general(
                queries(), key_block, (((1,), (1,)), ((), ())), preferred_element_type=jnp.float32
            )
            parts.append(scores if mask is None else jnp.where(mask, scores, LOWEST))
        return parts[0] if len(parts) == 1 else jnp.concatenate(parts, axis=1)

    upcoming = scores_of(jobs[0])
    for at, (place, _, _, values) in enumerate(jobs):
        scores = upcoming
        if at + 1 < len(jobs):
            upcoming = scores_of(jobs[at + 1])
        old_max = m_ref[place]
        new_max = jnp.maximum(old_max, jnp.max(scores, axis=1, keepdims=True))
        factor = jnp.exp2((old_max - new_max) * scale)
        shift = new_max * scale
        tiles = scores.shape[1] // HEAD_DIM
        weights = jnp.exp2(scores * scale - jnp.concatenate([shift] * tiles, axis=1))
        seen = values()
        widened = jnp.concatenate([seen, jnp.ones(seen.shape, jnp.bfloat16)], axis=1)
        product = jnp.dot(
            weights.astype(jnp.bfloat16), widened, preferred_element_type=jnp.float32
        )
        acc_ref[place] = acc_ref[place] * jnp.concatenate([factor, factor], axis=1) + product
        m_ref[place] = new_max


def attend_kernel(causal, chunk, chunks, piece, sides, count_ref, q_ref, k_ref, v_ref, *refs):
    if causal:
        new_refs, refs = refs[: 2 * chunks], refs[2 * chunks :]
    o_ref, lse_ref, m_ref, acc_ref = refs
    scale = HEAD_DIM**-0.5 * LOG2E
    rows_in = q_ref.shape[0]
    per_step = q_ref.shape[1] // HEAD_DIM
    step = pl.program_id(0)
    used = count_ref[0]
    blocks = [slice(at, at + ROW_BLOCK) for at in range(0, rows_in, ROW_BLOCK)]
    places = [(head, block) for head in range(per_step) for block in blocks]
    m_ref[...] = jnp.full(m_ref.shape, LOWEST, jnp.float32)
    acc_ref[...] = jnp.zeros(acc_ref.shape, jnp.float32)
    k_all = k_ref.at[(0,) * (len(k_ref.shape) - 2)]
    v_all = v_ref.at[(0,) * (len(v_ref.shape) - 2)]

    def head_cut(head):
        return slice(head * HEAD_DIM, (head + 1) * HEAD_DIM)

    def job(place, picks):
        head, block = place
        cut = head_cut(head)

        def values():
            found = [values_ref[at, cut] for _, values_ref, at, _ in picks]
            return found[0] if len(found) == 1 else jnp.concatenate(found, axis=0)

        return (
            place,
            lambda: q_ref[block, cut],
            lambda: [(keys_ref[at, cut], mask) for keys_ref, _, at, mask in picks],
            values,
        )

    def visit(block, masked):
        start = pl.multiple_of(block * KEY_BLOCK, KEY_BLOCK)
        mask = None
        if masked:
            mask = lax.broadcasted_iota(jnp.int32, (1, KEY_BLOCK), 1) < used - start
        picks = [(k_all, v_all, pl.ds(start, KEY_BLOCK), mask)]
        fold_keys([job(place, picks) for place in places], m_ref, acc_ref)

    full = used // KEY_BLOCK
    pl.loop(0, full)(lambda block: visit(block, False))

    @pl.when(used % KEY_BLOCK > 0)
    def _():
        visit(full, True)

    if causal:
        each = piece // sides
        row = lax.broadcasted_iota(jnp.int32, (ROW_BLOCK, ROW_BLOCK), 0)
        key = lax.broadcasted_iota(jnp.int32, (ROW_BLOCK, ROW_BLOCK), 1)

        def natural(at, of_chunk):
            within = at % piece
            inside = (within // each) * (each * chunks) + of_chunk * each + within % each
            return (at // piece) * (piece * chunks) + inside

        row_at = natural(row, chunk)
        masks = [natural(key, key_chunk) <= row_at for key_chunk in range(chunks)]
        jobs = []
        for place in places:
            picks = []
            for key_chunk in range(chunks):
                pair = new_refs[2 * key_chunk : 2 * key_chunk + 2]
                if place[1].start:
                    picks.append((*pair, slice(0, place[1].start), None))
                picks.append((*pair, place[1], masks[key_chunk]))
            jobs.append(job(place, picks))
        fold_keys(jobs, m_ref, acc_ref)

    for head, block in places:
        rows = block
        total = acc_ref[head, block, HEAD_DIM:]
        seen = total > 0.0
        safe = jnp.where(seen, total, 1.0)
        out = (acc_ref[head, block, :HEAD_DIM] / safe).astype(jnp.bfloat16)
        column = step * per_step + head
        o_ref[rows, pl.ds(pl.multiple_of(column * HEAD_DIM, HEAD_DIM), HEAD_DIM)] = out
        lse = jnp.where(seen, m_ref[head, block] * scale + jnp.log2(safe), LOWEST)
        lane = lax.broadcasted_iota(jnp.int32, (ROW_BLOCK, STATS), 1)
        before = jnp.where(column == 0, 0.0, lse_ref[rows, :])
        lse_ref[rows, :] = jnp.where(lane == column, lse, before)

    @pl.when(step == pl.num_programs(0) - 1)
    def _():
        for rows in blocks:
            left = lse_ref[rows, :]
            packed = jnp.zeros_like(left)
            for turn in range(3):
                part = left.astype(jnp.bfloat16).astype(jnp.float32)
                left = left - part
                packed = packed + (pltpu.roll(part, turn * STATS // 4, 1) if turn else part)
            o_ref[rows, o_ref.shape[1] - STATS :] = packed.astype(jnp.bfloat16)


def attend(count, groups, chunk, chunks, sides, queries, cache, new=()):
    width = queries.shape[1]
    heads = width // HEAD_DIM
    per_step = 2
    rows = cache.shape[-2]
    causal = len(new) > 0
    rows_in = queries.shape[0]
    lead = cache.ndim - 3
    shape = (1,) * (lead + 1) + (rows, per_step * HEAD_DIM)
    every = pl.BlockSpec((rows_in, per_step * HEAD_DIM), lambda h, n: (0, h))

    def half(which):
        return pl.BlockSpec(shape, lambda h, n: (0,) * lead + (which, 0, h))

    keys_seen = rows + (rows_in if causal else 0)
    out = pl.pallas_call(
        functools.partial(attend_kernel, causal, chunk, chunks, rows_in // groups, sides),
        grid_spec=pltpu.PrefetchScalarGridSpec(
            num_scalar_prefetch=1,
            grid=(heads // per_step,),
            in_specs=[
                pl.BlockSpec((rows_in, per_step * HEAD_DIM), lambda h, n: (0, h)),
                half(0),
                half(1),
            ]
            + [every] * len(new),
            out_specs=pl.BlockSpec((rows_in, width + STATS), lambda h, n: (0, 0)),
            scratch_shapes=[
                pltpu.VMEM((rows_in, STATS), jnp.float32),
                pltpu.VMEM((per_step, rows_in, HEAD_DIM), jnp.float32),
                pltpu.VMEM((per_step, rows_in, 2 * HEAD_DIM), jnp.float32),
            ],
        ),
        out_shape=jax.ShapeDtypeStruct((rows_in, width + STATS), jnp.bfloat16),
        compiler_params=params(),
        cost_estimate=pl.CostEstimate(
            flops=16 * rows_in * keys_seen * width,
            bytes_accessed=4 * rows * width + 4 * rows_in * width,
            transcendentals=0,
        ),
        name="attend_own" if causal else "attend_guest",
    )(count, queries, cache, cache, *new)
    return out.reshape(groups, rows_in // groups, width + STATS)


def merge_kernel(groups, heads, inverse_ref, tp_ref, own_ref, guest_ref, w_ref, *refs):
    *out_refs, att_ref, share_ref = refs
    piece = own_ref.shape[1]
    width = heads * HEAD_DIM
    step = pl.program_id(0)

    def stats(part_ref, at):
        packed = part_ref[at, :, width:].astype(jnp.float32)
        return (
            packed
            + pltpu.roll(packed, STATS - STATS // 4, 1)
            + pltpu.roll(packed, STATS - STATS // 2, 1)
        )

    @pl.when(step == 0)
    def _():
        lane = lax.broadcasted_iota(jnp.int32, (piece, STATS), 1)
        rows = [pl.ds(request * piece, piece) for request in range(groups)]
        for request in range(groups):
            source = inverse_ref[request]
            helper = lax.rem(source + groups // 2, groups)
            ahead = stats(guest_ref, helper) - stats(own_ref, source)
            share = jnp.where(lane < heads, 1.0 / (1.0 + jnp.exp2(ahead)), 0.0)
            high = share.astype(jnp.bfloat16).astype(jnp.float32)
            rest = pltpu.roll(share - high, STATS // 4, 1)
            share_ref[rows[request], :] = (high + rest).astype(jnp.bfloat16)
        lane = lax.broadcasted_iota(jnp.int32, (STATS, width), 0)
        head = lax.broadcasted_iota(jnp.int32, (STATS, width), 1) // HEAD_DIM
        spread = jnp.where((lane == head) | (lane == head + STATS // 4), 1.0, 0.0)
        shares = jnp.dot(
            share_ref[...], spread.astype(jnp.bfloat16), preferred_element_type=jnp.float32
        )
        for request in range(groups):
            source = inverse_ref[request]
            helper = lax.rem(source + groups // 2, groups)
            own = own_ref[source, :, :width].astype(jnp.float32)
            guest = guest_ref[helper, :, :width].astype(jnp.float32)
            share = shares[request * piece : (request + 1) * piece]
            att_ref[rows[request], :] = (guest + share * (own - guest)).astype(jnp.bfloat16)

    product = jnp.dot(att_ref[...], w_ref[...], preferred_element_type=jnp.float32).astype(
        jnp.bfloat16
    )
    each = pl.num_programs(0) // len(out_refs)
    for at, out_ref in enumerate(out_refs):
        pl.when(step // each == at)(functools.partial(out_ref.__setitem__, ..., product))


def merge(inverse, tp_index, splits, own, guest, w_out):
    groups, piece, _ = guest.shape
    width = w_out.shape[0]
    heads = width // HEAD_DIM
    columns = w_out.shape[1]
    block = 512
    rows = groups * piece
    steps = columns // block
    each = steps // splits

    def w_at(n, i, t):
        return (0, (n + each * (1 - t[0])) % steps if splits == 2 else n)

    def out_at(which):
        return lambda n, i, t: (0, jnp.clip(n - which * each, 0, each - 1))

    part = pl.BlockSpec(guest.shape, lambda n, i, t: (0, 0, 0))
    return pl.pallas_call(
        functools.partial(merge_kernel, groups, heads),
        grid_spec=pltpu.PrefetchScalarGridSpec(
            num_scalar_prefetch=2,
            grid=(steps,),
            in_specs=[part, part, pl.BlockSpec((width, block), w_at)],
            out_specs=[pl.BlockSpec((rows, block), out_at(which)) for which in range(splits)],
            scratch_shapes=[
                pltpu.VMEM((rows, width), jnp.bfloat16),
                pltpu.VMEM((rows, STATS), jnp.bfloat16),
            ],
        ),
        out_shape=[jax.ShapeDtypeStruct((rows, columns // splits), jnp.bfloat16)] * splits,
        compiler_params=params(),
        cost_estimate=pl.CostEstimate(
            flops=rows * width * columns,
            bytes_accessed=rows * columns,
            transcendentals=0,
        ),
        name="merge",
    )(inverse, tp_index, own, guest, w_out)


def exchange(value):
    return lax.all_to_all(value, "grp", split_axis=0, concat_axis=0, tiled=True)


def shards(
    tokens,
    w_query,
    w_key,
    w_value,
    w_out,
    own_cache,
    guest_cache,
    rec_hidden,
    deal_order,
    own_len,
    guest_len,
    rec_index,
):
    groups = lax.axis_size("grp")
    tp_size = lax.axis_size("tp")
    group_id = lax.axis_index("grp")
    tp_id = lax.axis_index("tp")
    partner_id = (group_id + groups // 2) % groups
    width = w_query.shape[1]
    heads = width // HEAD_DIM
    shard_rows = tokens.shape[1]
    span = shard_rows * groups
    piece = shard_rows // tp_size

    chunks = 2
    chunk_rows = shard_rows // chunks
    paired = tp_size == 2 and piece % 32 == 0
    sides = 2 if paired else 1
    each = chunk_rows // sides
    tp_index = tp_id.astype(jnp.int32)[None]
    tied = lax.optimization_barrier
    neighbour = [(0, 1), (1, 0)]

    if paired:
        dealt = deal(tokens, deal_order, tp_index, piece)
        own_rows, guest_rows = dealt[:2], dealt[2]
    else:
        mine = lax.dynamic_slice_in_dim(tokens, tp_id * piece, piece, 1)
        normed = layer_norm(mine).astype(jnp.bfloat16)
        own_rows = jnp.take(normed, deal_order, axis=0)
        guest_rows = jnp.roll(own_rows, groups // 2, axis=0)

    def in_chunks(rows):
        rows = rows.reshape(groups, sides, chunks, each, -1)
        return jnp.transpose(rows, (2, 0, 1, 3, 4)).reshape(chunks, span // chunks, -1)

    def with_other(arrived):
        return [arrived, lax.ppermute(arrived, "tp", neighbour)]

    def gathered(rows):
        arrived = lax.all_gather(exchange(rows), "tp", axis=0)
        parts = in_chunks(jnp.transpose(arrived, (1, 0, 2, 3)))
        return [[part] for part in parts]

    row_order = in_chunks(jnp.arange(span, dtype=jnp.int32)).reshape(span)

    def place(owner, helper):
        return own_len[owner] + guest_len[helper] + row_order

    def projected(x, tables, chunk, weights, turned):
        return project(x, each, tp_index, tables, chunk, weights, turned)

    def own_project(chunk):
        return projected(
            own_x[chunk], own_tables, chunk, (w_query, w_key, w_value), (True, True, False)
        )

    def own_attend(chunk, queries):
        count = own_len[group_id][None]
        return attend(count, groups, chunk, chunks, sides, queries, cache, new)

    def guest_attend(chunk, x):
        (queries,) = projected(x, guest_tables, chunk, (w_query,), (True,))
        count = guest_len[group_id][None]
        return attend(count, groups, chunk, chunks, sides, queries, guest_cache)

    own_tables = rope_tables(place(group_id, partner_id))
    guest_tables = rope_tables(place(partner_id, group_id))
    rec_tables = rope_tables(rec_index[0])
    rec_rows = layer_norm(rec_hidden[0]).astype(jnp.bfloat16)
    rec_parts = projected((rec_rows,), rec_tables, 0, (w_key, w_value), (True, False))

    if paired:
        arrived = exchange(own_rows[0])
        arrived, own_tables, guest_tables, rec_parts, own_rows = tied(
            (arrived, own_tables, guest_tables, rec_parts, own_rows)
        )
        own_x = [with_other(arrived)]
        cache = replace_rows(own_cache, *rec_parts, rec_index)
        arrived = exchange(own_rows[1])
        arrived, cache, own_x, guest_rows = tied((arrived, cache, own_x, guest_rows))
        own_x.append(with_other(arrived))
        arrived = exchange(guest_rows)
        made = [own_project(chunk) for chunk in range(chunks)]
        arrived, made = tied((arrived, made))
        guest_x = [with_other(arrived[:, :each])]
        guest_x, arrived = tied((guest_x, arrived[:, each:]))
        guest_x.append(with_other(arrived))
    else:
        cache = replace_rows(own_cache, *rec_parts, rec_index)
        own_x = gathered(own_rows)
        guest_x = gathered(guest_rows)
        made = [own_project(chunk) for chunk in range(chunks)]
    new = [part for parts in made for part in parts[1:]]
    inverse = jnp.sum(
        jnp.where(
            deal_order[None, :] == jnp.arange(groups, dtype=deal_order.dtype)[:, None],
            jnp.arange(groups, dtype=jnp.int32)[None, :],
            0,
        ),
        axis=1,
    )

    first, second = guest_x
    own_out = own_attend(0, made[0][0])
    own_out, query, first = tied((own_out, made[1][0], first))
    own_part = [exchange(own_out)]
    guest_out = guest_attend(0, first)
    own_part, guest_out, query = tied((own_part, guest_out, query))
    guest_part = [exchange(guest_out)]
    own_out = own_attend(1, query)
    guest_part, own_out, second = tied((guest_part, own_out, second))
    own_part.append(exchange(own_out))
    guest_out = guest_attend(1, second)

    def merged(chunk):
        splits = 2 if paired else 1
        return merge(inverse, tp_index, splits, own_part[chunk], guest_part[chunk], w_out)

    def summed(partial):
        if paired:
            theirs, mine = partial
            arrived = lax.ppermute(theirs, "tp", neighbour).astype(jnp.float32)
            total = (mine.astype(jnp.float32) + arrived).astype(jnp.bfloat16)
        else:
            total = lax.psum_scatter(partial[0], "tp", scatter_dimension=1, tiled=True)
        return total.reshape(groups, sides, 1, each, -1)

    partial = merged(0)
    own_part[1], guest_out, partial = tied((own_part[1], guest_out, partial))
    guest_part.append(exchange(guest_out))
    mixed = [summed(partial)]
    guest_part[1], mixed = tied((guest_part[1], mixed))
    mixed.append(summed(merged(1)))
    return jnp.concatenate(mixed, axis=2).reshape(groups, shard_rows, -1)


def solution(mesh):
    return jax.shard_map(
        shards,
        mesh=mesh,
        in_specs=(
            P(None, "grp", None),
            P(None, "tp"),
            P(None, "tp"),
            P(None, "tp"),
            P("tp", None),
            P("grp", None, None, "tp"),
            P("grp", None, None, "tp"),
            P("grp", None, None),
            P(),
            P(),
            P(),
            P("grp", None),
        ),
        out_specs=P(None, "grp", "tp"),
        check_vma=False,
    )
```

```python
import functools
import math

import jax
import jax.numpy as jnp
from jax import lax
from jax.experimental import pallas as pl
from jax.experimental.pallas import tpu as pltpu
from jax.sharding import PartitionSpec as P

HEAD_DIM = 128
KEY_BLOCK = 1024
ROW_BLOCK = 256
STATS = 128
VMEM_LIMIT = 60 * 1024 * 1024

rope_base = 10000.0
norm_eps = 1e-05
LOG2E = math.log2(math.e)
LOWEST = -1e30


def params():
    return pltpu.CompilerParams(vmem_limit_bytes=VMEM_LIMIT)


def layer_norm(token_rows):
    widened = token_rows.astype(jnp.float32)
    centred = widened - jnp.mean(widened, axis=-1, keepdims=True)
    variance = jnp.mean(centred * centred, axis=-1, keepdims=True)
    return centred * lax.rsqrt(variance + norm_eps)


def rope_tables(positions):
    half_dim = HEAD_DIM // 2
    frequency = jnp.exp(-jnp.log(rope_base) * jnp.arange(half_dim, dtype=jnp.float32) / half_dim)
    angles = positions.astype(jnp.float32)[:, None] * frequency[None, :]
    cosine = jnp.cos(angles)
    sine = jnp.sin(angles)
    return (
        jnp.concatenate([cosine, cosine], axis=-1),
        jnp.concatenate([-sine, sine], axis=-1),
    )


def deal_kernel(order_ref, tp_ref, x_ref, first_ref, second_ref, guest_ref):
    each, cut, _ = first_ref.shape
    start = pl.program_id(0) * each
    for at in range(each):
        normed = layer_norm(x_ref[order_ref[start + at]]).astype(jnp.bfloat16)
        first_ref[at] = normed[:cut]
        second_ref[at] = normed[cut:]
        guest_ref[at] = normed


def deal(tokens, deal_order, tp_index, piece):
    groups, _, width = tokens.shape
    each = 4
    steps = groups // each
    cut = piece // 2
    own = pl.BlockSpec((each, cut, width), lambda d, order, t: (d, 0, 0))
    guest = pl.BlockSpec((each, piece, width), lambda d, order, t: ((d + steps // 2) % steps, 0, 0))
    return pl.pallas_call(
        deal_kernel,
        grid_spec=pltpu.PrefetchScalarGridSpec(
            num_scalar_prefetch=2,
            grid=(steps,),
            in_specs=[pl.BlockSpec((groups, piece, width), lambda d, order, t: (0, t[0], 0))],
            out_specs=[own, own, guest],
        ),
        out_shape=[
            jax.ShapeDtypeStruct((groups, rows, width), jnp.bfloat16) for rows in (cut, cut, piece)
        ],
        compiler_params=params(),
        name="deal",
    )(deal_order, tp_index, tokens)


def project_kernel(turned, heads, sources, cut, tp_ref, *refs):
    if sources > 1:
        mine_ref, other_ref, cos_ref, sin_ref, *refs, x_ref = refs
        shards_in, rows_each, _ = mine_ref.shape

        @pl.when(pl.program_id(0) == 0)
        def _():
            t = tp_ref[0]
            for piece in range(rows_each // cut):
                rows = slice(piece * cut, (piece + 1) * cut)
                for shard in range(shards_in):
                    at = (piece * shards_in + shard) * 2
                    for part_ref, side in ((mine_ref, t), (other_ref, 1 - t)):
                        start = pl.multiple_of((at + side) * cut, cut)
                        x_ref[pl.ds(start, cut), :] = part_ref[shard, rows, :]
    else:
        x_ref, cos_ref, sin_ref, *refs = refs
    count = len(turned)
    step = min(512, x_ref.shape[0])
    for first in range(0, x_ref.shape[0], step):
        rows = slice(first, first + step)
        for w_ref, out_ref, turn in zip(refs[:count], refs[count:], turned):
            product = jnp.dot(x_ref[rows, :], w_ref[...], preferred_element_type=jnp.float32)
            if not turn:
                out_ref[rows, :] = product.astype(jnp.bfloat16)
                continue
            for head in range(heads):
                cut = slice(head * HEAD_DIM, (head + 1) * HEAD_DIM)
                part = product[:, cut]
                swapped = pltpu.roll(part, HEAD_DIM // 2, 1)
                out_ref[rows, cut] = (
                    part * cos_ref[rows, :] + swapped * sin_ref[rows, :]
                ).astype(jnp.bfloat16)


def project(x, cut, tp_index, tables, table_at, weights, turned):
    depth = x[0].shape[-1]
    rows = sum(math.prod(part.shape[:-1]) for part in x)
    width = weights[0].shape[1]
    block = min(256, width)
    table = pl.BlockSpec((rows, HEAD_DIM), lambda n, t: (table_at, 0))
    count = len(weights)
    return pl.pallas_call(
        functools.partial(project_kernel, turned, block // HEAD_DIM, len(x), cut),
        grid_spec=pltpu.PrefetchScalarGridSpec(
            num_scalar_prefetch=1,
            grid=(width // block,),
            in_specs=[pl.BlockSpec(part.shape, lambda n, t, r=part.ndim: (0,) * r) for part in x]
            + [table, table]
            + [pl.BlockSpec((depth, block), lambda n, t: (0, n))] * count,
            out_specs=[pl.BlockSpec((rows, block), lambda n, t: (0, n))] * count,
            scratch_shapes=[pltpu.VMEM((rows, depth), jnp.bfloat16)] if len(x) > 1 else [],
        ),
        out_shape=[jax.ShapeDtypeStruct((rows, width), jnp.bfloat16)] * count,
        compiler_params=params(),
        cost_estimate=pl.CostEstimate(
            flops=2 * rows * depth * width * count,
            bytes_accessed=2 * (rows * depth + count * width * (rows + depth)),
            transcendentals=0,
        ),
        name="project",
    )(tp_index, *x, *tables, *weights)


def replace_kernel(block, index_ref, cache_ref, keys_ref, values_ref, out_ref):
    first = pl.program_id(1) * block
    count = index_ref.shape[1]

    def fill(fresh_ref):
        row = first + lax.broadcasted_iota(jnp.int32, (block, count), 0)
        hits = jnp.where(row == index_ref[...], 1.0, 0.0)
        picked = jnp.dot(
            hits.astype(jnp.bfloat16), fresh_ref[...], preferred_element_type=jnp.float32
        )
        is_hit = jnp.sum(hits, axis=1, keepdims=True) > 0.5
        out_ref[0] = jnp.where(is_hit, picked, cache_ref[0, 0].astype(jnp.float32)).astype(
            jnp.bfloat16
        )

    for which, fresh_ref in enumerate((keys_ref, values_ref)):
        pl.when(pl.program_id(0) == which)(functools.partial(fill, fresh_ref))


def replace_rows(cache, keys, values, rec_index):
    _, _, rows, width = cache.shape
    count = rec_index.shape[1]
    block = 512
    return pl.pallas_call(
        functools.partial(replace_kernel, block),
        grid=(2, rows // block),
        in_specs=[
            pl.BlockSpec((1, count), lambda c, r: (0, 0)),
            pl.BlockSpec((1, 1, block, width), lambda c, r: (0, c, r, 0)),
            pl.BlockSpec((count, width), lambda c, r: (0, 0)),
            pl.BlockSpec((count, width), lambda c, r: (0, 0)),
        ],
        out_specs=pl.BlockSpec((1, block, width), lambda c, r: (c, r, 0)),
        out_shape=jax.ShapeDtypeStruct((2, rows, width), jnp.bfloat16),
        compiler_params=params(),
        cost_estimate=pl.CostEstimate(
            flops=4 * rows * count * width, bytes_accessed=10 * rows * width, transcendentals=0
        ),
        name="replace_rows",
    )(rec_index, cache, keys, values)


def fold_keys(jobs, m_ref, acc_ref):
    scale = HEAD_DIM**-0.5 * LOG2E

    def scores_of(job):
        _, queries, keys, _ = job
        parts = []
        for key_block, mask in keys():
            scores = lax.dot_general(
                queries(), key_block, (((1,), (1,)), ((), ())), preferred_element_type=jnp.float32
            )
            parts.append(scores if mask is None else jnp.where(mask, scores, LOWEST))
        return parts[0] if len(parts) == 1 else jnp.concatenate(parts, axis=1)

    upcoming = scores_of(jobs[0])
    for at, (place, _, _, values) in enumerate(jobs):
        scores = upcoming
        if at + 1 < len(jobs):
            upcoming = scores_of(jobs[at + 1])
        old_max = m_ref[place]
        new_max = jnp.maximum(old_max, jnp.max(scores, axis=1, keepdims=True))
        factor = jnp.exp2((old_max - new_max) * scale)
        shift = new_max * scale
        tiles = scores.shape[1] // HEAD_DIM
        weights = jnp.exp2(scores * scale - jnp.concatenate([shift] * tiles, axis=1))
        seen = values()
        widened = jnp.concatenate([seen, jnp.ones(seen.shape, jnp.bfloat16)], axis=1)
        product = jnp.dot(
            weights.astype(jnp.bfloat16), widened, preferred_element_type=jnp.float32
        )
        acc_ref[place] = acc_ref[place] * jnp.concatenate([factor, factor], axis=1) + product
        m_ref[place] = new_max


def attend_kernel(causal, chunk, chunks, piece, sides, count_ref, q_ref, k_ref, v_ref, *refs):
    if causal:
        new_refs, refs = refs[: 2 * chunks], refs[2 * chunks :]
    o_ref, lse_ref, m_ref, acc_ref = refs
    scale = HEAD_DIM**-0.5 * LOG2E
    rows_in = q_ref.shape[0]
    per_step = q_ref.shape[1] // HEAD_DIM
    step = pl.program_id(0)
    used = count_ref[0]
    blocks = [slice(at, at + ROW_BLOCK) for at in range(0, rows_in, ROW_BLOCK)]
    places = [(head, block) for head in range(per_step) for block in blocks]
    m_ref[...] = jnp.full(m_ref.shape, LOWEST, jnp.float32)
    acc_ref[...] = jnp.zeros(acc_ref.shape, jnp.float32)
    k_all = k_ref.at[(0,) * (len(k_ref.shape) - 2)]
    v_all = v_ref.at[(0,) * (len(v_ref.shape) - 2)]

    def head_cut(head):
        return slice(head * HEAD_DIM, (head + 1) * HEAD_DIM)

    def job(place, picks):
        head, block = place
        cut = head_cut(head)

        def values():
            found = [values_ref[at, cut] for _, values_ref, at, _ in picks]
            return found[0] if len(found) == 1 else jnp.concatenate(found, axis=0)

        return (
            place,
            lambda: q_ref[block, cut],
            lambda: [(keys_ref[at, cut], mask) for keys_ref, _, at, mask in picks],
            values,
        )

    def visit(block, masked):
        start = pl.multiple_of(block * KEY_BLOCK, KEY_BLOCK)
        mask = None
        if masked:
            mask = lax.broadcasted_iota(jnp.int32, (1, KEY_BLOCK), 1) < used - start
        picks = [(k_all, v_all, pl.ds(start, KEY_BLOCK), mask)]
        fold_keys([job(place, picks) for place in places], m_ref, acc_ref)

    full = used // KEY_BLOCK
    pl.loop(0, full)(lambda block: visit(block, False))

    @pl.when(used % KEY_BLOCK > 0)
    def _():
        visit(full, True)

    if causal:
        each = piece // sides
        row = lax.broadcasted_iota(jnp.int32, (ROW_BLOCK, ROW_BLOCK), 0)
        key = lax.broadcasted_iota(jnp.int32, (ROW_BLOCK, ROW_BLOCK), 1)

        def natural(at, of_chunk):
            within = at % piece
            inside = (within // each) * (each * chunks) + of_chunk * each + within % each
            return (at // piece) * (piece * chunks) + inside

        row_at = natural(row, chunk)
        masks = [natural(key, key_chunk) <= row_at for key_chunk in range(chunks)]
        jobs = []
        for place in places:
            picks = []
            for key_chunk in range(chunks):
                pair = new_refs[2 * key_chunk : 2 * key_chunk + 2]
                if place[1].start:
                    picks.append((*pair, slice(0, place[1].start), None))
                picks.append((*pair, place[1], masks[key_chunk]))
            jobs.append(job(place, picks))
        fold_keys(jobs, m_ref, acc_ref)

    for head, block in places:
        rows = block
        total = acc_ref[head, block, HEAD_DIM:]
        seen = total > 0.0
        safe = jnp.where(seen, total, 1.0)
        out = (acc_ref[head, block, :HEAD_DIM] / safe).astype(jnp.bfloat16)
        column = step * per_step + head
        o_ref[rows, pl.ds(pl.multiple_of(column * HEAD_DIM, HEAD_DIM), HEAD_DIM)] = out
        lse = jnp.where(seen, m_ref[head, block] * scale + jnp.log2(safe), LOWEST)
        lane = lax.broadcasted_iota(jnp.int32, (ROW_BLOCK, STATS), 1)
        before = jnp.where(column == 0, 0.0, lse_ref[rows, :])
        lse_ref[rows, :] = jnp.where(lane == column, lse, before)

    @pl.when(step == pl.num_programs(0) - 1)
    def _():
        for rows in blocks:
            left = lse_ref[rows, :]
            packed = jnp.zeros_like(left)
            for turn in range(3):
                part = left.astype(jnp.bfloat16).astype(jnp.float32)
                left = left - part
                packed = packed + (pltpu.roll(part, turn * STATS // 4, 1) if turn else part)
            o_ref[rows, o_ref.shape[1] - STATS :] = packed.astype(jnp.bfloat16)


def attend(count, groups, chunk, chunks, sides, queries, cache, new=()):
    width = queries.shape[1]
    heads = width // HEAD_DIM
    per_step = 2
    rows = cache.shape[-2]
    causal = len(new) > 0
    rows_in = queries.shape[0]
    lead = cache.ndim - 3
    shape = (1,) * (lead + 1) + (rows, per_step * HEAD_DIM)
    every = pl.BlockSpec((rows_in, per_step * HEAD_DIM), lambda h, n: (0, h))

    def half(which):
        return pl.BlockSpec(shape, lambda h, n: (0,) * lead + (which, 0, h))

    keys_seen = rows + (rows_in if causal else 0)
    out = pl.pallas_call(
        functools.partial(attend_kernel, causal, chunk, chunks, rows_in // groups, sides),
        grid_spec=pltpu.PrefetchScalarGridSpec(
            num_scalar_prefetch=1,
            grid=(heads // per_step,),
            in_specs=[
                pl.BlockSpec((rows_in, per_step * HEAD_DIM), lambda h, n: (0, h)),
                half(0),
                half(1),
            ]
            + [every] * len(new),
            out_specs=pl.BlockSpec((rows_in, width + STATS), lambda h, n: (0, 0)),
            scratch_shapes=[
                pltpu.VMEM((rows_in, STATS), jnp.float32),
                pltpu.VMEM((per_step, rows_in, HEAD_DIM), jnp.float32),
                pltpu.VMEM((per_step, rows_in, 2 * HEAD_DIM), jnp.float32),
            ],
        ),
        out_shape=jax.ShapeDtypeStruct((rows_in, width + STATS), jnp.bfloat16),
        compiler_params=params(),
        cost_estimate=pl.CostEstimate(
            flops=16 * rows_in * keys_seen * width,
            bytes_accessed=4 * rows * width + 4 * rows_in * width,
            transcendentals=0,
        ),
        name="attend_own" if causal else "attend_guest",
    )(count, queries, cache, cache, *new)
    return out.reshape(groups, rows_in // groups, width + STATS)


def merge_kernel(groups, heads, inverse_ref, tp_ref, own_ref, guest_ref, w_ref, *refs):
    *out_refs, att_ref, share_ref = refs
    piece = own_ref.shape[1]
    width = heads * HEAD_DIM
    step = pl.program_id(0)

    def stats(part_ref, at):
        packed = part_ref[at, :, width:].astype(jnp.float32)
        return (
            packed
            + pltpu.roll(packed, STATS - STATS // 4, 1)
            + pltpu.roll(packed, STATS - STATS // 2, 1)
        )

    @pl.when(step == 0)
    def _():
        lane = lax.broadcasted_iota(jnp.int32, (piece, STATS), 1)
        rows = [pl.ds(request * piece, piece) for request in range(groups)]
        for request in range(groups):
            source = inverse_ref[request]
            helper = lax.rem(source + groups // 2, groups)
            ahead = stats(guest_ref, helper) - stats(own_ref, source)
            share = jnp.where(lane < heads, 1.0 / (1.0 + jnp.exp2(ahead)), 0.0)
            high = share.astype(jnp.bfloat16).astype(jnp.float32)
            rest = pltpu.roll(share - high, STATS // 4, 1)
            share_ref[rows[request], :] = (high + rest).astype(jnp.bfloat16)
        lane = lax.broadcasted_iota(jnp.int32, (STATS, width), 0)
        head = lax.broadcasted_iota(jnp.int32, (STATS, width), 1) // HEAD_DIM
        spread = jnp.where((lane == head) | (lane == head + STATS // 4), 1.0, 0.0)
        shares = jnp.dot(
            share_ref[...], spread.astype(jnp.bfloat16), preferred_element_type=jnp.float32
        )
        for request in range(groups):
            source = inverse_ref[request]
            helper = lax.rem(source + groups // 2, groups)
            own = own_ref[source, :, :width].astype(jnp.float32)
            guest = guest_ref[helper, :, :width].astype(jnp.float32)
            share = shares[request * piece : (request + 1) * piece]
            att_ref[rows[request], :] = (guest + share * (own - guest)).astype(jnp.bfloat16)

    product = jnp.dot(att_ref[...], w_ref[...], preferred_element_type=jnp.float32).astype(
        jnp.bfloat16
    )
    each = pl.num_programs(0) // len(out_refs)
    for at, out_ref in enumerate(out_refs):
        pl.when(step // each == at)(functools.partial(out_ref.__setitem__, ..., product))


def merge(inverse, tp_index, splits, own, guest, w_out):
    groups, piece, _ = guest.shape
    width = w_out.shape[0]
    heads = width // HEAD_DIM
    columns = w_out.shape[1]
    block = 512
    rows = groups * piece
    steps = columns // block
    each = steps // splits

    def w_at(n, i, t):
        return (0, (n + each * (1 - t[0])) % steps if splits == 2 else n)

    def out_at(which):
        return lambda n, i, t: (0, jnp.clip(n - which * each, 0, each - 1))

    part = pl.BlockSpec(guest.shape, lambda n, i, t: (0, 0, 0))
    return pl.pallas_call(
        functools.partial(merge_kernel, groups, heads),
        grid_spec=pltpu.PrefetchScalarGridSpec(
            num_scalar_prefetch=2,
            grid=(steps,),
            in_specs=[part, part, pl.BlockSpec((width, block), w_at)],
            out_specs=[pl.BlockSpec((rows, block), out_at(which)) for which in range(splits)],
            scratch_shapes=[
                pltpu.VMEM((rows, width), jnp.bfloat16),
                pltpu.VMEM((rows, STATS), jnp.bfloat16),
            ],
        ),
        out_shape=[jax.ShapeDtypeStruct((rows, columns // splits), jnp.bfloat16)] * splits,
        compiler_params=params(),
        cost_estimate=pl.CostEstimate(
            flops=rows * width * columns,
            bytes_accessed=rows * columns,
            transcendentals=0,
        ),
        name="merge",
    )(inverse, tp_index, own, guest, w_out)


def exchange(value):
    return lax.all_to_all(value, "grp", split_axis=0, concat_axis=0, tiled=True)


def shards(
    tokens,
    w_query,
    w_key,
    w_value,
    w_out,
    own_cache,
    guest_cache,
    rec_hidden,
    deal_order,
    own_len,
    guest_len,
    rec_index,
):
    groups = lax.axis_size("grp")
    tp_size = lax.axis_size("tp")
    group_id = lax.axis_index("grp")
    tp_id = lax.axis_index("tp")
    partner_id = (group_id + groups // 2) % groups
    width = w_query.shape[1]
    heads = width // HEAD_DIM
    shard_rows = tokens.shape[1]
    span = shard_rows * groups
    piece = shard_rows // tp_size

    chunks = 2
    chunk_rows = shard_rows // chunks
    paired = tp_size == 2 and piece % 32 == 0
    sides = 2 if paired else 1
    each = chunk_rows // sides
    tp_index = tp_id.astype(jnp.int32)[None]
    tied = lax.optimization_barrier
    neighbour = [(0, 1), (1, 0)]

    if paired:
        dealt = deal(tokens, deal_order, tp_index, piece)
        own_rows, guest_rows = dealt[:2], dealt[2]
    else:
        mine = lax.dynamic_slice_in_dim(tokens, tp_id * piece, piece, 1)
        normed = layer_norm(mine).astype(jnp.bfloat16)
        own_rows = jnp.take(normed, deal_order, axis=0)
        guest_rows = jnp.roll(own_rows, groups // 2, axis=0)

    def in_chunks(rows):
        rows = rows.reshape(groups, sides, chunks, each, -1)
        return jnp.transpose(rows, (2, 0, 1, 3, 4)).reshape(chunks, span // chunks, -1)

    def with_other(arrived):
        return [arrived, lax.ppermute(arrived, "tp", neighbour)]

    def gathered(rows):
        arrived = lax.all_gather(exchange(rows), "tp", axis=0)
        parts = in_chunks(jnp.transpose(arrived, (1, 0, 2, 3)))
        return [[part] for part in parts]

    row_order = in_chunks(jnp.arange(span, dtype=jnp.int32)).reshape(span)

    def place(owner, helper):
        return own_len[owner] + guest_len[helper] + row_order

    def projected(x, tables, chunk, weights, turned):
        return project(x, each, tp_index, tables, chunk, weights, turned)

    def own_project(chunk):
        return projected(
            own_x[chunk], own_tables, chunk, (w_query, w_key, w_value), (True, True, False)
        )

    def own_attend(chunk, queries):
        count = own_len[group_id][None]
        return attend(count, groups, chunk, chunks, sides, queries, cache, new)

    def guest_attend(chunk, x):
        (queries,) = projected(x, guest_tables, chunk, (w_query,), (True,))
        count = guest_len[group_id][None]
        return attend(count, groups, chunk, chunks, sides, queries, guest_cache)

    own_tables = rope_tables(place(group_id, partner_id))
    guest_tables = rope_tables(place(partner_id, group_id))
    rec_tables = rope_tables(rec_index[0])
    rec_rows = layer_norm(rec_hidden[0]).astype(jnp.bfloat16)
    rec_parts = projected((rec_rows,), rec_tables, 0, (w_key, w_value), (True, False))

    if paired:
        arrived = exchange(own_rows[0])
        arrived, own_tables, guest_tables, rec_parts, own_rows = tied(
            (arrived, own_tables, guest_tables, rec_parts, own_rows)
        )
        own_x = [with_other(arrived)]
        cache = replace_rows(own_cache, *rec_parts, rec_index)
        arrived = exchange(own_rows[1])
        arrived, cache, own_x, guest_rows = tied((arrived, cache, own_x, guest_rows))
        own_x.append(with_other(arrived))
        arrived = exchange(guest_rows)
        made = [own_project(chunk) for chunk in range(chunks)]
        arrived, made = tied((arrived, made))
        guest_x = [with_other(arrived[:, :each])]
        guest_x, arrived = tied((guest_x, arrived[:, each:]))
        guest_x.append(with_other(arrived))
    else:
        cache = replace_rows(own_cache, *rec_parts, rec_index)
        own_x = gathered(own_rows)
        guest_x = gathered(guest_rows)
        made = [own_project(chunk) for chunk in range(chunks)]
    new = [part for parts in made for part in parts[1:]]
    inverse = jnp.sum(
        jnp.where(
            deal_order[None, :] == jnp.arange(groups, dtype=deal_order.dtype)[:, None],
            jnp.arange(groups, dtype=jnp.int32)[None, :],
            0,
        ),
        axis=1,
    )

    first, second = guest_x
    own_out = own_attend(0, made[0][0])
    own_out, query, first = tied((own_out, made[1][0], first))
    own_part = [exchange(own_out)]
    guest_out = guest_attend(0, first)
    own_part, guest_out, query = tied((own_part, guest_out, query))
    guest_part = [exchange(guest_out)]
    own_out = own_attend(1, query)
    guest_part, own_out, second = tied((guest_part, own_out, second))
    own_part.append(exchange(own_out))
    guest_out = guest_attend(1, second)

    def merged(chunk):
        splits = 2 if paired else 1
        return merge(inverse, tp_index, splits, own_part[chunk], guest_part[chunk], w_out)

    def summed(mine, arrived):
        total = (mine.astype(jnp.float32) + arrived.astype(jnp.float32)).astype(jnp.bfloat16)
        return total.reshape(groups, sides, 1, each, -1)

    def swapped(partial):
        if paired:
            return partial[1], lax.ppermute(partial[0], "tp", neighbour)
        total = lax.psum_scatter(partial[0], "tp", scatter_dimension=1, tiled=True)
        return total, jnp.zeros_like(total)

    partial = merged(0)
    own_part[1], guest_out, partial = tied((own_part[1], guest_out, partial))
    guest_part.append(exchange(guest_out))
    terms = swapped(partial)
    guest_part[1], terms = tied((guest_part[1], terms))
    mixed = [summed(*terms), summed(*swapped(merged(1)))]
    return jnp.concatenate(mixed, axis=2).reshape(groups, shard_rows, -1)


def solution(mesh):
    return jax.shard_map(
        shards,
        mesh=mesh,
        in_specs=(
            P(None, "grp", None),
            P(None, "tp"),
            P(None, "tp"),
            P(None, "tp"),
            P("tp", None),
            P("grp", None, None, "tp"),
            P("grp", None, None, "tp"),
            P("grp", None, None),
            P(),
            P(),
            P(),
            P("grp", None),
        ),
        out_specs=P(None, "grp", "tp"),
        check_vma=False,
    )
```
